256 devices in a mesh: wide: 32 (over z_lo, y, core), narrow: 8 (over z_hi, x).
Axes of the slice: x: 4, y: 4, z: 8 (z_hi: 2, z_lo: 4; z = z_hi * 4 + z_lo), core: 2. Of those that a mesh axis runs over, the one named last changes fastest.
Arguments:
- divergence: float32 [256, 256, 256], P('wide', 'narrow'), may hold values from -5 to 5
- screening: float32 [256, 256, 256], P('wide', 'narrow'), may hold values from 0.0001 to 0.1
Outputs:
- solution_field: float32 [256, 256, 256], P('wide', 'narrow')
- residual: float32 [256, 256, 256], P('wide', 'narrow')
The draws below stay inside these ranges and needn't reach their ends.
All inputs are finite; a program needn't handle non-finite values.
Results may differ from the reference program's by a relative error of at most 0.0003.
Values sent between devices are 32-bit elements; how exact they have to be, the bound alone decides.
A program may use at most 128 MiB of HBM per device.

```python
import math
import jax
import jax.numpy as jnp
from jax import lax

NZ = 256
SWEEPS = 2
NX = 256
NY = 256


def draw_divergence(key, part):
    key = jax.random.fold_in(key, 11)
    return jax.random.truncated_normal(key, -5.0, 5.0, (NX, NY, NZ), jnp.float32)


def shard_levels(key, shape, split, least, high):
    level = 1.0
    for position, shards_of in split:
        steps = jax.random.uniform(jax.random.fold_in(jax.random.fold_in(key, 6), position), (shards_of,), jnp.float32, least / len(split), high / len(split))
        level = level * jnp.repeat(jnp.exp(steps), shape[position] // shards_of).reshape((-1,) + (1,) * (len(shape) - 1 - position))
    return level


def setup_inputs(seed: int = 0) -> dict:
    keys = jax.random.split(jax.random.key(seed), 3)
    divergence = draw_divergence(jax.random.fold_in(keys[2], 71), 0)
    screening = jnp.clip(jnp.exp(math.log(0.1) - 6.9077553 * jax.random.uniform(keys[1], (NX, NY, NZ), jnp.float32) ** shard_levels(keys[1], (NX, NY, NZ), ((0, 32), (1, 8)), -0.2, 0.2)), 0.0001, 0.1)
    return {"divergence": divergence, "screening": screening}


relaxation = 0.8


def neighbour_sum(padded):
    summed = padded[2:, 1:-1, 1:-1] + padded[:-2, 1:-1, 1:-1]
    summed = summed + padded[1:-1, 2:, 1:-1] + padded[1:-1, :-2, 1:-1]
    return summed + padded[1:-1, 1:-1, 2:] + padded[1:-1, 1:-1, :-2]


def operate(iterate, screen):
    return (6.0 + screen) * iterate - neighbour_sum(jnp.pad(iterate, 1))


def relax_sweep(iterate, source, screen):
    return iterate + relaxation * (source - operate(iterate, screen)) / (6.0 + screen)


def coarsen(values):
    extent = values.shape
    blocks = values.reshape(extent[0] // 2, 2, extent[1] // 2, 2, extent[2] // 2, 2)
    return 0.5 * jnp.sum(blocks, axis=(1, 3, 5))


def refine(values):
    return jnp.repeat(jnp.repeat(jnp.repeat(values, 2, axis=0), 2, axis=1), 2, axis=2)


def sine_table(count):
    ladder = jnp.arange(count, dtype=jnp.float32) + 1.0
    return jnp.sin(jnp.pi * ladder[:, None] * ladder[None, :] / (count + 1.0))


def sine_eigen(count):
    ladder = jnp.arange(count, dtype=jnp.float32) + 1.0
    return 2.0 - 2.0 * jnp.cos(jnp.pi * ladder / (count + 1.0))


def transform_all(values, tables):
    first, second, third = tables
    values = jnp.einsum("ai,ijk->ajk", first, values, precision=lax.Precision.HIGHEST)
    values = jnp.einsum("bj,ajk->abk", second, values, precision=lax.Precision.HIGHEST)
    return jnp.einsum("ck,abk->abc", third, values, precision=lax.Precision.HIGHEST)


def coarse_solve(source, screen):
    extent = source.shape
    tables = (sine_table(extent[0]), sine_table(extent[1]), sine_table(extent[2]))
    shift_mean = jnp.mean(screen)
    spectrum = shift_mean + sine_eigen(extent[0])[:, None, None] + sine_eigen(extent[1])[None, :, None] + sine_eigen(extent[2])[None, None, :]
    scaled = transform_all(source, tables) / spectrum
    factor = (2.0 / (extent[0] + 1.0)) * (2.0 / (extent[1] + 1.0)) * (2.0 / (extent[2] + 1.0))
    return factor * transform_all(scaled, tables)


def reference(divergence, screening):
    sources = [divergence]
    screens = [screening]
    smoothed = []
    for level_index in range(3):
        source = sources[level_index]
        screen = screens[level_index]
        iterate = jnp.zeros_like(source)
        for sweep_index in range(SWEEPS):
            iterate = relax_sweep(iterate, source, screen)
        smoothed.append(iterate)
        remainder = source - operate(iterate, screen)
        sources.append(coarsen(remainder))
        screens.append(coarsen(screen) * 0.25)
    iterate = coarse_solve(sources[3], screens[3])
    for level_index in (2, 1, 0):
        iterate = smoothed[level_index] + refine(iterate)
        for sweep_index in range(SWEEPS):
            iterate = relax_sweep(iterate, sources[level_index], screens[level_index])
    return iterate, divergence - operate(iterate, screening)
```

```python
import functools

import numpy as np
import jax
import jax.numpy as jnp
from jax import lax
from jax.experimental import pallas as pl
from jax.experimental.pallas import tpu as pltpu
from jax.sharding import PartitionSpec as P

MESH = pl.DeviceIdType.MESH
F32 = jnp.float32
OMEGA = 0.8
KEEP = 0.2
WINDOW = 24


def sine_table(count):
    ladder = np.arange(count, dtype=np.float64) + 1.0
    return np.sin(np.pi * ladder[:, None] * ladder[None, :] / (count + 1.0))


def sine_eigen(count):
    ladder = np.arange(count, dtype=np.float64) + 1.0
    return 2.0 - 2.0 * np.cos(np.pi * ladder / (count + 1.0))


def tables(wide, narrow):
    count_y, count_z = 4 * narrow, 32
    sine_x, sine_y, sine_z = sine_table(wide), sine_table(count_y), sine_table(count_z)
    to_modes = np.tile(np.repeat(sine_z.T, 2, axis=0), (2, 4))
    from_modes = np.tile(np.repeat(sine_z, 2, axis=1), (4, 2))
    rows_y = 0.5 * np.repeat(sine_y, 2, axis=1)
    rows_y = np.pad(rows_y, ((0, 0), (0, 128 - rows_y.shape[1])))
    eigen_y = sine_eigen(count_y).reshape(4, narrow)
    eigen = eigen_y.T[:, :, None] + sine_eigen(count_z)[None, None, :]
    eigen = eigen.reshape(narrow, 128)
    common = np.concatenate([to_modes, from_modes, rows_y, eigen], axis=0)
    inverse_x = np.pad(sine_x, ((2, 2), (0, 0)))
    inverse_x = np.repeat(inverse_x[:, :, None], 128, axis=2)
    fine_y = np.pad(np.repeat(sine_y, 2, axis=0), ((8, 8), (0, 0)))
    inverse_y = np.zeros((narrow, 4, WINDOW, 128))
    for n in range(narrow):
        for g in range(4):
            inverse_y[n, g, :, :narrow] = fine_y[8 * n : 8 * n + WINDOW, g * narrow : (g + 1) * narrow]
    inverse_y = inverse_y.reshape(narrow, 4 * WINDOW, 128)
    return [a.astype(np.float32) for a in (common, inverse_x, inverse_y)]


def rolled(value, shift, axis):
    return pltpu.roll(value, shift % value.shape[axis], axis)


def lanes_of(rows):
    return lax.broadcasted_iota(jnp.int32, (rows, 128), 1)


def z_sum_halves(low, high):
    lane = lanes_of(low.shape[0])
    up_low, up_high = rolled(low, -1, 1), rolled(high, -1, 1)
    down_low, down_high = rolled(low, 1, 1), rolled(high, 1, 1)
    last, first = lane == 127, lane == 0
    sum_low = jnp.where(last, up_high, up_low) + jnp.where(first, 0.0, down_low)
    sum_high = jnp.where(last, 0.0, up_high) + jnp.where(first, down_low, down_high)
    return sum_low, sum_high


def z_sum(value, period):
    lane = lanes_of(value.shape[0]) % period
    up = jnp.where(lane == period - 1, 0.0, rolled(value, -1, 1))
    return up + jnp.where(lane == 0, 0.0, rolled(value, 1, 1))


def fine_sum(ref, r, a, n):
    centre = [ref[r, h, pl.ds(a, n), :] for h in range(2)]
    along_z = z_sum_halves(*centre)
    summed = []
    for h in range(2):
        along_x = ref[r - 1, h, pl.ds(a, n), :] + ref[r + 1, h, pl.ds(a, n), :]
        along_y = ref[r, h, pl.ds(a - 1, n), :] + ref[r, h, pl.ds(a + 1, n), :]
        summed.append(along_x + along_y + along_z[h])
    return centre, summed


def middle_sum(ref, r, a, n):
    centre = ref[r, pl.ds(a, n), :]
    along_x = ref[r - 1, pl.ds(a, n), :] + ref[r + 1, pl.ds(a, n), :]
    along_y = ref[r, pl.ds(a - 1, n), :] + ref[r, pl.ds(a + 1, n), :]
    return centre, along_x + along_y + z_sum(centre, 128)


def pair_x_sum(before, here, after):
    return here + jnp.where(lanes_of(here.shape[0]) < 64, before, after)


def fold_lanes(low, high):
    rows = low.shape[0]
    lane = lanes_of(rows)
    index = (lane * 2) % 128
    low = jnp.take_along_axis(low + rolled(low, -1, 1), index, axis=1)
    high = jnp.take_along_axis(high + rolled(high, -1, 1), index, axis=1)
    return jnp.where(lane < 64, low, high)


def spread_lanes(value):
    lane = lanes_of(value.shape[0])
    index = lane // 2
    return jnp.take_along_axis(value, index, axis=1), jnp.take_along_axis(value, index + 64, axis=1)


def dot(a, b):
    return jnp.dot(a, b, precision=lax.Precision.HIGHEST, preferred_element_type=F32)


def cycle_kernel(
    W, N,
    f_hbm, s_hbm, common_hbm, invx_hbm, invy_hbm,
    out_hbm, res_hbm,
    f_in, s_in, common, invx, invy, out_v, res_v,
    va, wa, v2a, ua, ub, fold,
    vb, wb, v2b, tb, ub1, ub2, fb, db, foldb,
    gvw, gv2, t2, u2,
    modes,
    in_sem, out_sem, send_sem, recv_sem, gather_send, gather_recv, wide_send, wide_recv,
):
    i = lax.axis_index("wide")
    n = lax.axis_index("narrow")

    loads = [
        pltpu.make_async_copy(src, dst, in_sem.at[k])
        for k, (src, dst) in enumerate(
            (
                (s_hbm, s_in),
                (f_hbm, f_in),
                (common_hbm, common),
                (invx_hbm.at[pl.ds(i, 5)], invx),
                (invy_hbm.at[n], invy),
            )
        )
    ]
    for load in loads:
        load.start()

    barrier = pltpu.get_barrier_semaphore()

    def greet(wide_id, narrow_id):
        pl.semaphore_signal(barrier, inc=1, device_id=(wide_id, narrow_id), device_id_type=MESH)

    has_low, has_high = i > 0, i < W - 1

    def greet_narrow(k, _):
        other = lax.rem(n + k, N)
        greet(i, other)

        @pl.when(has_low)
        def _():
            greet(i - 1, other)

        @pl.when(has_high)
        def _():
            greet(i + 1, other)

        return 0

    lax.fori_loop(1, N, greet_narrow, 0)

    def greet_wide(k, _):
        greet(lax.rem(i + k, W), n)
        return 0

    lax.fori_loop(1, W, greet_wide, 0)

    def zero(ref, *index):
        shape = ref.at[index].shape if index else ref.shape
        ref[index if index else ...] = jnp.zeros(shape, F32)

    all_ = slice(None)

    @pl.when(i == 0)
    def _():
        for ref in (va, wa):
            zero(ref, pl.ds(0, 4))
        for ref in (vb, wb, v2b):
            zero(ref, pl.ds(0, 4))
        zero(gvw, pl.ds(0, 2))
        zero(gv2, pl.ds(0, 2))

    @pl.when(i == W - 1)
    def _():
        for ref in (va, wa):
            zero(ref, pl.ds(12, 4))
        for ref in (vb, wb, v2b):
            zero(ref, pl.ds(8, 4))
        zero(gvw, pl.ds(3, 2))
        zero(gv2, pl.ds(3, 2))

    @pl.when(i == 1)
    def _():
        zero(gvw, 0)
        zero(gv2, 0)

    @pl.when(i == W - 2)
    def _():
        zero(gvw, 4)
        zero(gv2, 4)

    @pl.when(n == 0)
    def _():
        for ref in (va, wa):
            zero(ref, all_, all_, pl.ds(0, 8))
        for ref in (vb, wb, v2b):
            zero(ref, all_, pl.ds(0, 8))

    @pl.when(n == N - 1)
    def _():
        for ref in (va, wa):
            zero(ref, all_, all_, pl.ds(40, 8))
        for ref in (vb, wb, v2b):
            zero(ref, all_, pl.ds(24, 8))

    cols = 8 * N
    zero(gvw, pl.ds(1, 3), all_, pl.ds(0, 8))
    zero(gvw, pl.ds(1, 3), all_, pl.ds(8 + cols, 8))
    zero(gv2, 2, pl.ds(0, 8))
    zero(gv2, 2, pl.ds(8 + cols, 8))
    zero(t2, all_, pl.ds(0, 8))
    zero(t2, all_, pl.ds(8 + cols, 8))

    loads[0].wait()
    loads[1].wait()

    def start_fine(r, _):
        for h in range(2):
            screen = s_in[r, :, pl.ds(128 * h, 128)]
            weight = OMEGA / (6.0 + screen)
            wa[r + 4, h, pl.ds(8, 32), :] = weight
            va[r + 4, h, pl.ds(8, 32), :] = f_in[r, :, pl.ds(128 * h, 128)] * weight
        return 0

    lax.fori_loop(0, 8, start_fine, 0)

    counter = [0]

    def span(step, first, size, depths):
        if step == 0:
            return pl.ds(first, size), pl.ds(first, size)
        low, high = depths
        count = high - low + 1
        if step > 0:
            return pl.ds(first + size - high, count), pl.ds(first - high, count)
        return pl.ds(first + low - 1, count), pl.ds(first + size + low - 1, count)

    def there(dx, dy):
        terms = []
        if dx > 0:
            terms.append(i < W - dx)
        if dx < 0:
            terms.append(i >= -dx)
        if dy > 0:
            terms.append(n < N - dy)
        if dy < 0:
            terms.append(n >= -dy)
        return functools.reduce(jnp.logical_and, terms)

    def exchange(src, dst, dx, dy):
        k = counter[0]
        counter[0] += 1
        copy = pltpu.make_async_remote_copy(
            src_ref=src, dst_ref=dst, send_sem=send_sem.at[k], recv_sem=recv_sem.at[k],
            device_id=(lax.rem(i + dx + W, W), lax.rem(n + dy + N, N)), device_id_type=MESH,
        )
        return copy, there(dx, dy), there(-dx, -dy)

    def fine_piece(ref, dx, dy, depth_x=None, depth_y=None):
        src_x, dst_x = span(dx, 4, 8, depth_x)
        src_y, dst_y = span(dy, 8, 32, depth_y)
        return exchange(ref.at[src_x, :, src_y, :], ref.at[dst_x, :, dst_y, :], dx, dy)

    def middle_piece(ref, dx, dy, depth_x=None, depth_y=None):
        src_x, dst_x = span(dx, 4, 4, depth_x)
        src_y, dst_y = span(dy, 8, 16, depth_y)
        return exchange(ref.at[src_x, src_y, :], ref.at[dst_x, dst_y, :], dx, dy)

    sides = (-1, 1)
    corners = [(dx, dy) for dx in sides for dy in sides]

    def start(pieces):
        for copy, to, _ in pieces:
            pl.when(to)(copy.start)

    def receive(pieces):
        for copy, _, come in pieces:
            pl.when(come)(copy.wait_recv)

    def sent(pieces):
        for copy, to, _ in pieces:
            pl.when(to)(copy.wait_send)

    fine_near = (
        [fine_piece(va, 0, d, None, (1, 2)) for d in sides]
        + [fine_piece(wa, 0, d, None, (1, 1)) for d in sides]
        + [fine_piece(va, dx, dy, (1, 1), (1, 1)) for dx, dy in corners]
        + [fine_piece(va, d, 0, (1, 2)) for d in sides]
        + [fine_piece(wa, d, 0, (1, 1)) for d in sides]
    )
    fine_far = (
        [fine_piece(va, 0, d, None, (3, 4)) for d in sides]
        + [fine_piece(wa, 0, d, None, (2, 3)) for d in sides]
        + [fine_piece(va, dx, dy, (1, 1), (2, 3)) for dx, dy in corners]
        + [fine_piece(va, dx, dy, (2, 3), (1, 2)) for dx, dy in corners]
        + [fine_piece(wa, dx, dy, (1, 2), (1, 2)) for dx, dy in corners]
        + [fine_piece(va, d, 0, (3, 4)) for d in sides]
        + [fine_piece(wa, d, 0, (2, 3)) for d in sides]
    )

    def middle_pieces(ref, depth, corner):
        return (
            [middle_piece(ref, 0, d, None, (1, depth)) for d in sides]
            + [middle_piece(ref, dx, dy, (1, corner), (1, corner)) for dx, dy in corners]
            + [middle_piece(ref, d, 0, (1, depth)) for d in sides]
        )

    middle_w = middle_pieces(wb, 3, 2)
    middle_v = middle_pieces(vb, 3, 2)
    middle_v2 = middle_pieces(v2b, 4, 3)

    window = pl.ds(pl.multiple_of(8 * n, 8), WINDOW)
    coarse_far = [exchange(gv2.at[2, window, :], gv2.at[2 - d, window, :], d, 0) for d in (-1, 1, -2, 2)]
    coarse_far += [exchange(gvw.at[2, :, window, :], gvw.at[2 - d, :, window, :], d, 0) for d in (-2, 2)]

    greeted = (W - 1) + (N - 1) * (1 + has_low.astype(jnp.int32) + has_high.astype(jnp.int32))
    pl.semaphore_wait(barrier, greeted)

    start(fine_near)
    start(fine_far)

    def screen_middle(q, _):
        for h in range(2):
            lanes = pl.ds(128 * h, 128)
            fold[q, h, :, :] = s_in[2 * q, :, lanes] + s_in[2 * q + 1, :, lanes]
        low, high = (
            fold[q, h, pl.ds(0, 16, stride=2), :] + fold[q, h, pl.ds(1, 16, stride=2), :] for h in range(2)
        )
        diagonal = 6.0 + 0.125 * fold_lanes(low, high)
        db[q, :, :] = diagonal
        wb[q + 4, pl.ds(8, 16), :] = OMEGA / diagonal
        return 0

    lax.fori_loop(0, 4, screen_middle, 0)
    start(middle_w)

    for h in range(2):
        foldb[h, :, :] = (db[2 * h, :, :] - 6.0) + (db[2 * h + 1, :, :] - 6.0)
    low, high = (foldb[h, pl.ds(0, 8, stride=2), :] + foldb[h, pl.ds(1, 8, stride=2), :] for h in range(2))
    coarse_d = 6.0 + 0.125 * fold_lanes(low, high)
    own_cols = pl.ds(pl.multiple_of(8 + 8 * n, 8), 8)
    gvw[2, 1, own_cols, :] = coarse_d

    def fine_v2(a, count, r, _):
        centre, summed = fine_sum(va, r, a, count)
        for h in range(2):
            v2a[r, h, pl.ds(a, count), :] = (1.0 + KEEP) * centre[h] + wa[r, h, pl.ds(a, count), :] * summed[h]
        return 0

    receive(fine_near)
    fine_v2(8, 32, 3, 0)
    lax.fori_loop(4, 12, functools.partial(fine_v2, 7, 34), 0)
    fine_v2(8, 32, 12, 0)

    def fine_residual(ref, r, h, centre, summed):
        lanes = pl.ds(128 * h, 128)
        return f_in[r, :, lanes] - (6.0 + s_in[r, :, lanes]) * centre + summed

    def fine_down(q, _):
        c0, n0 = fine_sum(v2a, 2 * q + 4, 8, 32)
        c1, n1 = fine_sum(v2a, 2 * q + 5, 8, 32)
        for h in range(2):
            fold[q, h, :, :] = fine_residual(v2a, 2 * q, h, c0[h], n0[h]) + fine_residual(
                v2a, 2 * q + 1, h, c1[h], n1[h]
            )
        low, high = (
            fold[q, h, pl.ds(0, 16, stride=2), :] + fold[q, h, pl.ds(1, 16, stride=2), :] for h in range(2)
        )
        source = 0.5 * fold_lanes(low, high)
        fb[q, :, :] = source
        vb[q + 4, pl.ds(8, 16), :] = source * wb[q + 4, pl.ds(8, 16), :]
        return 0

    lax.fori_loop(0, 4, fine_down, 0)
    start(middle_v)

    receive(fine_far)
    lax.fori_loop(1, 15, functools.partial(fine_v2, 4, 40), 0)

    receive(middle_w)
    receive(middle_v)
    for r in range(3, 9):
        centre, summed = middle_sum(vb, r, 4, 24)
        tb[r, pl.ds(4, 24), :] = (1.0 + KEEP) * centre + wb[r, pl.ds(4, 24), :] * summed
    for r in range(4):
        centre, summed = middle_sum(tb, r + 4, 8, 16)
        v2b[r + 4, pl.ds(8, 16), :] = centre
        rest = fb[r, :, :] - db[r, :, :] * centre + summed
        if r % 2 == 0:
            held = rest
        else:
            foldb[r // 2, :, :] = held + rest
    low, high = (foldb[h, pl.ds(0, 8, stride=2), :] + foldb[h, pl.ds(1, 8, stride=2), :] for h in range(2))
    gvw[2, 0, own_cols, :] = 0.5 * fold_lanes(low, high) * (OMEGA / coarse_d)

    def gather_copy(dx, k):
        other = lax.rem(n + k, N)
        target = lax.rem(i + dx + W, W)
        return pltpu.make_async_remote_copy(
            src_ref=gvw.at[2, :, own_cols, :], dst_ref=gvw.at[2 - dx, :, own_cols, :],
            send_sem=gather_send.at[dx + 1, k], recv_sem=gather_recv.at[1 - dx, n],
            device_id=(target, other), device_id_type=MESH,
        )

    def arrived(slot, k):
        other = lax.rem(n + k, N)
        cells = pl.ds(pl.multiple_of(8 + 8 * other, 8), 8)
        return pltpu.make_async_remote_copy(
            src_ref=gvw.at[2, :, own_cols, :], dst_ref=gvw.at[1 + slot, :, cells, :],
            send_sem=gather_send.at[0, 0], recv_sem=gather_recv.at[slot, other],
            device_id=(lax.rem(i + 1, W), n), device_id_type=MESH,
        )

    def gather_start(k, _):
        @pl.when(k > 0)
        def _():
            gather_copy(0, k).start()

        @pl.when(has_low)
        def _():
            gather_copy(-1, k).start()

        @pl.when(has_high)
        def _():
            gather_copy(1, k).start()

        return 0

    def gather_receive(k, _):
        @pl.when(k > 0)
        def _():
            arrived(1, k).wait_recv()

        @pl.when(has_low)
        def _():
            arrived(0, k).wait_recv()

        @pl.when(has_high)
        def _():
            arrived(2, k).wait_recv()

        return 0

    def gather_sent(k, _):
        @pl.when(k > 0)
        def _():
            gather_copy(0, k).wait_send()

        @pl.when(has_low)
        def _():
            gather_copy(-1, k).wait_send()

        @pl.when(has_high)
        def _():
            gather_copy(1, k).wait_send()

        return 0

    lax.fori_loop(0, N, gather_start, 0)
    start(middle_v2)
    lax.fori_loop(0, N, gather_receive, 0)

    slab = pl.ds(8, cols)
    turned = [rolled(gvw[t, 0, slab, :], 64, 1) for t in (1, 2, 3)]
    for t in range(3):
        centre = gvw[t + 1, 0, slab, :]
        along_x = pair_x_sum(turned[max(t - 1, 0)], turned[t], turned[min(t + 1, 2)])
        along_y = gvw[t + 1, 0, pl.ds(7, cols), :] + gvw[t + 1, 0, pl.ds(9, cols), :]
        diagonal = gvw[t + 1, 1, slab, :]
        weight = jnp.where(diagonal > 0.0, OMEGA / diagonal, 0.0)
        t2[t, slab, :] = (1.0 + KEEP) * centre + weight * (along_x + along_y + z_sum(centre, 64))
    turned = [rolled(t2[t, slab, :], 64, 1) for t in range(3)]
    centre = t2[1, slab, :]
    gv2[2, slab, :] = centre
    diagonal = gvw[2, 1, slab, :]
    along_x = pair_x_sum(*turned)
    along_y = t2[1, pl.ds(7, cols), :] + t2[1, pl.ds(9, cols), :]
    rest = diagonal * (gvw[2, 0, slab, :] * (1.0 / OMEGA) - centre) + (along_x + along_y + z_sum(centre, 64))

    for load in loads[2:]:
        load.wait()
    along_z = dot(rest, common[pl.ds(0, 128), :])
    along_yz = dot(common[pl.ds(256, 4 * N), pl.ds(0, cols)], along_z)
    group = lanes_of(N) // 32
    mine = along_yz[0:N, :]
    for g in range(1, 4):
        mine = jnp.where(group == g, along_yz[g * N : (g + 1) * N, :], mine)
    modes[i, pl.ds(0, N), :] = mine
    modes[i, pl.ds(N, 1), :] = jnp.sum(diagonal - 6.0, axis=0, keepdims=True)

    def wide_copy(k):
        return pltpu.make_async_remote_copy(
            src_ref=modes.at[i], dst_ref=modes.at[i], send_sem=wide_send.at[k], recv_sem=wide_recv.at[i],
            device_id=(lax.rem(i + k, W), n), device_id_type=MESH,
        )

    def wide_start(k, _):
        wide_copy(k).start()
        return 0

    def wide_receive(k, _):
        other = lax.rem(i + k, W)
        pltpu.make_async_remote_copy(
            src_ref=modes.at[i], dst_ref=modes.at[other], send_sem=wide_send.at[0], recv_sem=wide_recv.at[other],
            device_id=(other, n), device_id_type=MESH,
        ).wait_recv()
        return 0

    def wide_sent(k, _):
        wide_copy(k).wait_send()
        return 0

    lax.fori_loop(1, W, wide_start, 0)
    start(coarse_far)
    receive(middle_v2)
    lax.fori_loop(1, W, wide_receive, 0)

    total = jnp.sum(modes[:, N, :], keepdims=True)
    mean = total * (1.0 / (2 * W * 8 * N * 64))
    shifted = common[pl.ds(256 + 4 * N, N), :] + mean
    sine_x, eigen_x = sine_table(W), sine_eigen(W)
    factor = (2.0 / (W + 1.0)) * (2.0 / (4 * N + 1.0)) * (2.0 / 33.0)
    half = W // 2
    even, odd = [], []
    for j in range(half):
        first, second = modes[j, pl.ds(0, N), :], modes[W - 1 - j, pl.ds(0, N), :]
        even.append(first + second)
        odd.append(first - second)
    found = [None] * 5
    for a in range(W):
        values = even if a % 2 == 0 else odd
        acc = None
        for j in range(half):
            term = values[j] * np.float32(sine_x[a, j])
            acc = term if acc is None else acc + term
        scaled = acc * np.float32(factor) / (shifted + np.float32(eigen_x[a]))
        for t in range(5):
            term = invx[t, pl.ds(a, 1), :] * scaled
            found[t] = term if found[t] is None else found[t] + term
    spread = dot(invy[:, pl.ds(0, N)], jnp.concatenate(found, axis=1))
    group = lanes_of(WINDOW) // 32
    parts = []
    for t in range(5):
        lanes = slice(128 * t, 128 * t + 128)
        part = spread[0:WINDOW, lanes]
        for g in range(1, 4):
            part = jnp.where(group == g, spread[g * WINDOW : (g + 1) * WINDOW, lanes], part)
        parts.append(part)
    correction = dot(jnp.concatenate(parts, axis=0), common[pl.ds(128, 128), :])

    receive(coarse_far)
    u = [gv2[t, window, :] + correction[WINDOW * t : WINDOW * (t + 1), :] for t in range(5)]

    def pair_sweep(u, slots):
        turned = {t: rolled(u[t], 64, 1) for t in u}
        swept = {}
        for t in slots:
            along_x = pair_x_sum(turned.get(t - 1, turned[t]), turned[t], turned.get(t + 1, turned[t]))
            along_y = rolled(u[t], 1, 0) + rolled(u[t], -1, 0)
            diagonal = gvw[t, 1, window, :]
            weight = jnp.where(diagonal > 0.0, OMEGA / diagonal, 0.0)
            summed = along_x + along_y + z_sum(u[t], 64)
            swept[t] = KEEP * u[t] + gvw[t, 0, window, :] + weight * summed
        return swept

    u = pair_sweep(dict(enumerate(u)), range(5))
    u = pair_sweep(u, range(1, 4))

    for t in (1, 2, 3):
        u2[t - 1, :, :] = u[t]
    for t in range(3):
        halves = spread_lanes(u2[t, pl.ds(4, 16), :])
        for h in range(2):
            for k in range(2):
                r = 4 * t + 2 * h + k
                ub1[r, pl.ds(0, 16, stride=2), :] = halves[h]
                ub1[r, pl.ds(1, 16, stride=2), :] = halves[h]
    for r in range(12):
        ub1[r, :, :] = ub1[r, :, :] + v2b[r, :, :]

    def middle_sweep(src, dst, r):
        centre, summed = middle_sum(src, r, 4, 24)
        part = (r, pl.ds(4, 24), slice(None))
        dst[part] = KEEP * centre + vb[part] + wb[part] * summed

    for r in range(1, 11):
        middle_sweep(ub1, ub2, r)
    for r in range(2, 10):
        middle_sweep(ub2, ub1, r)

    def fine_spread(q, _):
        halves = spread_lanes(ub1[q + 2, pl.ds(4, 24), :])
        for k in range(2):
            r = 2 * q + k
            for h in range(2):
                ua[r, h, pl.ds(0, 24, stride=2), :] = halves[h]
                ua[r, h, pl.ds(1, 24, stride=2), :] = halves[h]
        for k in range(2):
            r = 2 * q + k
            for h in range(2):
                ua[r, h, :, :] = ua[r, h, :, :] + v2a[r, h, :, :]
        return 0

    lax.fori_loop(0, 8, fine_spread, 0)

    def fine_sweep(src, dst, r, _):
        centre, summed = fine_sum(src, r, 4, 40)
        for h in range(2):
            part = (r, h, pl.ds(4, 40), slice(None))
            dst[part] = KEEP * centre[h] + va[part] + wa[part] * summed[h]
        return 0

    lax.fori_loop(2, 14, functools.partial(fine_sweep, ua, ub), 0)
    lax.fori_loop(3, 13, functools.partial(fine_sweep, ub, ua), 0)

    def fine_end(r, _):
        centre, summed = fine_sum(ua, r + 4, 8, 32)
        for h in range(2):
            lanes = pl.ds(128 * h, 128)
            out_v[r, :, lanes] = centre[h]
            res_v[r, :, lanes] = fine_residual(ua, r, h, centre[h], summed[h])
        return 0

    lax.fori_loop(0, 8, fine_end, 0)
    stores = [
        pltpu.make_async_copy(out_v, out_hbm, out_sem.at[0]),
        pltpu.make_async_copy(res_v, res_hbm, out_sem.at[1]),
    ]
    for store in stores:
        store.start()

    for pieces in (fine_near, fine_far, middle_w, middle_v, middle_v2, coarse_far):
        sent(pieces)
    lax.fori_loop(0, N, gather_sent, 0)
    lax.fori_loop(1, W, wide_sent, 0)
    for store in stores:
        store.wait()


def solution(mesh):
    W, N = mesh.shape["wide"], mesh.shape["narrow"]
    common, invx, invy = tables(W, N)
    cols = 8 * N
    vmem = pltpu.VMEM
    dma = pltpu.SemaphoreType.DMA
    fine, middle = (16, 2, 48, 128), (12, 32, 128)
    scratch = [
        vmem((8, 32, 256), F32), vmem((8, 32, 256), F32),
        vmem(common.shape, F32), vmem((5, W, 128), F32), vmem((4 * WINDOW, 128), F32),
        vmem((8, 32, 256), F32), vmem((8, 32, 256), F32),
        vmem(fine, F32), vmem(fine, F32), vmem(fine, F32), vmem(fine, F32), vmem(fine, F32),
        vmem((4, 2, 32, 128), F32),
        vmem(middle, F32), vmem(middle, F32), vmem(middle, F32), vmem(middle, F32),
        vmem(middle, F32), vmem(middle, F32),
        vmem((4, 16, 128), F32), vmem((4, 16, 128), F32), vmem((2, 16, 128), F32),
        vmem((5, 2, cols + 16, 128), F32), vmem((5, cols + 16, 128), F32),
        vmem((3, cols + 16, 128), F32), vmem((3, WINDOW, 128), F32),
        vmem((W, N + 1, 128), F32),
        dma((5,)), dma((2,)), dma((70,)), dma((70,)), dma((3, N)), dma((3, N)), dma((W,)), dma((W,)),
    ]

    def per_device(divergence, screening):
        block = jax.ShapeDtypeStruct((8, 32, 256), F32)
        anywhere = pl.BlockSpec(memory_space=pl.ANY)
        return pl.pallas_call(
            functools.partial(cycle_kernel, W, N),
            out_shape=(block, block),
            in_specs=[anywhere] * 5,
            out_specs=(anywhere, anywhere),
            scratch_shapes=scratch,
            compiler_params=pltpu.CompilerParams(
                collective_id=0, has_side_effects=True, vmem_limit_bytes=32 * 1024 * 1024
            ),
        )(divergence, screening, jnp.asarray(common), jnp.asarray(invx), jnp.asarray(invy))

    spec = P("wide", "narrow", None)
    return jax.shard_map(
        per_device, mesh=mesh, in_specs=(spec, spec), out_specs=(spec, spec), check_vma=False
    )
```

```python
import functools

import numpy as np
import jax
import jax.numpy as jnp
from jax import lax
from jax.experimental import pallas as pl
from jax.experimental.pallas import tpu as pltpu
from jax.sharding import PartitionSpec as P

MESH = pl.DeviceIdType.MESH
F32 = jnp.float32
OMEGA = 0.8
KEEP = 0.2
WINDOW = 24


def sine_table(count):
    ladder = np.arange(count, dtype=np.float64) + 1.0
    return np.sin(np.pi * ladder[:, None] * ladder[None, :] / (count + 1.0))


def sine_eigen(count):
    ladder = np.arange(count, dtype=np.float64) + 1.0
    return 2.0 - 2.0 * np.cos(np.pi * ladder / (count + 1.0))


def tables(wide, narrow):
    count_y, count_z = 4 * narrow, 32
    sine_x, sine_y, sine_z = sine_table(wide), sine_table(count_y), sine_table(count_z)
    to_modes = np.tile(np.repeat(sine_z.T, 2, axis=0), (2, 4))
    from_modes = np.tile(np.repeat(sine_z, 2, axis=1), (4, 2))
    rows_y = 0.5 * np.repeat(sine_y, 2, axis=1)
    rows_y = np.pad(rows_y, ((0, 0), (0, 128 - rows_y.shape[1])))
    eigen_y = sine_eigen(count_y).reshape(4, narrow)
    eigen = eigen_y.T[:, :, None] + sine_eigen(count_z)[None, None, :]
    eigen = eigen.reshape(narrow, 128)
    common = np.concatenate([to_modes, from_modes, rows_y, eigen], axis=0)
    inverse_x = np.pad(sine_x, ((2, 2), (0, 0)))
    inverse_x = np.repeat(inverse_x[:, :, None], 128, axis=2)
    fine_y = np.pad(np.repeat(sine_y, 2, axis=0), ((8, 8), (0, 0)))
    inverse_y = np.zeros((narrow, 4, WINDOW, 128))
    for n in range(narrow):
        for g in range(4):
            inverse_y[n, g, :, :narrow] = fine_y[8 * n : 8 * n + WINDOW, g * narrow : (g + 1) * narrow]
    inverse_y = inverse_y.reshape(narrow, 4 * WINDOW, 128)
    return [a.astype(np.float32) for a in (common, inverse_x, inverse_y)]


def rolled(value, shift, axis):
    return pltpu.roll(value, shift % value.shape[axis], axis)


def lanes_of(rows):
    return lax.broadcasted_iota(jnp.int32, (rows, 128), 1)


def z_sum_halves(low, high):
    lane = lanes_of(low.shape[0])
    up_low, up_high = rolled(low, -1, 1), rolled(high, -1, 1)
    down_low, down_high = rolled(low, 1, 1), rolled(high, 1, 1)
    last, first = lane == 127, lane == 0
    sum_low = jnp.where(last, up_high, up_low) + jnp.where(first, 0.0, down_low)
    sum_high = jnp.where(last, 0.0, up_high) + jnp.where(first, down_low, down_high)
    return sum_low, sum_high


def z_sum(value, period):
    lane = lanes_of(value.shape[0]) % period
    up = jnp.where(lane == period - 1, 0.0, rolled(value, -1, 1))
    return up + jnp.where(lane == 0, 0.0, rolled(value, 1, 1))


def fine_sum(ref, r, a, n):
    centre = [ref[r, h, pl.ds(a, n), :] for h in range(2)]
    along_z = z_sum_halves(*centre)
    summed = []
    for h in range(2):
        along_x = ref[r - 1, h, pl.ds(a, n), :] + ref[r + 1, h, pl.ds(a, n), :]
        along_y = ref[r, h, pl.ds(a - 1, n), :] + ref[r, h, pl.ds(a + 1, n), :]
        summed.append(along_x + along_y + along_z[h])
    return centre, summed


def middle_sum(ref, r, a, n):
    centre = ref[r, pl.ds(a, n), :]
    along_x = ref[r - 1, pl.ds(a, n), :] + ref[r + 1, pl.ds(a, n), :]
    along_y = ref[r, pl.ds(a - 1, n), :] + ref[r, pl.ds(a + 1, n), :]
    return centre, along_x + along_y + z_sum(centre, 128)


def pair_x_sum(before, here, after):
    return here + jnp.where(lanes_of(here.shape[0]) < 64, before, after)


def fold_lanes(low, high):
    rows = low.shape[0]
    lane = lanes_of(rows)
    index = (lane * 2) % 128
    low = jnp.take_along_axis(low + rolled(low, -1, 1), index, axis=1)
    high = jnp.take_along_axis(high + rolled(high, -1, 1), index, axis=1)
    return jnp.where(lane < 64, low, high)


def spread_lanes(value):
    lane = lanes_of(value.shape[0])
    index = lane // 2
    return jnp.take_along_axis(value, index, axis=1), jnp.take_along_axis(value, index + 64, axis=1)


def dot(a, b):
    return jnp.dot(a, b, precision=lax.Precision.HIGHEST, preferred_element_type=F32)


def cycle_kernel(
    W, N,
    f_hbm, s_hbm, common_hbm, invx_hbm, invy_hbm,
    out_hbm, res_hbm,
    f_in, s_in, common, invx, invy, out_v, res_v,
    va, wa, v2a, ua, ub, fold,
    vb, wb, v2b, tb, ub1, ub2, fb, db, foldb,
    gvw, gv2, t2, u2,
    modes,
    in_sem, out_sem, send_sem, recv_sem, gather_send, gather_recv, wide_send, wide_recv,
):
    i = lax.axis_index("wide")
    n = lax.axis_index("narrow")

    loads = [
        pltpu.make_async_copy(src, dst, in_sem.at[k])
        for k, (src, dst) in enumerate(
            (
                (s_hbm, s_in),
                (f_hbm, f_in),
                (common_hbm, common),
                (invx_hbm.at[pl.ds(i, 5)], invx),
                (invy_hbm.at[n], invy),
            )
        )
    ]
    barrier = pltpu.get_barrier_semaphore()

    def greet(wide_id, narrow_id):
        pl.semaphore_signal(barrier, inc=1, device_id=(wide_id, narrow_id), device_id_type=MESH)

    has_low, has_high = i > 0, i < W - 1

    def there(dx, dy):
        terms = []
        if dx > 0:
            terms.append(i < W - dx)
        if dx < 0:
            terms.append(i >= -dx)
        if dy > 0:
            terms.append(n < N - dy)
        if dy < 0:
            terms.append(n >= -dy)
        return functools.reduce(jnp.logical_and, terms)

    sides = (-1, 1)
    corners = [(dx, dy) for dx in sides for dy in sides]
    for dx, dy in [(0, -1), (0, 1)] + corners + [(-1, 0), (1, 0)]:
        pl.when(there(dx, dy))(functools.partial(greet, i + dx, n + dy))

    for load in loads:
        load.start()

    def greet_narrow(k, _):
        other = lax.rem(n + k, N)

        @pl.when(jnp.logical_and(other != n - 1, other != n + 1))
        def _():
            greet_column(other)

        return 0

    def greet_column(other):
        greet(i, other)

        @pl.when(has_low)
        def _():
            greet(i - 1, other)

        @pl.when(has_high)
        def _():
            greet(i + 1, other)

    lax.fori_loop(1, N, greet_narrow, 0)

    def greet_wide(k, _):
        other = lax.rem(i + k, W)

        @pl.when(jnp.logical_and(other != i - 1, other != i + 1))
        def _():
            greet(other, n)

        return 0

    lax.fori_loop(1, W, greet_wide, 0)

    def zero(ref, *index):
        shape = ref.at[index].shape if index else ref.shape
        ref[index if index else ...] = jnp.zeros(shape, F32)

    all_ = slice(None)

    @pl.when(i == 0)
    def _():
        for ref in (va, wa):
            zero(ref, pl.ds(0, 4))
        for ref in (vb, wb, v2b):
            zero(ref, pl.ds(0, 4))
        zero(gvw, pl.ds(0, 2))
        zero(gv2, pl.ds(0, 2))

    @pl.when(i == W - 1)
    def _():
        for ref in (va, wa):
            zero(ref, pl.ds(12, 4))
        for ref in (vb, wb, v2b):
            zero(ref, pl.ds(8, 4))
        zero(gvw, pl.ds(3, 2))
        zero(gv2, pl.ds(3, 2))

    @pl.when(i == 1)
    def _():
        zero(gvw, 0)
        zero(gv2, 0)

    @pl.when(i == W - 2)
    def _():
        zero(gvw, 4)
        zero(gv2, 4)

    @pl.when(n == 0)
    def _():
        for ref in (va, wa):
            zero(ref, all_, all_, pl.ds(0, 8))
        for ref in (vb, wb, v2b):
            zero(ref, all_, pl.ds(0, 8))

    @pl.when(n == N - 1)
    def _():
        for ref in (va, wa):
            zero(ref, all_, all_, pl.ds(40, 8))
        for ref in (vb, wb, v2b):
            zero(ref, all_, pl.ds(24, 8))

    cols = 8 * N
    zero(gvw, pl.ds(1, 3), all_, pl.ds(0, 8))
    zero(gvw, pl.ds(1, 3), all_, pl.ds(8 + cols, 8))
    zero(gv2, 2, pl.ds(0, 8))
    zero(gv2, 2, pl.ds(8 + cols, 8))
    zero(t2, all_, pl.ds(0, 8))
    zero(t2, all_, pl.ds(8 + cols, 8))

    loads[0].wait()
    loads[1].wait()

    def start_fine(r, _):
        for h in range(2):
            screen = s_in[r, :, pl.ds(128 * h, 128)]
            weight = OMEGA / (6.0 + screen)
            wa[r + 4, h, pl.ds(8, 32), :] = weight
            va[r + 4, h, pl.ds(8, 32), :] = f_in[r, :, pl.ds(128 * h, 128)] * weight
        return 0

    lax.fori_loop(0, 8, start_fine, 0, unroll=True)

    counter = [0]

    def span(step, first, size, depths):
        if step == 0:
            return pl.ds(first, size), pl.ds(first, size)
        low, high = depths
        count = high - low + 1
        if step > 0:
            return pl.ds(first + size - high, count), pl.ds(first - high, count)
        return pl.ds(first + low - 1, count), pl.ds(first + size + low - 1, count)

    def exchange(src, dst, dx, dy):
        k = counter[0]
        counter[0] += 1
        copy = pltpu.make_async_remote_copy(
            src_ref=src, dst_ref=dst, send_sem=send_sem.at[k], recv_sem=recv_sem.at[k],
            device_id=(lax.rem(i + dx + W, W), lax.rem(n + dy + N, N)), device_id_type=MESH,
        )
        return copy, there(dx, dy), there(-dx, -dy)

    def fine_piece(ref, dx, dy, depth_x=None, depth_y=None):
        src_x, dst_x = span(dx, 4, 8, depth_x)
        src_y, dst_y = span(dy, 8, 32, depth_y)
        return exchange(ref.at[src_x, :, src_y, :], ref.at[dst_x, :, dst_y, :], dx, dy)

    def middle_piece(ref, dx, dy, depth_x=None, depth_y=None):
        src_x, dst_x = span(dx, 4, 4, depth_x)
        src_y, dst_y = span(dy, 8, 16, depth_y)
        return exchange(ref.at[src_x, src_y, :], ref.at[dst_x, dst_y, :], dx, dy)

    def start(pieces):
        for copy, to, _ in pieces:
            pl.when(to)(copy.start)

    def receive(pieces):
        for copy, _, come in pieces:
            pl.when(come)(copy.wait_recv)

    def sent(pieces):
        for copy, to, _ in pieces:
            pl.when(to)(copy.wait_send)

    fine_near = (
        [fine_piece(va, 0, d, None, (1, 2)) for d in sides]
        + [fine_piece(wa, 0, d, None, (1, 1)) for d in sides]
        + [fine_piece(va, dx, dy, (1, 1), (1, 1)) for dx, dy in corners]
        + [fine_piece(va, d, 0, (1, 2)) for d in sides]
        + [fine_piece(wa, d, 0, (1, 1)) for d in sides]
    )
    fine_far = (
        [fine_piece(va, 0, d, None, (3, 4)) for d in sides]
        + [fine_piece(wa, 0, d, None, (2, 3)) for d in sides]
        + [fine_piece(va, dx, dy, (1, 1), (2, 3)) for dx, dy in corners]
        + [fine_piece(va, dx, dy, (2, 3), (1, 2)) for dx, dy in corners]
        + [fine_piece(wa, dx, dy, (1, 2), (1, 2)) for dx, dy in corners]
        + [fine_piece(va, d, 0, (3, 4)) for d in sides]
        + [fine_piece(wa, d, 0, (2, 3)) for d in sides]
    )

    def middle_pieces(ref, depth, corner):
        return (
            [middle_piece(ref, 0, d, None, (1, depth)) for d in sides]
            + [middle_piece(ref, dx, dy, (1, corner), (1, corner)) for dx, dy in corners]
            + [middle_piece(ref, d, 0, (1, depth)) for d in sides]
        )

    middle_w = middle_pieces(wb, 3, 2)
    middle_v = middle_pieces(vb, 3, 2)
    middle_v2 = middle_pieces(v2b, 4, 3)

    window = pl.ds(pl.multiple_of(8 * n, 8), WINDOW)
    coarse_far = [exchange(gv2.at[2, window, :], gv2.at[2 - d, window, :], d, 0) for d in (-1, 1, -2, 2)]
    coarse_far += [exchange(gvw.at[2, :, window, :], gvw.at[2 - d, :, window, :], d, 0) for d in (-2, 2)]

    greeted = (W - 1) + (N - 1) * (1 + has_low.astype(jnp.int32) + has_high.astype(jnp.int32))
    pl.semaphore_wait(barrier, greeted)

    start(fine_near)
    start(fine_far)

    def screen_middle(q, _):
        for h in range(2):
            lanes = pl.ds(128 * h, 128)
            fold[q, h, :, :] = s_in[2 * q, :, lanes] + s_in[2 * q + 1, :, lanes]
        low, high = (
            fold[q, h, pl.ds(0, 16, stride=2), :] + fold[q, h, pl.ds(1, 16, stride=2), :] for h in range(2)
        )
        diagonal = 6.0 + 0.125 * fold_lanes(low, high)
        db[q, :, :] = diagonal
        wb[q + 4, pl.ds(8, 16), :] = OMEGA / diagonal
        return 0

    lax.fori_loop(0, 4, screen_middle, 0, unroll=True)
    start(middle_w)

    for h in range(2):
        foldb[h, :, :] = (db[2 * h, :, :] - 6.0) + (db[2 * h + 1, :, :] - 6.0)
    low, high = (foldb[h, pl.ds(0, 8, stride=2), :] + foldb[h, pl.ds(1, 8, stride=2), :] for h in range(2))
    coarse_d = 6.0 + 0.125 * fold_lanes(low, high)
    own_cols = pl.ds(pl.multiple_of(8 + 8 * n, 8), 8)
    gvw[2, 1, own_cols, :] = coarse_d

    def gather_copy(what, dx, k):
        other = lax.rem(n + k, N)
        target = lax.rem(i + dx + W, W)
        return pltpu.make_async_remote_copy(
            src_ref=gvw.at[2, what, own_cols, :], dst_ref=gvw.at[2 - dx, what, own_cols, :],
            send_sem=gather_send.at[what, dx + 1, k], recv_sem=gather_recv.at[what, 1 - dx, n],
            device_id=(target, other), device_id_type=MESH,
        )

    def arrived(what, slot, k):
        other = lax.rem(n + k, N)
        cells = pl.ds(pl.multiple_of(8 + 8 * other, 8), 8)
        return pltpu.make_async_remote_copy(
            src_ref=gvw.at[2, what, own_cols, :], dst_ref=gvw.at[1 + slot, what, cells, :],
            send_sem=gather_send.at[what, 0, 0], recv_sem=gather_recv.at[what, slot, other],
            device_id=(lax.rem(i + 1, W), n), device_id_type=MESH,
        )

    def for_each(k, call):
        pl.when(k > 0)(functools.partial(call, 0))
        pl.when(has_low)(functools.partial(call, -1))
        pl.when(has_high)(functools.partial(call, 1))

    def gather_start(what, k, _):
        for_each(k, lambda dx: gather_copy(what, dx, k).start())
        return 0

    def gather_receive(what, k, _):
        for_each(k, lambda dx: arrived(what, 1 + dx, k).wait_recv())
        return 0

    def gather_sent(what, k, _):
        for_each(k, lambda dx: gather_copy(what, dx, k).wait_send())
        return 0

    lax.fori_loop(0, N, functools.partial(gather_start, 1), 0)

    def fine_v2(a, count, r, _):
        centre, summed = fine_sum(va, r, a, count)
        for h in range(2):
            v2a[r, h, pl.ds(a, count), :] = (1.0 + KEEP) * centre[h] + wa[r, h, pl.ds(a, count), :] * summed[h]
        return 0

    receive(fine_near)
    fine_v2(8, 32, 3, 0)
    lax.fori_loop(4, 12, functools.partial(fine_v2, 7, 34), 0, unroll=True)
    fine_v2(8, 32, 12, 0)

    def fine_residual(ref, r, h, centre, summed):
        lanes = pl.ds(128 * h, 128)
        return f_in[r, :, lanes] - (6.0 + s_in[r, :, lanes]) * centre + summed

    def fine_down(q, _):
        c0, n0 = fine_sum(v2a, 2 * q + 4, 8, 32)
        c1, n1 = fine_sum(v2a, 2 * q + 5, 8, 32)
        for h in range(2):
            fold[q, h, :, :] = fine_residual(v2a, 2 * q, h, c0[h], n0[h]) + fine_residual(
                v2a, 2 * q + 1, h, c1[h], n1[h]
            )
        low, high = (
            fold[q, h, pl.ds(0, 16, stride=2), :] + fold[q, h, pl.ds(1, 16, stride=2), :] for h in range(2)
        )
        source = 0.5 * fold_lanes(low, high)
        fb[q, :, :] = source
        vb[q + 4, pl.ds(8, 16), :] = source * wb[q + 4, pl.ds(8, 16), :]
        return 0

    lax.fori_loop(0, 4, fine_down, 0, unroll=True)
    start(middle_v)

    receive(fine_far)
    lax.fori_loop(1, 15, functools.partial(fine_v2, 4, 40), 0, unroll=True)

    receive(middle_w)
    receive(middle_v)
    for r in range(3, 9):
        centre, summed = middle_sum(vb, r, 4, 24)
        tb[r, pl.ds(4, 24), :] = (1.0 + KEEP) * centre + wb[r, pl.ds(4, 24), :] * summed
    for r in range(4):
        centre, summed = middle_sum(tb, r + 4, 8, 16)
        v2b[r + 4, pl.ds(8, 16), :] = centre
        rest = fb[r, :, :] - db[r, :, :] * centre + summed
        if r % 2 == 0:
            held = rest
        else:
            foldb[r // 2, :, :] = held + rest
    low, high = (foldb[h, pl.ds(0, 8, stride=2), :] + foldb[h, pl.ds(1, 8, stride=2), :] for h in range(2))
    gvw[2, 0, own_cols, :] = 0.5 * fold_lanes(low, high) * (OMEGA / coarse_d)

    lax.fori_loop(0, N, functools.partial(gather_start, 0), 0)
    start(middle_v2)
    lax.fori_loop(0, N, functools.partial(gather_receive, 1), 0)
    lax.fori_loop(0, N, functools.partial(gather_receive, 0), 0)

    slab = pl.ds(8, cols)
    turned = [rolled(gvw[t, 0, slab, :], 64, 1) for t in (1, 2, 3)]
    for t in range(3):
        centre = gvw[t + 1, 0, slab, :]
        along_x = pair_x_sum(turned[max(t - 1, 0)], turned[t], turned[min(t + 1, 2)])
        along_y = gvw[t + 1, 0, pl.ds(7, cols), :] + gvw[t + 1, 0, pl.ds(9, cols), :]
        diagonal = gvw[t + 1, 1, slab, :]
        weight = jnp.where(diagonal > 0.0, OMEGA / diagonal, 0.0)
        t2[t, slab, :] = (1.0 + KEEP) * centre + weight * (along_x + along_y + z_sum(centre, 64))
    turned = [rolled(t2[t, slab, :], 64, 1) for t in range(3)]
    centre = t2[1, slab, :]
    gv2[2, slab, :] = centre
    diagonal = gvw[2, 1, slab, :]
    along_x = pair_x_sum(*turned)
    along_y = t2[1, pl.ds(7, cols), :] + t2[1, pl.ds(9, cols), :]
    rest = diagonal * (gvw[2, 0, slab, :] * (1.0 / OMEGA) - centre) + (along_x + along_y + z_sum(centre, 64))

    for load in loads[2:]:
        load.wait()
    along_z = dot(rest, common[pl.ds(0, 128), :])
    along_yz = dot(common[pl.ds(256, 4 * N), pl.ds(0, cols)], along_z)
    group = lanes_of(N) // 32
    mine = along_yz[0:N, :]
    for g in range(1, 4):
        mine = jnp.where(group == g, along_yz[g * N : (g + 1) * N, :], mine)
    modes[i, pl.ds(0, N), :] = mine
    modes[i, pl.ds(N, 1), :] = jnp.sum(diagonal - 6.0, axis=0, keepdims=True)

    def wide_copy(k):
        return pltpu.make_async_remote_copy(
            src_ref=modes.at[i], dst_ref=modes.at[i], send_sem=wide_send.at[k], recv_sem=wide_recv.at[i],
            device_id=(lax.rem(i + k, W), n), device_id_type=MESH,
        )

    def wide_start(k, _):
        wide_copy(k).start()
        return 0

    def wide_receive(k, _):
        other = lax.rem(i + k, W)
        pltpu.make_async_remote_copy(
            src_ref=modes.at[i], dst_ref=modes.at[other], send_sem=wide_send.at[0], recv_sem=wide_recv.at[other],
            device_id=(other, n), device_id_type=MESH,
        ).wait_recv()
        return 0

    def wide_sent(k, _):
        wide_copy(k).wait_send()
        return 0

    lax.fori_loop(1, W, wide_start, 0)
    start(coarse_far)
    for pieces in (fine_near, fine_far, middle_w, middle_v, middle_v2):
        sent(pieces)
    for what in range(2):
        lax.fori_loop(0, N, functools.partial(gather_sent, what), 0)
    receive(middle_v2)
    lax.fori_loop(1, W, wide_receive, 0)

    total = jnp.sum(modes[:, N, :], keepdims=True)
    mean = total * (1.0 / (2 * W * 8 * N * 64))
    shifted = common[pl.ds(256 + 4 * N, N), :] + mean
    sine_x, eigen_x = sine_table(W), sine_eigen(W)
    factor = (2.0 / (W + 1.0)) * (2.0 / (4 * N + 1.0)) * (2.0 / 33.0)
    half = W // 2
    even, odd = [], []
    for j in range(half):
        first, second = modes[j, pl.ds(0, N), :], modes[W - 1 - j, pl.ds(0, N), :]
        even.append(first + second)
        odd.append(first - second)
    found = [None] * 5
    for a in range(W):
        values = even if a % 2 == 0 else odd
        acc = None
        for j in range(half):
            term = values[j] * np.float32(sine_x[a, j])
            acc = term if acc is None else acc + term
        scaled = acc * np.float32(factor) / (shifted + np.float32(eigen_x[a]))
        for t in range(5):
            term = invx[t, pl.ds(a, 1), :] * scaled
            found[t] = term if found[t] is None else found[t] + term
    spread = dot(invy[:, pl.ds(0, N)], jnp.concatenate(found, axis=1))
    group = lanes_of(WINDOW) // 32
    parts = []
    for t in range(5):
        lanes = slice(128 * t, 128 * t + 128)
        part = spread[0:WINDOW, lanes]
        for g in range(1, 4):
            part = jnp.where(group == g, spread[g * WINDOW : (g + 1) * WINDOW, lanes], part)
        parts.append(part)
    correction = dot(jnp.concatenate(parts, axis=0), common[pl.ds(128, 128), :])

    receive(coarse_far)
    u = [gv2[t, window, :] + correction[WINDOW * t : WINDOW * (t + 1), :] for t in range(5)]

    def pair_sweep(u, slots):
        turned = {t: rolled(u[t], 64, 1) for t in u}
        swept = {}
        for t in slots:
            along_x = pair_x_sum(turned.get(t - 1, turned[t]), turned[t], turned.get(t + 1, turned[t]))
            along_y = rolled(u[t], 1, 0) + rolled(u[t], -1, 0)
            diagonal = gvw[t, 1, window, :]
            weight = jnp.where(diagonal > 0.0, OMEGA / diagonal, 0.0)
            summed = along_x + along_y + z_sum(u[t], 64)
            swept[t] = KEEP * u[t] + gvw[t, 0, window, :] + weight * summed
        return swept

    u = pair_sweep(dict(enumerate(u)), range(5))
    u = pair_sweep(u, range(1, 4))

    for t in (1, 2, 3):
        u2[t - 1, :, :] = u[t]
    for t in range(3):
        halves = spread_lanes(u2[t, pl.ds(4, 16), :])
        for h in range(2):
            for k in range(2):
                r = 4 * t + 2 * h + k
                ub1[r, pl.ds(0, 16, stride=2), :] = halves[h]
                ub1[r, pl.ds(1, 16, stride=2), :] = halves[h]
    for r in range(12):
        ub1[r, :, :] = ub1[r, :, :] + v2b[r, :, :]

    def middle_sweep(src, dst, r):
        centre, summed = middle_sum(src, r, 4, 24)
        part = (r, pl.ds(4, 24), slice(None))
        dst[part] = KEEP * centre + vb[part] + wb[part] * summed

    for r in range(1, 11):
        middle_sweep(ub1, ub2, r)
    for r in range(2, 10):
        middle_sweep(ub2, ub1, r)

    def fine_spread(q, _):
        halves = spread_lanes(ub1[q + 2, pl.ds(4, 24), :])
        for k in range(2):
            r = 2 * q + k
            for h in range(2):
                ua[r, h, pl.ds(0, 24, stride=2), :] = halves[h]
                ua[r, h, pl.ds(1, 24, stride=2), :] = halves[h]
        for k in range(2):
            r = 2 * q + k
            for h in range(2):
                ua[r, h, :, :] = ua[r, h, :, :] + v2a[r, h, :, :]
        return 0

    lax.fori_loop(0, 8, fine_spread, 0, unroll=True)

    def fine_sweep(src, dst, r, _):
        centre, summed = fine_sum(src, r, 4, 40)
        for h in range(2):
            part = (r, h, pl.ds(4, 40), slice(None))
            dst[part] = KEEP * centre[h] + va[part] + wa[part] * summed[h]
        return 0

    lax.fori_loop(2, 14, functools.partial(fine_sweep, ua, ub), 0, unroll=True)
    lax.fori_loop(3, 13, functools.partial(fine_sweep, ub, ua), 0, unroll=True)

    def fine_end(r, _):
        centre, summed = fine_sum(ua, r + 4, 8, 32)
        for h in range(2):
            lanes = pl.ds(128 * h, 128)
            out_v[r, :, lanes] = centre[h]
            res_v[r, :, lanes] = fine_residual(ua, r, h, centre[h], summed[h])
        return 0

    lax.fori_loop(0, 8, fine_end, 0, unroll=True)
    stores = [
        pltpu.make_async_copy(out_v, out_hbm, out_sem.at[0]),
        pltpu.make_async_copy(res_v, res_hbm, out_sem.at[1]),
    ]
    for store in stores:
        store.start()

    sent(coarse_far)
    lax.fori_loop(1, W, wide_sent, 0)
    for store in stores:
        store.wait()


def solution(mesh):
    W, N = mesh.shape["wide"], mesh.shape["narrow"]
    common, invx, invy = tables(W, N)
    cols = 8 * N
    vmem = pltpu.VMEM
    dma = pltpu.SemaphoreType.DMA
    fine, middle = (16, 2, 48, 128), (12, 32, 128)
    scratch = [
        vmem((8, 32, 256), F32), vmem((8, 32, 256), F32),
        vmem(common.shape, F32), vmem((5, W, 128), F32), vmem((4 * WINDOW, 128), F32),
        vmem((8, 32, 256), F32), vmem((8, 32, 256), F32),
        vmem(fine, F32), vmem(fine, F32), vmem(fine, F32), vmem(fine, F32), vmem(fine, F32),
        vmem((4, 2, 32, 128), F32),
        vmem(middle, F32), vmem(middle, F32), vmem(middle, F32), vmem(middle, F32),
        vmem(middle, F32), vmem(middle, F32),
        vmem((4, 16, 128), F32), vmem((4, 16, 128), F32), vmem((2, 16, 128), F32),
        vmem((5, 2, cols + 16, 128), F32), vmem((5, cols + 16, 128), F32),
        vmem((3, cols + 16, 128), F32), vmem((3, WINDOW, 128), F32),
        vmem((W, N + 1, 128), F32),
        dma((5,)), dma((2,)), dma((70,)), dma((70,)), dma((2, 3, N)), dma((2, 3, N)), dma((W,)), dma((W,)),
    ]

    def per_device(divergence, screening):
        block = jax.ShapeDtypeStruct((8, 32, 256), F32)
        anywhere = pl.BlockSpec(memory_space=pl.ANY)
        return pl.pallas_call(
            functools.partial(cycle_kernel, W, N),
            out_shape=(block, block),
            in_specs=[pl.BlockSpec(memory_space=pltpu.HBM)] * 5,
            out_specs=(anywhere, anywhere),
            scratch_shapes=scratch,
            compiler_params=pltpu.CompilerParams(
                collective_id=0, has_side_effects=True, vmem_limit_bytes=32 * 1024 * 1024
            ),
        )(divergence, screening, jnp.asarray(common), jnp.asarray(invx), jnp.asarray(invy))

    spec = P("wide", "narrow", None)
    return jax.shard_map(
        per_device, mesh=mesh, in_specs=(spec, spec), out_specs=(spec, spec), check_vma=False
    )
```

```python
import functools

import numpy as np
import jax
import jax.numpy as jnp
from jax import lax
from jax.experimental import pallas as pl
from jax.experimental.pallas import tpu as pltpu
from jax.sharding import PartitionSpec as P

MESH = pl.DeviceIdType.MESH
F32 = jnp.float32
OMEGA = 0.8
KEEP = 0.2
WINDOW = 24


def sine_table(count):
    ladder = np.arange(count, dtype=np.float64) + 1.0
    return np.sin(np.pi * ladder[:, None] * ladder[None, :] / (count + 1.0))


def sine_eigen(count):
    ladder = np.arange(count, dtype=np.float64) + 1.0
    return 2.0 - 2.0 * np.cos(np.pi * ladder / (count + 1.0))


def tables(wide, narrow):
    count_y, count_z = 4 * narrow, 32
    sine_x, sine_y, sine_z = sine_table(wide), sine_table(count_y), sine_table(count_z)
    to_modes = np.tile(np.repeat(sine_z.T, 2, axis=0), (2, 4))
    from_modes = np.tile(np.repeat(sine_z, 2, axis=1), (4, 2))
    rows_y = 0.5 * np.repeat(sine_y, 2, axis=1)
    rows_y = np.pad(rows_y, ((0, 0), (0, 128 - rows_y.shape[1])))
    eigen_y = sine_eigen(count_y).reshape(4, narrow)
    eigen = eigen_y.T[:, :, None] + sine_eigen(count_z)[None, None, :]
    eigen = eigen.reshape(narrow, 128)
    common = np.concatenate([to_modes, from_modes, rows_y, eigen], axis=0)
    inverse_x = np.pad(sine_x, ((2, 2), (0, 0)))
    inverse_x = np.repeat(inverse_x[:, :, None], 128, axis=2)
    fine_y = np.pad(np.repeat(sine_y, 2, axis=0), ((8, 8), (0, 0)))
    inverse_y = np.zeros((narrow, 4, WINDOW, 128))
    for n in range(narrow):
        for g in range(4):
            inverse_y[n, g, :, :narrow] = fine_y[8 * n : 8 * n + WINDOW, g * narrow : (g + 1) * narrow]
    inverse_y = inverse_y.reshape(narrow, 4 * WINDOW, 128)
    return [a.astype(np.float32) for a in (common, inverse_x, inverse_y)]


def rolled(value, shift, axis):
    return pltpu.roll(value, shift % value.shape[axis], axis)


def lanes_of(rows):
    return lax.broadcasted_iota(jnp.int32, (rows, 128), 1)


def z_sum_halves(low, high):
    lane = lanes_of(low.shape[0])
    up_low, up_high = rolled(low, -1, 1), rolled(high, -1, 1)
    down_low, down_high = rolled(low, 1, 1), rolled(high, 1, 1)
    last, first = lane == 127, lane == 0
    sum_low = jnp.where(last, up_high, up_low) + jnp.where(first, 0.0, down_low)
    sum_high = jnp.where(last, 0.0, up_high) + jnp.where(first, down_low, down_high)
    return sum_low, sum_high


def z_sum(value, period):
    lane = lanes_of(value.shape[0]) % period
    up = jnp.where(lane == period - 1, 0.0, rolled(value, -1, 1))
    return up + jnp.where(lane == 0, 0.0, rolled(value, 1, 1))


def fine_sum(ref, r, a, n):
    centre = [ref[r, h, pl.ds(a, n), :] for h in range(2)]
    along_z = z_sum_halves(*centre)
    summed = []
    for h in range(2):
        along_x = ref[r - 1, h, pl.ds(a, n), :] + ref[r + 1, h, pl.ds(a, n), :]
        along_y = ref[r, h, pl.ds(a - 1, n), :] + ref[r, h, pl.ds(a + 1, n), :]
        summed.append(along_x + along_y + along_z[h])
    return centre, summed


def middle_sum(ref, r, a, n):
    centre = ref[r, pl.ds(a, n), :]
    along_x = ref[r - 1, pl.ds(a, n), :] + ref[r + 1, pl.ds(a, n), :]
    along_y = ref[r, pl.ds(a - 1, n), :] + ref[r, pl.ds(a + 1, n), :]
    return centre, along_x + along_y + z_sum(centre, 128)


def pair_x_sum(before, here, after):
    return here + jnp.where(lanes_of(here.shape[0]) < 64, before, after)


def fold_lanes(low, high):
    rows = low.shape[0]
    lane = lanes_of(rows)
    index = (lane * 2) % 128
    low = jnp.take_along_axis(low + rolled(low, -1, 1), index, axis=1)
    high = jnp.take_along_axis(high + rolled(high, -1, 1), index, axis=1)
    return jnp.where(lane < 64, low, high)


def spread_lanes(value):
    lane = lanes_of(value.shape[0])
    index = lane // 2
    return jnp.take_along_axis(value, index, axis=1), jnp.take_along_axis(value, index + 64, axis=1)


def dot(a, b):
    return jnp.dot(a, b, precision=lax.Precision.HIGHEST, preferred_element_type=F32)


def cycle_kernel(
    W, N,
    f_hbm, s_hbm, common_hbm, invx_hbm, invy_hbm,
    out_v, res_v,
    f_in, s_in, common, invx, invy,
    va, wa, v2a, ua, ub, fold,
    vb, wb, v2b, tb, ub1, ub2, fb, db, foldb,
    gvw, gv2, t2, u2,
    modes,
    in_sem, send_sem, recv_sem, gather_send, gather_recv, wide_send, wide_recv,
):
    i = lax.axis_index("wide")
    n = lax.axis_index("narrow")

    loads = [
        pltpu.make_async_copy(src, dst, in_sem.at[k])
        for k, (src, dst) in enumerate(
            (
                (s_hbm, s_in),
                (f_hbm, f_in),
                (common_hbm, common),
                (invx_hbm.at[pl.ds(i, 5)], invx),
                (invy_hbm.at[n], invy),
            )
        )
    ]
    barrier = pltpu.get_barrier_semaphore()

    def greet(wide_id, narrow_id):
        pl.semaphore_signal(barrier, inc=1, device_id=(wide_id, narrow_id), device_id_type=MESH)

    has_low, has_high = i > 0, i < W - 1

    def there(dx, dy):
        terms = []
        if dx > 0:
            terms.append(i < W - dx)
        if dx < 0:
            terms.append(i >= -dx)
        if dy > 0:
            terms.append(n < N - dy)
        if dy < 0:
            terms.append(n >= -dy)
        return functools.reduce(jnp.logical_and, terms)

    sides = (-1, 1)
    corners = [(dx, dy) for dx in sides for dy in sides]
    for dx, dy in [(0, -1), (0, 1)] + corners + [(-1, 0), (1, 0)]:
        pl.when(there(dx, dy))(functools.partial(greet, i + dx, n + dy))

    for load in loads:
        load.start()

    def greet_narrow(k, _):
        other = lax.rem(n + k, N)

        @pl.when(jnp.logical_and(other != n - 1, other != n + 1))
        def _():
            greet_column(other)

        return 0

    def greet_column(other):
        greet(i, other)

        @pl.when(has_low)
        def _():
            greet(i - 1, other)

        @pl.when(has_high)
        def _():
            greet(i + 1, other)

    lax.fori_loop(1, N, greet_narrow, 0)

    def greet_wide(k, _):
        other = lax.rem(i + k, W)

        @pl.when(jnp.logical_and(other != i - 1, other != i + 1))
        def _():
            greet(other, n)

        return 0

    lax.fori_loop(1, W, greet_wide, 0)

    def zero(ref, *index):
        shape = ref.at[index].shape if index else ref.shape
        ref[index if index else ...] = jnp.zeros(shape, F32)

    all_ = slice(None)

    @pl.when(i == 0)
    def _():
        for ref in (va, wa):
            zero(ref, pl.ds(0, 4))
        for ref in (vb, wb, v2b):
            zero(ref, pl.ds(0, 4))
        zero(gvw, pl.ds(0, 2))
        zero(gv2, pl.ds(0, 2))

    @pl.when(i == W - 1)
    def _():
        for ref in (va, wa):
            zero(ref, pl.ds(12, 4))
        for ref in (vb, wb, v2b):
            zero(ref, pl.ds(8, 4))
        zero(gvw, pl.ds(3, 2))
        zero(gv2, pl.ds(3, 2))

    @pl.when(i == 1)
    def _():
        zero(gvw, 0)
        zero(gv2, 0)

    @pl.when(i == W - 2)
    def _():
        zero(gvw, 4)
        zero(gv2, 4)

    @pl.when(n == 0)
    def _():
        for ref in (va, wa):
            zero(ref, all_, all_, pl.ds(0, 8))
        for ref in (vb, wb, v2b):
            zero(ref, all_, pl.ds(0, 8))

    @pl.when(n == N - 1)
    def _():
        for ref in (va, wa):
            zero(ref, all_, all_, pl.ds(40, 8))
        for ref in (vb, wb, v2b):
            zero(ref, all_, pl.ds(24, 8))

    cols = 8 * N
    zero(gvw, pl.ds(1, 3), all_, pl.ds(0, 8))
    zero(gvw, pl.ds(1, 3), all_, pl.ds(8 + cols, 8))
    zero(gv2, 2, pl.ds(0, 8))
    zero(gv2, 2, pl.ds(8 + cols, 8))
    zero(t2, all_, pl.ds(0, 8))
    zero(t2, all_, pl.ds(8 + cols, 8))

    loads[0].wait()
    loads[1].wait()

    def start_fine(r, _):
        for h in range(2):
            screen = s_in[r, :, pl.ds(128 * h, 128)]
            weight = OMEGA / (6.0 + screen)
            wa[r + 4, h, pl.ds(8, 32), :] = weight
            va[r + 4, h, pl.ds(8, 32), :] = f_in[r, :, pl.ds(128 * h, 128)] * weight
        return 0

    lax.fori_loop(0, 8, start_fine, 0, unroll=True)

    counter = [0]

    def span(step, first, size, depths):
        if step == 0:
            return pl.ds(first, size), pl.ds(first, size)
        low, high = depths
        count = high - low + 1
        if step > 0:
            return pl.ds(first + size - high, count), pl.ds(first - high, count)
        return pl.ds(first + low - 1, count), pl.ds(first + size + low - 1, count)

    def exchange(src, dst, dx, dy):
        k = counter[0]
        counter[0] += 1
        copy = pltpu.make_async_remote_copy(
            src_ref=src, dst_ref=dst, send_sem=send_sem.at[k], recv_sem=recv_sem.at[k],
            device_id=(lax.rem(i + dx + W, W), lax.rem(n + dy + N, N)), device_id_type=MESH,
        )
        return copy, there(dx, dy), there(-dx, -dy)

    def fine_piece(ref, dx, dy, depth_x=None, depth_y=None):
        src_x, dst_x = span(dx, 4, 8, depth_x)
        src_y, dst_y = span(dy, 8, 32, depth_y)
        return exchange(ref.at[src_x, :, src_y, :], ref.at[dst_x, :, dst_y, :], dx, dy)

    def middle_piece(ref, dx, dy, depth_x=None, depth_y=None):
        src_x, dst_x = span(dx, 4, 4, depth_x)
        src_y, dst_y = span(dy, 8, 16, depth_y)
        return exchange(ref.at[src_x, src_y, :], ref.at[dst_x, dst_y, :], dx, dy)

    def start(pieces):
        for copy, to, _ in pieces:
            pl.when(to)(copy.start)

    def receive(pieces):
        for copy, _, come in pieces:
            pl.when(come)(copy.wait_recv)

    def sent(pieces):
        for copy, to, _ in pieces:
            pl.when(to)(copy.wait_send)

    fine_near = (
        [fine_piece(va, 0, d, None, (1, 2)) for d in sides]
        + [fine_piece(wa, 0, d, None, (1, 1)) for d in sides]
        + [fine_piece(va, dx, dy, (1, 1), (1, 1)) for dx, dy in corners]
        + [fine_piece(va, d, 0, (1, 2)) for d in sides]
        + [fine_piece(wa, d, 0, (1, 1)) for d in sides]
    )
    fine_far = (
        [fine_piece(va, 0, d, None, (3, 4)) for d in sides]
        + [fine_piece(wa, 0, d, None, (2, 3)) for d in sides]
        + [fine_piece(va, dx, dy, (1, 1), (2, 3)) for dx, dy in corners]
        + [fine_piece(va, dx, dy, (2, 3), (1, 2)) for dx, dy in corners]
        + [fine_piece(wa, dx, dy, (1, 2), (1, 2)) for dx, dy in corners]
        + [fine_piece(va, d, 0, (3, 4)) for d in sides]
        + [fine_piece(wa, d, 0, (2, 3)) for d in sides]
    )

    def middle_pieces(ref, depth, corner):
        return (
            [middle_piece(ref, 0, d, None, (1, depth)) for d in sides]
            + [middle_piece(ref, dx, dy, (1, corner), (1, corner)) for dx, dy in corners]
            + [middle_piece(ref, d, 0, (1, depth)) for d in sides]
        )

    middle_w = middle_pieces(wb, 3, 2)
    middle_v = middle_pieces(vb, 3, 2)
    middle_v2 = middle_pieces(v2b, 4, 3)

    window = pl.ds(pl.multiple_of(8 * n, 8), WINDOW)
    coarse_far = [exchange(gv2.at[2, window, :], gv2.at[2 - d, window, :], d, 0) for d in (-1, 1, -2, 2)]
    coarse_far += [exchange(gvw.at[2, :, window, :], gvw.at[2 - d, :, window, :], d, 0) for d in (-2, 2)]

    greeted = (W - 1) + (N - 1) * (1 + has_low.astype(jnp.int32) + has_high.astype(jnp.int32))
    pl.semaphore_wait(barrier, greeted)

    start(fine_near)
    start(fine_far)

    def screen_middle(q, _):
        for h in range(2):
            lanes = pl.ds(128 * h, 128)
            fold[q, h, :, :] = s_in[2 * q, :, lanes] + s_in[2 * q + 1, :, lanes]
        low, high = (
            fold[q, h, pl.ds(0, 16, stride=2), :] + fold[q, h, pl.ds(1, 16, stride=2), :] for h in range(2)
        )
        diagonal = 6.0 + 0.125 * fold_lanes(low, high)
        db[q, :, :] = diagonal
        wb[q + 4, pl.ds(8, 16), :] = OMEGA / diagonal
        return 0

    lax.fori_loop(0, 4, screen_middle, 0, unroll=True)
    start(middle_w)

    for h in range(2):
        foldb[h, :, :] = (db[2 * h, :, :] - 6.0) + (db[2 * h + 1, :, :] - 6.0)
    low, high = (foldb[h, pl.ds(0, 8, stride=2), :] + foldb[h, pl.ds(1, 8, stride=2), :] for h in range(2))
    coarse_d = 6.0 + 0.125 * fold_lanes(low, high)
    own_cols = pl.ds(pl.multiple_of(8 + 8 * n, 8), 8)
    gvw[2, 1, own_cols, :] = coarse_d

    def gather_copy(what, dx, k):
        other = lax.rem(n + k, N)
        target = lax.rem(i + dx + W, W)
        return pltpu.make_async_remote_copy(
            src_ref=gvw.at[2, what, own_cols, :], dst_ref=gvw.at[2 - dx, what, own_cols, :],
            send_sem=gather_send.at[what, dx + 1, k], recv_sem=gather_recv.at[what, 1 - dx, n],
            device_id=(target, other), device_id_type=MESH,
        )

    def arrived(what, slot, k):
        other = lax.rem(n + k, N)
        cells = pl.ds(pl.multiple_of(8 + 8 * other, 8), 8)
        return pltpu.make_async_remote_copy(
            src_ref=gvw.at[2, what, own_cols, :], dst_ref=gvw.at[1 + slot, what, cells, :],
            send_sem=gather_send.at[what, 0, 0], recv_sem=gather_recv.at[what, slot, other],
            device_id=(lax.rem(i + 1, W), n), device_id_type=MESH,
        )

    def for_each(k, call):
        pl.when(k > 0)(functools.partial(call, 0))
        pl.when(has_low)(functools.partial(call, -1))
        pl.when(has_high)(functools.partial(call, 1))

    def gather_start(what, k, _):
        for_each(k, lambda dx: gather_copy(what, dx, k).start())
        return 0

    def gather_receive(what, k, _):
        for_each(k, lambda dx: arrived(what, 1 + dx, k).wait_recv())
        return 0

    def gather_sent(what, k, _):
        for_each(k, lambda dx: gather_copy(what, dx, k).wait_send())
        return 0

    lax.fori_loop(0, N, functools.partial(gather_start, 1), 0)

    def fine_v2(a, count, r, _):
        centre, summed = fine_sum(va, r, a, count)
        for h in range(2):
            v2a[r, h, pl.ds(a, count), :] = (1.0 + KEEP) * centre[h] + wa[r, h, pl.ds(a, count), :] * summed[h]
        return 0

    receive(fine_near)
    fine_v2(8, 32, 3, 0)
    lax.fori_loop(4, 12, functools.partial(fine_v2, 7, 34), 0, unroll=True)
    fine_v2(8, 32, 12, 0)

    def fine_residual(ref, r, h, centre, summed):
        lanes = pl.ds(128 * h, 128)
        return f_in[r, :, lanes] - (6.0 + s_in[r, :, lanes]) * centre + summed

    def fine_down(q, _):
        c0, n0 = fine_sum(v2a, 2 * q + 4, 8, 32)
        c1, n1 = fine_sum(v2a, 2 * q + 5, 8, 32)
        for h in range(2):
            fold[q, h, :, :] = fine_residual(v2a, 2 * q, h, c0[h], n0[h]) + fine_residual(
                v2a, 2 * q + 1, h, c1[h], n1[h]
            )
        low, high = (
            fold[q, h, pl.ds(0, 16, stride=2), :] + fold[q, h, pl.ds(1, 16, stride=2), :] for h in range(2)
        )
        source = 0.5 * fold_lanes(low, high)
        fb[q, :, :] = source
        vb[q + 4, pl.ds(8, 16), :] = source * wb[q + 4, pl.ds(8, 16), :]
        return 0

    lax.fori_loop(0, 4, fine_down, 0, unroll=True)
    start(middle_v)

    receive(fine_far)
    lax.fori_loop(1, 15, functools.partial(fine_v2, 4, 40), 0, unroll=True)

    receive(middle_w)
    receive(middle_v)
    for r in range(3, 9):
        centre, summed = middle_sum(vb, r, 4, 24)
        tb[r, pl.ds(4, 24), :] = (1.0 + KEEP) * centre + wb[r, pl.ds(4, 24), :] * summed
    for r in range(4):
        centre, summed = middle_sum(tb, r + 4, 8, 16)
        v2b[r + 4, pl.ds(8, 16), :] = centre
        rest = fb[r, :, :] - db[r, :, :] * centre + summed
        if r % 2 == 0:
            held = rest
        else:
            foldb[r // 2, :, :] = held + rest
    low, high = (foldb[h, pl.ds(0, 8, stride=2), :] + foldb[h, pl.ds(1, 8, stride=2), :] for h in range(2))
    gvw[2, 0, own_cols, :] = 0.5 * fold_lanes(low, high) * (OMEGA / coarse_d)

    lax.fori_loop(0, N, functools.partial(gather_start, 0), 0)
    start(middle_v2)
    lax.fori_loop(0, N, functools.partial(gather_receive, 1), 0)
    lax.fori_loop(0, N, functools.partial(gather_receive, 0), 0)

    slab = pl.ds(8, cols)
    turned = [rolled(gvw[t, 0, slab, :], 64, 1) for t in (1, 2, 3)]
    for t in range(3):
        centre = gvw[t + 1, 0, slab, :]
        along_x = pair_x_sum(turned[max(t - 1, 0)], turned[t], turned[min(t + 1, 2)])
        along_y = gvw[t + 1, 0, pl.ds(7, cols), :] + gvw[t + 1, 0, pl.ds(9, cols), :]
        diagonal = gvw[t + 1, 1, slab, :]
        weight = jnp.where(diagonal > 0.0, OMEGA / diagonal, 0.0)
        t2[t, slab, :] = (1.0 + KEEP) * centre + weight * (along_x + along_y + z_sum(centre, 64))
    turned = [rolled(t2[t, slab, :], 64, 1) for t in range(3)]
    centre = t2[1, slab, :]
    gv2[2, slab, :] = centre
    diagonal = gvw[2, 1, slab, :]
    along_x = pair_x_sum(*turned)
    along_y = t2[1, pl.ds(7, cols), :] + t2[1, pl.ds(9, cols), :]
    rest = diagonal * (gvw[2, 0, slab, :] * (1.0 / OMEGA) - centre) + (along_x + along_y + z_sum(centre, 64))

    for load in loads[2:]:
        load.wait()
    along_z = dot(rest, common[pl.ds(0, 128), :])
    along_yz = dot(common[pl.ds(256, 4 * N), pl.ds(0, cols)], along_z)
    group = lanes_of(N) // 32
    mine = along_yz[0:N, :]
    for g in range(1, 4):
        mine = jnp.where(group == g, along_yz[g * N : (g + 1) * N, :], mine)
    modes[i, pl.ds(0, N), :] = mine
    modes[i, pl.ds(N, 1), :] = jnp.sum(diagonal - 6.0, axis=0, keepdims=True)

    def wide_copy(k):
        return pltpu.make_async_remote_copy(
            src_ref=modes.at[i], dst_ref=modes.at[i], send_sem=wide_send.at[k], recv_sem=wide_recv.at[i],
            device_id=(lax.rem(i + k, W), n), device_id_type=MESH,
        )

    def wide_start(k, _):
        wide_copy(k).start()
        return 0

    def wide_receive(k, _):
        other = lax.rem(i + k, W)
        pltpu.make_async_remote_copy(
            src_ref=modes.at[i], dst_ref=modes.at[other], send_sem=wide_send.at[0], recv_sem=wide_recv.at[other],
            device_id=(other, n), device_id_type=MESH,
        ).wait_recv()
        return 0

    def wide_sent(k, _):
        wide_copy(k).wait_send()
        return 0

    lax.fori_loop(1, W, wide_start, 0)
    start(coarse_far)
    for pieces in (fine_near, fine_far, middle_w, middle_v, middle_v2):
        sent(pieces)
    for what in range(2):
        lax.fori_loop(0, N, functools.partial(gather_sent, what), 0)
    receive(middle_v2)
    lax.fori_loop(1, W, wide_receive, 0)

    total = jnp.sum(modes[:, N, :], keepdims=True)
    mean = total * (1.0 / (2 * W * 8 * N * 64))
    shifted = common[pl.ds(256 + 4 * N, N), :] + mean
    sine_x, eigen_x = sine_table(W), sine_eigen(W)
    factor = (2.0 / (W + 1.0)) * (2.0 / (4 * N + 1.0)) * (2.0 / 33.0)
    half = W // 2
    even, odd = [], []
    for j in range(half):
        first, second = modes[j, pl.ds(0, N), :], modes[W - 1 - j, pl.ds(0, N), :]
        even.append(first + second)
        odd.append(first - second)
    found = [None] * 5
    for a in range(W):
        values = even if a % 2 == 0 else odd
        acc = None
        for j in range(half):
            term = values[j] * np.float32(sine_x[a, j])
            acc = term if acc is None else acc + term
        scaled = acc * np.float32(factor) / (shifted + np.float32(eigen_x[a]))
        for t in range(5):
            term = invx[t, pl.ds(a, 1), :] * scaled
            found[t] = term if found[t] is None else found[t] + term
    spread = dot(invy[:, pl.ds(0, N)], jnp.concatenate(found, axis=1))
    group = lanes_of(WINDOW) // 32
    parts = []
    for t in range(5):
        lanes = slice(128 * t, 128 * t + 128)
        part = spread[0:WINDOW, lanes]
        for g in range(1, 4):
            part = jnp.where(group == g, spread[g * WINDOW : (g + 1) * WINDOW, lanes], part)
        parts.append(part)
    correction = dot(jnp.concatenate(parts, axis=0), common[pl.ds(128, 128), :])

    receive(coarse_far)
    u = [gv2[t, window, :] + correction[WINDOW * t : WINDOW * (t + 1), :] for t in range(5)]

    def pair_sweep(u, slots):
        turned = {t: rolled(u[t], 64, 1) for t in u}
        swept = {}
        for t in slots:
            along_x = pair_x_sum(turned.get(t - 1, turned[t]), turned[t], turned.get(t + 1, turned[t]))
            along_y = rolled(u[t], 1, 0) + rolled(u[t], -1, 0)
            diagonal = gvw[t, 1, window, :]
            weight = jnp.where(diagonal > 0.0, OMEGA / diagonal, 0.0)
            summed = along_x + along_y + z_sum(u[t], 64)
            swept[t] = KEEP * u[t] + gvw[t, 0, window, :] + weight * summed
        return swept

    u = pair_sweep(dict(enumerate(u)), range(5))
    u = pair_sweep(u, range(1, 4))

    for t in (1, 2, 3):
        u2[t - 1, :, :] = u[t]
    for t in range(3):
        halves = spread_lanes(u2[t, pl.ds(4, 16), :])
        for h in range(2):
            for k in range(2):
                r = 4 * t + 2 * h + k
                ub1[r, pl.ds(0, 16, stride=2), :] = halves[h]
                ub1[r, pl.ds(1, 16, stride=2), :] = halves[h]
    for r in range(12):
        ub1[r, :, :] = ub1[r, :, :] + v2b[r, :, :]

    def middle_sweep(src, dst, r):
        centre, summed = middle_sum(src, r, 4, 24)
        part = (r, pl.ds(4, 24), slice(None))
        dst[part] = KEEP * centre + vb[part] + wb[part] * summed

    for r in range(1, 11):
        middle_sweep(ub1, ub2, r)
    for r in range(2, 10):
        middle_sweep(ub2, ub1, r)

    def fine_spread(q, _):
        halves = spread_lanes(ub1[q + 2, pl.ds(4, 24), :])
        for k in range(2):
            r = 2 * q + k
            for h in range(2):
                ua[r, h, pl.ds(0, 24, stride=2), :] = halves[h]
                ua[r, h, pl.ds(1, 24, stride=2), :] = halves[h]
        for k in range(2):
            r = 2 * q + k
            for h in range(2):
                ua[r, h, :, :] = ua[r, h, :, :] + v2a[r, h, :, :]
        return 0

    lax.fori_loop(0, 8, fine_spread, 0, unroll=True)

    def fine_sweep(src, dst, r, _):
        centre, summed = fine_sum(src, r, 4, 40)
        for h in range(2):
            part = (r, h, pl.ds(4, 40), slice(None))
            dst[part] = KEEP * centre[h] + va[part] + wa[part] * summed[h]
        return 0

    lax.fori_loop(2, 14, functools.partial(fine_sweep, ua, ub), 0, unroll=True)
    lax.fori_loop(3, 13, functools.partial(fine_sweep, ub, ua), 0, unroll=True)

    def fine_end(r, _):
        centre, summed = fine_sum(ua, r + 4, 8, 32)
        for h in range(2):
            lanes = pl.ds(128 * h, 128)
            out_v[r, :, lanes] = centre[h]
            res_v[r, :, lanes] = fine_residual(ua, r, h, centre[h], summed[h])
        return 0

    lax.fori_loop(0, 8, fine_end, 0, unroll=True)
    sent(coarse_far)
    lax.fori_loop(1, W, wide_sent, 0)


def solution(mesh):
    W, N = mesh.shape["wide"], mesh.shape["narrow"]
    common, invx, invy = tables(W, N)
    cols = 8 * N
    vmem = pltpu.VMEM
    dma = pltpu.SemaphoreType.DMA
    fine, middle = (16, 2, 48, 128), (12, 32, 128)
    scratch = [
        vmem((8, 32, 256), F32), vmem((8, 32, 256), F32),
        vmem(common.shape, F32), vmem((5, W, 128), F32), vmem((4 * WINDOW, 128), F32),
        vmem(fine, F32), vmem(fine, F32), vmem(fine, F32), vmem(fine, F32), vmem(fine, F32),
        vmem((4, 2, 32, 128), F32),
        vmem(middle, F32), vmem(middle, F32), vmem(middle, F32), vmem(middle, F32),
        vmem(middle, F32), vmem(middle, F32),
        vmem((4, 16, 128), F32), vmem((4, 16, 128), F32), vmem((2, 16, 128), F32),
        vmem((5, 2, cols + 16, 128), F32), vmem((5, cols + 16, 128), F32),
        vmem((3, cols + 16, 128), F32), vmem((3, WINDOW, 128), F32),
        vmem((W, N + 1, 128), F32),
        dma((5,)), dma((70,)), dma((70,)), dma((2, 3, N)), dma((2, 3, N)), dma((W,)), dma((W,)),
    ]

    def per_device(divergence, screening):
        block = pltpu.VMEM((8, 32, 256), F32)
        return pl.pallas_call(
            functools.partial(cycle_kernel, W, N),
            out_shape=(block, block),
            in_specs=[pl.BlockSpec(memory_space=pltpu.HBM)] * 5,
            out_specs=(pl.BlockSpec(memory_space=pltpu.VMEM),) * 2,
            scratch_shapes=scratch,
            compiler_params=pltpu.CompilerParams(
                collective_id=0, has_side_effects=True, vmem_limit_bytes=56 * 1024 * 1024
            ),
        )(divergence, screening, jnp.asarray(common), jnp.asarray(invx), jnp.asarray(invy))

    spec = P("wide", "narrow", None)
    return jax.shard_map(
        per_device, mesh=mesh, in_specs=(spec, spec), out_specs=(spec, spec), check_vma=False
    )
```

```python
import functools

import numpy as np
import jax
import jax.numpy as jnp
from jax import lax
from jax.experimental import pallas as pl
from jax.experimental.pallas import tpu as pltpu
from jax.sharding import PartitionSpec as P

MESH = pl.DeviceIdType.MESH
F32 = jnp.float32
OMEGA = 0.8
KEEP = 0.2
WINDOW = 24


def sine_table(count):
    ladder = np.arange(count, dtype=np.float64) + 1.0
    return np.sin(np.pi * ladder[:, None] * ladder[None, :] / (count + 1.0))


def sine_eigen(count):
    ladder = np.arange(count, dtype=np.float64) + 1.0
    return 2.0 - 2.0 * np.cos(np.pi * ladder / (count + 1.0))


def tables(wide, narrow):
    count_y, count_z = 4 * narrow, 32
    sine_x, sine_y, sine_z = sine_table(wide), sine_table(count_y), sine_table(count_z)
    to_modes = np.tile(np.repeat(sine_z.T, 2, axis=0), (2, 4))
    from_modes = np.tile(np.repeat(sine_z, 2, axis=1), (4, 2))
    rows_y = 0.5 * np.repeat(sine_y, 2, axis=1)
    rows_y = np.pad(rows_y, ((0, 0), (0, 128 - rows_y.shape[1])))
    eigen_y = sine_eigen(count_y).reshape(4, narrow)
    eigen = eigen_y.T[:, :, None] + sine_eigen(count_z)[None, None, :]
    eigen = eigen.reshape(narrow, 128)
    common = np.concatenate([to_modes, from_modes, rows_y, eigen], axis=0)
    inverse_x = np.pad(sine_x, ((2, 2), (0, 0)))
    inverse_x = np.repeat(inverse_x[:, :, None], 128, axis=2)
    fine_y = np.pad(np.repeat(sine_y, 2, axis=0), ((8, 8), (0, 0)))
    inverse_y = np.zeros((narrow, 4, WINDOW, 128))
    for n in range(narrow):
        for g in range(4):
            inverse_y[n, g, :, :narrow] = fine_y[8 * n : 8 * n + WINDOW, g * narrow : (g + 1) * narrow]
    inverse_y = inverse_y.reshape(narrow, 4 * WINDOW, 128)
    return [a.astype(np.float32) for a in (common, inverse_x, inverse_y)]


def rolled(value, shift, axis):
    return pltpu.roll(value, shift % value.shape[axis], axis)


def lanes_of(rows):
    return lax.broadcasted_iota(jnp.int32, (rows, 128), 1)


def z_sum_halves(low, high):
    lane = lanes_of(low.shape[0])
    up_low, up_high = rolled(low, -1, 1), rolled(high, -1, 1)
    down_low, down_high = rolled(low, 1, 1), rolled(high, 1, 1)
    last, first = lane == 127, lane == 0
    sum_low = jnp.where(last, up_high, up_low) + jnp.where(first, 0.0, down_low)
    sum_high = jnp.where(last, 0.0, up_high) + jnp.where(first, down_low, down_high)
    return sum_low, sum_high


def z_sum(value, period):
    lane = lanes_of(value.shape[0]) % period
    up = jnp.where(lane == period - 1, 0.0, rolled(value, -1, 1))
    return up + jnp.where(lane == 0, 0.0, rolled(value, 1, 1))


def fine_sum(ref, r, a, n):
    centre = [ref[r, h, pl.ds(a, n), :] for h in range(2)]
    along_z = z_sum_halves(*centre)
    summed = []
    for h in range(2):
        along_x = ref[r - 1, h, pl.ds(a, n), :] + ref[r + 1, h, pl.ds(a, n), :]
        along_y = ref[r, h, pl.ds(a - 1, n), :] + ref[r, h, pl.ds(a + 1, n), :]
        summed.append(along_x + along_y + along_z[h])
    return centre, summed


def middle_sum(ref, r, a, n):
    centre = ref[r, pl.ds(a, n), :]
    along_x = ref[r - 1, pl.ds(a, n), :] + ref[r + 1, pl.ds(a, n), :]
    along_y = ref[r, pl.ds(a - 1, n), :] + ref[r, pl.ds(a + 1, n), :]
    return centre, along_x + along_y + z_sum(centre, 128)


def pair_x_sum(before, here, after):
    return here + jnp.where(lanes_of(here.shape[0]) < 64, before, after)


def fold_lanes(low, high):
    rows = low.shape[0]
    lane = lanes_of(rows)
    index = (lane * 2) % 128
    low = jnp.take_along_axis(low + rolled(low, -1, 1), index, axis=1)
    high = jnp.take_along_axis(high + rolled(high, -1, 1), index, axis=1)
    return jnp.where(lane < 64, low, high)


def spread_lanes(value):
    lane = lanes_of(value.shape[0])
    index = lane // 2
    return jnp.take_along_axis(value, index, axis=1), jnp.take_along_axis(value, index + 64, axis=1)


def dot(a, b):
    return jnp.dot(a, b, precision=lax.Precision.HIGHEST, preferred_element_type=F32)


def cycle_kernel(
    W, N,
    f_hbm, s_hbm, common_hbm, invx_hbm, invy_hbm,
    out_v, res_v,
    f_in, s_in, common, invx, invy,
    va, wa, v2a, ua, ub, fold,
    vb, wb, v2b, tb, ub1, ub2, fb, db, foldb,
    gvw, gv2, t2, u2,
    modes, tally,
    in_sem, send_sem, recv_sem, far_send, far_recv, gather_send, gather_recv, wide_send, wide_recv,
):
    i = lax.axis_index("wide")
    n = lax.axis_index("narrow")

    loads = [
        pltpu.make_async_copy(src, dst, in_sem.at[min(k, 2)])
        for k, (src, dst) in enumerate(
            (
                (s_hbm, s_in),
                (f_hbm, f_in),
                (common_hbm, common),
                (invx_hbm.at[pl.ds(i, 5)], invx),
                (invy_hbm.at[n], invy),
            )
        )
    ]
    barrier = pltpu.get_barrier_semaphore()

    def greet(wide_id, narrow_id):
        pl.semaphore_signal(barrier, inc=1, device_id=(wide_id, narrow_id), device_id_type=MESH)

    has_low, has_high = i > 0, i < W - 1

    def there(dx, dy):
        terms = []
        if dx > 0:
            terms.append(i < W - dx)
        if dx < 0:
            terms.append(i >= -dx)
        if dy > 0:
            terms.append(n < N - dy)
        if dy < 0:
            terms.append(n >= -dy)
        return functools.reduce(jnp.logical_and, terms)

    sides = (-1, 1)
    corners = [(dx, dy) for dx in sides for dy in sides]
    for dx, dy in [(0, -1), (0, 1)] + corners + [(-1, 0), (1, 0)]:
        pl.when(there(dx, dy))(functools.partial(greet, i + dx, n + dy))

    for load in loads:
        load.start()

    def greet_narrow(k, _):
        other = lax.rem(n + k, N)

        @pl.when(jnp.logical_and(other != n - 1, other != n + 1))
        def _():
            greet_column(other)

        return 0

    def greet_column(other):
        greet(i, other)

        @pl.when(has_low)
        def _():
            greet(i - 1, other)

        @pl.when(has_high)
        def _():
            greet(i + 1, other)

    lax.fori_loop(1, N, greet_narrow, 0)

    def greet_wide(k, _):
        other = lax.rem(i + k, W)

        @pl.when(jnp.logical_and(other != i - 1, other != i + 1))
        def _():
            greet(other, n)

        return 0

    lax.fori_loop(1, W, greet_wide, 0)

    def zero(ref, *index):
        shape = ref.at[index].shape if index else ref.shape
        ref[index if index else ...] = jnp.zeros(shape, F32)

    all_ = slice(None)

    @pl.when(i == 0)
    def _():
        for ref in (va, wa):
            zero(ref, pl.ds(0, 4))
        for ref in (vb, wb, v2b):
            zero(ref, pl.ds(0, 4))
        zero(gvw, pl.ds(0, 2))
        zero(gv2, pl.ds(0, 2))

    @pl.when(i == W - 1)
    def _():
        for ref in (va, wa):
            zero(ref, pl.ds(12, 4))
        for ref in (vb, wb, v2b):
            zero(ref, pl.ds(8, 4))
        zero(gvw, pl.ds(3, 2))
        zero(gv2, pl.ds(3, 2))

    @pl.when(i == 1)
    def _():
        zero(gvw, 0)
        zero(gv2, 0)

    @pl.when(i == W - 2)
    def _():
        zero(gvw, 4)
        zero(gv2, 4)

    @pl.when(n == 0)
    def _():
        for ref in (va, wa):
            zero(ref, all_, all_, pl.ds(0, 8))
        for ref in (vb, wb, v2b):
            zero(ref, all_, pl.ds(0, 8))

    @pl.when(n == N - 1)
    def _():
        for ref in (va, wa):
            zero(ref, all_, all_, pl.ds(40, 8))
        for ref in (vb, wb, v2b):
            zero(ref, all_, pl.ds(24, 8))

    cols = 8 * N
    zero(gvw, pl.ds(1, 3), all_, pl.ds(0, 8))
    zero(gvw, pl.ds(1, 3), all_, pl.ds(8 + cols, 8))
    zero(gv2, 2, pl.ds(0, 8))
    zero(gv2, 2, pl.ds(8 + cols, 8))
    zero(t2, all_, pl.ds(0, 8))
    zero(t2, all_, pl.ds(8 + cols, 8))

    loads[0].wait()
    loads[1].wait()

    def start_fine(r, _):
        for h in range(2):
            screen = s_in[r, :, pl.ds(128 * h, 128)]
            weight = OMEGA / (6.0 + screen)
            wa[r + 4, h, pl.ds(8, 32), :] = weight
            va[r + 4, h, pl.ds(8, 32), :] = f_in[r, :, pl.ds(128 * h, 128)] * weight
        return 0

    lax.fori_loop(0, 8, start_fine, 0, unroll=True)

    directions = [(0, -1), (0, 1)] + corners + [(-1, 0), (1, 0)]
    rows_of = {}

    def waiter(rows, send, recv, to):
        part = tally.at[pl.ds(0, rows), :]
        return pltpu.make_async_remote_copy(
            src_ref=part, dst_ref=part, send_sem=send, recv_sem=recv, device_id=to, device_id_type=MESH
        )

    def beside(dx, dy):
        return lax.rem(i + dx + W, W), lax.rem(n + dy + N, N)

    def span(step, first, size, depths):
        if step == 0:
            return pl.ds(first, size), pl.ds(first, size)
        low, high = depths
        count = high - low + 1
        if step > 0:
            return pl.ds(first + size - high, count), pl.ds(first - high, count)
        return pl.ds(first + low - 1, count), pl.ds(first + size + low - 1, count)

    def exchange(family, src, dst, dx, dy):
        d = directions.index((dx, dy))
        rows_of[family, d] = rows_of.get((family, d), 0) + int(np.prod(src.shape)) // 128
        copy = pltpu.make_async_remote_copy(
            src_ref=src, dst_ref=dst, send_sem=send_sem.at[d], recv_sem=recv_sem.at[family, d],
            device_id=beside(dx, dy), device_id_type=MESH,
        )
        return copy, there(dx, dy)

    def fine_piece(family, ref, dx, dy, depth_x=None, depth_y=None):
        src_x, dst_x = span(dx, 4, 8, depth_x)
        src_y, dst_y = span(dy, 8, 32, depth_y)
        return exchange(family, ref.at[src_x, :, src_y, :], ref.at[dst_x, :, dst_y, :], dx, dy)

    def middle_piece(family, ref, dx, dy, depth_x=None, depth_y=None):
        src_x, dst_x = span(dx, 4, 4, depth_x)
        src_y, dst_y = span(dy, 8, 16, depth_y)
        return exchange(family, ref.at[src_x, src_y, :], ref.at[dst_x, dst_y, :], dx, dy)

    def start(pieces):
        for copy, to in pieces:
            pl.when(to)(copy.start)

    def receive(family):
        for d, (dx, dy) in enumerate(directions):
            arrival = waiter(rows_of[family, d], send_sem.at[d], recv_sem.at[family, d], beside(dx, dy))
            pl.when(there(-dx, -dy))(arrival.wait_recv)

    def halo_sent():
        for d, (dx, dy) in enumerate(directions):
            rows = sum(rows_of[family, d] for family in range(4))
            pl.when(there(dx, dy))(waiter(rows, send_sem.at[d], recv_sem.at[0, d], beside(dx, dy)).wait_send)

    fine_near = (
        [fine_piece(0, va, 0, d, None, (1, 2)) for d in sides]
        + [fine_piece(0, wa, 0, d, None, (1, 1)) for d in sides]
        + [fine_piece(0, va, dx, dy, (1, 1), (1, 1)) for dx, dy in corners]
        + [fine_piece(0, va, d, 0, (1, 2)) for d in sides]
        + [fine_piece(0, wa, d, 0, (1, 1)) for d in sides]
    )
    fine_far = (
        [fine_piece(1, va, 0, d, None, (3, 4)) for d in sides]
        + [fine_piece(1, wa, 0, d, None, (2, 3)) for d in sides]
        + [fine_piece(1, va, dx, dy, (1, 1), (2, 3)) for dx, dy in corners]
        + [fine_piece(1, va, dx, dy, (2, 3), (1, 2)) for dx, dy in corners]
        + [fine_piece(1, wa, dx, dy, (1, 2), (1, 2)) for dx, dy in corners]
        + [fine_piece(1, va, d, 0, (3, 4)) for d in sides]
        + [fine_piece(1, wa, d, 0, (2, 3)) for d in sides]
    )

    def middle_pieces(family, ref, depth, corner):
        return (
            [middle_piece(family, ref, 0, d, None, (1, depth)) for d in sides]
            + [middle_piece(family, ref, dx, dy, (1, corner), (1, corner)) for dx, dy in corners]
            + [middle_piece(family, ref, d, 0, (1, depth)) for d in sides]
        )

    middle_w = middle_pieces(2, wb, 3, 2)
    middle_v = middle_pieces(2, vb, 3, 2)
    middle_v2 = middle_pieces(3, v2b, 4, 3)

    window = pl.ds(pl.multiple_of(8 * n, 8), WINDOW)
    reach = (-2, -1, 1, 2)

    def coarse_far(d):
        k = reach.index(d)
        args = dict(
            send_sem=far_send.at[k], recv_sem=far_recv.at[k], device_id=beside(d, 0), device_id_type=MESH
        )
        copies = [pltpu.make_async_remote_copy(src_ref=gv2.at[2, window, :], dst_ref=gv2.at[2 - d, window, :], **args)]
        if abs(d) == 2:
            copies.append(
                pltpu.make_async_remote_copy(
                    src_ref=gvw.at[2, :, window, :], dst_ref=gvw.at[2 - d, :, window, :], **args
                )
            )
        return copies

    def coarse_far_start():
        for d in reach:
            for copy in coarse_far(d):
                pl.when(there(d, 0))(copy.start)

    def coarse_far_waiter(d):
        k = reach.index(d)
        return waiter((3 if abs(d) == 2 else 1) * WINDOW, far_send.at[k], far_recv.at[k], beside(d, 0))

    greeted = (W - 1) + (N - 1) * (1 + has_low.astype(jnp.int32) + has_high.astype(jnp.int32))
    pl.semaphore_wait(barrier, greeted)

    start(fine_near)
    start(fine_far)

    def screen_middle(q, _):
        for h in range(2):
            lanes = pl.ds(128 * h, 128)
            fold[q, h, :, :] = s_in[2 * q, :, lanes] + s_in[2 * q + 1, :, lanes]
        low, high = (
            fold[q, h, pl.ds(0, 16, stride=2), :] + fold[q, h, pl.ds(1, 16, stride=2), :] for h in range(2)
        )
        diagonal = 6.0 + 0.125 * fold_lanes(low, high)
        db[q, :, :] = diagonal
        wb[q + 4, pl.ds(8, 16), :] = OMEGA / diagonal
        return 0

    lax.fori_loop(0, 4, screen_middle, 0, unroll=True)
    start(middle_w)

    for h in range(2):
        foldb[h, :, :] = (db[2 * h, :, :] - 6.0) + (db[2 * h + 1, :, :] - 6.0)
    low, high = (foldb[h, pl.ds(0, 8, stride=2), :] + foldb[h, pl.ds(1, 8, stride=2), :] for h in range(2))
    coarse_d = 6.0 + 0.125 * fold_lanes(low, high)
    own_cols = pl.ds(pl.multiple_of(8 + 8 * n, 8), 8)
    gvw[2, 1, own_cols, :] = coarse_d

    def gather_copy(what, dx, k):
        other = lax.rem(n + k, N)
        target = lax.rem(i + dx + W, W)
        return pltpu.make_async_remote_copy(
            src_ref=gvw.at[2, what, own_cols, :], dst_ref=gvw.at[2 - dx, what, own_cols, :],
            send_sem=gather_send.at[what, dx + 1], recv_sem=gather_recv.at[what, 1 - dx],
            device_id=(target, other), device_id_type=MESH,
        )

    def gather_waiter(what, dx):
        rows = 8 * (N if dx else N - 1)
        target = (lax.rem(i + 1, W), n)
        return waiter(rows, gather_send.at[what, dx + 1], gather_recv.at[what, dx + 1], target)

    def for_each(k, call):
        pl.when(k > 0)(functools.partial(call, 0))
        pl.when(has_low)(functools.partial(call, -1))
        pl.when(has_high)(functools.partial(call, 1))

    def gather_start(what, k, _):
        for_each(k, lambda dx: gather_copy(what, dx, k).start())
        return 0

    def gather_receive(what):
        for_each(1, lambda dx: gather_waiter(what, dx).wait_recv())

    def gather_sent(what):
        for_each(1, lambda dx: gather_waiter(what, dx).wait_send())

    lax.fori_loop(0, N, functools.partial(gather_start, 1), 0)

    def fine_v2(a, count, r, _):
        centre, summed = fine_sum(va, r, a, count)
        for h in range(2):
            v2a[r, h, pl.ds(a, count), :] = (1.0 + KEEP) * centre[h] + wa[r, h, pl.ds(a, count), :] * summed[h]
        return 0

    receive(0)
    fine_v2(8, 32, 3, 0)
    lax.fori_loop(4, 12, functools.partial(fine_v2, 7, 34), 0, unroll=True)
    fine_v2(8, 32, 12, 0)

    def fine_residual(ref, r, h, centre, summed):
        lanes = pl.ds(128 * h, 128)
        return f_in[r, :, lanes] - (6.0 + s_in[r, :, lanes]) * centre + summed

    def fine_down(q, _):
        c0, n0 = fine_sum(v2a, 2 * q + 4, 8, 32)
        c1, n1 = fine_sum(v2a, 2 * q + 5, 8, 32)
        for h in range(2):
            fold[q, h, :, :] = fine_residual(v2a, 2 * q, h, c0[h], n0[h]) + fine_residual(
                v2a, 2 * q + 1, h, c1[h], n1[h]
            )
        low, high = (
            fold[q, h, pl.ds(0, 16, stride=2), :] + fold[q, h, pl.ds(1, 16, stride=2), :] for h in range(2)
        )
        source = 0.5 * fold_lanes(low, high)
        fb[q, :, :] = source
        vb[q + 4, pl.ds(8, 16), :] = source * wb[q + 4, pl.ds(8, 16), :]
        return 0

    lax.fori_loop(0, 4, fine_down, 0, unroll=True)
    start(middle_v)

    receive(1)
    lax.fori_loop(1, 15, functools.partial(fine_v2, 4, 40), 0, unroll=True)

    receive(2)
    for r in range(3, 9):
        centre, summed = middle_sum(vb, r, 4, 24)
        tb[r, pl.ds(4, 24), :] = (1.0 + KEEP) * centre + wb[r, pl.ds(4, 24), :] * summed
    for r in range(4):
        centre, summed = middle_sum(tb, r + 4, 8, 16)
        v2b[r + 4, pl.ds(8, 16), :] = centre
        rest = fb[r, :, :] - db[r, :, :] * centre + summed
        if r % 2 == 0:
            held = rest
        else:
            foldb[r // 2, :, :] = held + rest
    low, high = (foldb[h, pl.ds(0, 8, stride=2), :] + foldb[h, pl.ds(1, 8, stride=2), :] for h in range(2))
    gvw[2, 0, own_cols, :] = 0.5 * fold_lanes(low, high) * (OMEGA / coarse_d)

    lax.fori_loop(0, N, functools.partial(gather_start, 0), 0)
    start(middle_v2)
    gather_receive(1)
    gather_receive(0)

    slab = pl.ds(8, cols)
    turned = [rolled(gvw[t, 0, slab, :], 64, 1) for t in (1, 2, 3)]
    for t in range(3):
        centre = gvw[t + 1, 0, slab, :]
        along_x = pair_x_sum(turned[max(t - 1, 0)], turned[t], turned[min(t + 1, 2)])
        along_y = gvw[t + 1, 0, pl.ds(7, cols), :] + gvw[t + 1, 0, pl.ds(9, cols), :]
        diagonal = gvw[t + 1, 1, slab, :]
        weight = jnp.where(diagonal > 0.0, OMEGA / diagonal, 0.0)
        t2[t, slab, :] = (1.0 + KEEP) * centre + weight * (along_x + along_y + z_sum(centre, 64))
    turned = [rolled(t2[t, slab, :], 64, 1) for t in range(3)]
    centre = t2[1, slab, :]
    gv2[2, slab, :] = centre
    diagonal = gvw[2, 1, slab, :]
    along_x = pair_x_sum(*turned)
    along_y = t2[1, pl.ds(7, cols), :] + t2[1, pl.ds(9, cols), :]
    rest = diagonal * (gvw[2, 0, slab, :] * (1.0 / OMEGA) - centre) + (along_x + along_y + z_sum(centre, 64))

    sizes = (common, invx, invy)
    part = tally.at[pl.ds(0, sum(int(np.prod(ref.shape)) // 128 for ref in sizes)), :]
    pltpu.make_async_copy(part, part, in_sem.at[2]).wait()
    along_z = dot(rest, common[pl.ds(0, 128), :])
    along_yz = dot(common[pl.ds(256, 4 * N), pl.ds(0, cols)], along_z)
    group = lanes_of(N) // 32
    mine = along_yz[0:N, :]
    for g in range(1, 4):
        mine = jnp.where(group == g, along_yz[g * N : (g + 1) * N, :], mine)
    modes[i, pl.ds(0, N), :] = mine
    modes[i, pl.ds(N, 1), :] = jnp.sum(diagonal - 6.0, axis=0, keepdims=True)

    def wide_copy(k):
        return pltpu.make_async_remote_copy(
            src_ref=modes.at[i], dst_ref=modes.at[i], send_sem=wide_send.at[0], recv_sem=wide_recv.at[0],
            device_id=(lax.rem(i + k, W), n), device_id_type=MESH,
        )

    def wide_start(k, _):
        wide_copy(k).start()
        return 0

    everyone = waiter((W - 1) * (N + 1), wide_send.at[0], wide_recv.at[0], (lax.rem(i + 1, W), n))

    lax.fori_loop(1, W, wide_start, 0)
    coarse_far_start()
    halo_sent()
    for what in range(2):
        gather_sent(what)
    receive(3)
    everyone.wait_recv()

    total = jnp.sum(modes[:, N, :], keepdims=True)
    mean = total * (1.0 / (2 * W * 8 * N * 64))
    shifted = common[pl.ds(256 + 4 * N, N), :] + mean
    sine_x, eigen_x = sine_table(W), sine_eigen(W)
    factor = (2.0 / (W + 1.0)) * (2.0 / (4 * N + 1.0)) * (2.0 / 33.0)
    half = W // 2
    even, odd = [], []
    for j in range(half):
        first, second = modes[j, pl.ds(0, N), :], modes[W - 1 - j, pl.ds(0, N), :]
        even.append(first + second)
        odd.append(first - second)
    found = [None] * 5
    for a in range(W):
        values = even if a % 2 == 0 else odd
        acc = None
        for j in range(half):
            term = values[j] * np.float32(sine_x[a, j])
            acc = term if acc is None else acc + term
        scaled = acc * np.float32(factor) / (shifted + np.float32(eigen_x[a]))
        for t in range(5):
            term = invx[t, pl.ds(a, 1), :] * scaled
            found[t] = term if found[t] is None else found[t] + term
    spread = dot(invy[:, pl.ds(0, N)], jnp.concatenate(found, axis=1))
    group = lanes_of(WINDOW) // 32
    parts = []
    for t in range(5):
        lanes = slice(128 * t, 128 * t + 128)
        part = spread[0:WINDOW, lanes]
        for g in range(1, 4):
            part = jnp.where(group == g, spread[g * WINDOW : (g + 1) * WINDOW, lanes], part)
        parts.append(part)
    correction = dot(jnp.concatenate(parts, axis=0), common[pl.ds(128, 128), :])

    for d in reach:
        pl.when(there(-d, 0))(coarse_far_waiter(d).wait_recv)
    u = [gv2[t, window, :] + correction[WINDOW * t : WINDOW * (t + 1), :] for t in range(5)]

    def pair_sweep(u, slots):
        turned = {t: rolled(u[t], 64, 1) for t in u}
        swept = {}
        for t in slots:
            along_x = pair_x_sum(turned.get(t - 1, turned[t]), turned[t], turned.get(t + 1, turned[t]))
            along_y = rolled(u[t], 1, 0) + rolled(u[t], -1, 0)
            diagonal = gvw[t, 1, window, :]
            weight = jnp.where(diagonal > 0.0, OMEGA / diagonal, 0.0)
            summed = along_x + along_y + z_sum(u[t], 64)
            swept[t] = KEEP * u[t] + gvw[t, 0, window, :] + weight * summed
        return swept

    u = pair_sweep(dict(enumerate(u)), range(5))
    u = pair_sweep(u, range(1, 4))

    for t in (1, 2, 3):
        u2[t - 1, :, :] = u[t]
    for t in range(3):
        halves = spread_lanes(u2[t, pl.ds(4, 16), :])
        for h in range(2):
            for k in range(2):
                r = 4 * t + 2 * h + k
                ub1[r, pl.ds(0, 16, stride=2), :] = halves[h]
                ub1[r, pl.ds(1, 16, stride=2), :] = halves[h]
    for r in range(12):
        ub1[r, :, :] = ub1[r, :, :] + v2b[r, :, :]

    def middle_sweep(src, dst, r):
        centre, summed = middle_sum(src, r, 4, 24)
        part = (r, pl.ds(4, 24), slice(None))
        dst[part] = KEEP * centre + vb[part] + wb[part] * summed

    for r in range(1, 11):
        middle_sweep(ub1, ub2, r)
    for r in range(2, 10):
        middle_sweep(ub2, ub1, r)

    def fine_spread(q, _):
        halves = spread_lanes(ub1[q + 2, pl.ds(4, 24), :])
        for k in range(2):
            r = 2 * q + k
            for h in range(2):
                ua[r, h, pl.ds(0, 24, stride=2), :] = halves[h]
                ua[r, h, pl.ds(1, 24, stride=2), :] = halves[h]
        for k in range(2):
            r = 2 * q + k
            for h in range(2):
                ua[r, h, :, :] = ua[r, h, :, :] + v2a[r, h, :, :]
        return 0

    lax.fori_loop(0, 8, fine_spread, 0, unroll=True)

    def fine_sweep(src, dst, r, _):
        centre, summed = fine_sum(src, r, 4, 40)
        for h in range(2):
            part = (r, h, pl.ds(4, 40), slice(None))
            dst[part] = KEEP * centre[h] + va[part] + wa[part] * summed[h]
        return 0

    lax.fori_loop(2, 14, functools.partial(fine_sweep, ua, ub), 0, unroll=True)
    lax.fori_loop(3, 13, functools.partial(fine_sweep, ub, ua), 0, unroll=True)

    def fine_end(r, _):
        centre, summed = fine_sum(ua, r + 4, 8, 32)
        for h in range(2):
            lanes = pl.ds(128 * h, 128)
            out_v[r, :, lanes] = centre[h]
            res_v[r, :, lanes] = fine_residual(ua, r, h, centre[h], summed[h])
        return 0

    lax.fori_loop(0, 8, fine_end, 0, unroll=True)
    for d in reach:
        pl.when(there(d, 0))(coarse_far_waiter(d).wait_send)
    everyone.wait_send()


def solution(mesh):
    W, N = mesh.shape["wide"], mesh.shape["narrow"]
    common, invx, invy = tables(W, N)
    cols = 8 * N
    vmem = pltpu.VMEM
    dma = pltpu.SemaphoreType.DMA
    fine, middle = (16, 2, 48, 128), (12, 32, 128)
    scratch = [
        vmem((8, 32, 256), F32), vmem((8, 32, 256), F32),
        vmem(common.shape, F32), vmem((5, W, 128), F32), vmem((4 * WINDOW, 128), F32),
        vmem(fine, F32), vmem(fine, F32), vmem(fine, F32), vmem(fine, F32), vmem(fine, F32),
        vmem((4, 2, 32, 128), F32),
        vmem(middle, F32), vmem(middle, F32), vmem(middle, F32), vmem(middle, F32),
        vmem(middle, F32), vmem(middle, F32),
        vmem((4, 16, 128), F32), vmem((4, 16, 128), F32), vmem((2, 16, 128), F32),
        vmem((5, 2, cols + 16, 128), F32), vmem((5, cols + 16, 128), F32),
        vmem((3, cols + 16, 128), F32), vmem((3, WINDOW, 128), F32),
        vmem((W, N + 1, 128), F32), vmem((640, 128), F32),
        dma((3,)), dma((8,)), dma((4, 8)), dma((4,)), dma((4,)), dma((2, 3)), dma((2, 3)), dma((1,)), dma((1,)),
    ]

    def per_device(divergence, screening):
        block = pltpu.VMEM((8, 32, 256), F32)
        return pl.pallas_call(
            functools.partial(cycle_kernel, W, N),
            out_shape=(block, block),
            in_specs=[pl.BlockSpec(memory_space=pltpu.HBM)] * 5,
            out_specs=(pl.BlockSpec(memory_space=pltpu.VMEM),) * 2,
            scratch_shapes=scratch,
            compiler_params=pltpu.CompilerParams(
                collective_id=0, has_side_effects=True, vmem_limit_bytes=56 * 1024 * 1024
            ),
        )(divergence, screening, jnp.asarray(common), jnp.asarray(invx), jnp.asarray(invy))

    spec = P("wide", "narrow", None)
    return jax.shard_map(
        per_device, mesh=mesh, in_specs=(spec, spec), out_specs=(spec, spec), check_vma=False
    )
```

```python
import functools

import numpy as np
import jax
import jax.numpy as jnp
from jax import lax
from jax.experimental import pallas as pl
from jax.experimental.pallas import tpu as pltpu
from jax.sharding import PartitionSpec as P

MESH = pl.DeviceIdType.MESH
F32 = jnp.float32
OMEGA = 0.8
KEEP = 0.2
WINDOW = 24


def sine_table(count):
    ladder = np.arange(count, dtype=np.float64) + 1.0
    return np.sin(np.pi * ladder[:, None] * ladder[None, :] / (count + 1.0))


def sine_eigen(count):
    ladder = np.arange(count, dtype=np.float64) + 1.0
    return 2.0 - 2.0 * np.cos(np.pi * ladder / (count + 1.0))


def tables(wide, narrow):
    count_y, count_z = 4 * narrow, 32
    sine_x, sine_y, sine_z = sine_table(wide), sine_table(count_y), sine_table(count_z)
    to_modes = np.tile(np.repeat(sine_z.T, 2, axis=0), (2, 4))
    from_modes = np.tile(np.repeat(sine_z, 2, axis=1), (4, 2))
    rows_y = 0.5 * np.repeat(sine_y, 2, axis=1)
    rows_y = np.pad(rows_y, ((0, 0), (0, 128 - rows_y.shape[1])))
    eigen_y = sine_eigen(count_y).reshape(4, narrow)
    eigen = eigen_y.T[:, :, None] + sine_eigen(count_z)[None, None, :]
    eigen = eigen.reshape(narrow, 128)
    common = np.concatenate([to_modes, from_modes, rows_y, eigen], axis=0)
    inverse_x = np.pad(sine_x, ((2, 2), (0, 0)))
    inverse_x = np.repeat(inverse_x[:, :, None], 128, axis=2)
    fine_y = np.pad(np.repeat(sine_y, 2, axis=0), ((8, 8), (0, 0)))
    inverse_y = np.zeros((narrow, 4, WINDOW, 128))
    for n in range(narrow):
        for g in range(4):
            inverse_y[n, g, :, :narrow] = fine_y[8 * n : 8 * n + WINDOW, g * narrow : (g + 1) * narrow]
    inverse_y = inverse_y.reshape(narrow, 4 * WINDOW, 128)
    return [a.astype(np.float32) for a in (common, inverse_x, inverse_y)]


def rolled(value, shift, axis):
    return pltpu.roll(value, shift % value.shape[axis], axis)


def lanes_of(rows):
    return lax.broadcasted_iota(jnp.int32, (rows, 128), 1)


def z_sum_halves(low, high):
    lane = lanes_of(low.shape[0])
    up_low, up_high = rolled(low, -1, 1), rolled(high, -1, 1)
    down_low, down_high = rolled(low, 1, 1), rolled(high, 1, 1)
    last, first = lane == 127, lane == 0
    sum_low = jnp.where(last, up_high, up_low) + jnp.where(first, 0.0, down_low)
    sum_high = jnp.where(last, 0.0, up_high) + jnp.where(first, down_low, down_high)
    return sum_low, sum_high


def z_sum(value, period):
    lane = lanes_of(value.shape[0]) % period
    up = jnp.where(lane == period - 1, 0.0, rolled(value, -1, 1))
    return up + jnp.where(lane == 0, 0.0, rolled(value, 1, 1))


def fine_sum(ref, r, a, n):
    centre = [ref[r, h, pl.ds(a, n), :] for h in range(2)]
    along_z = z_sum_halves(*centre)
    summed = []
    for h in range(2):
        along_x = ref[r - 1, h, pl.ds(a, n), :] + ref[r + 1, h, pl.ds(a, n), :]
        along_y = ref[r, h, pl.ds(a - 1, n), :] + ref[r, h, pl.ds(a + 1, n), :]
        summed.append(along_x + along_y + along_z[h])
    return centre, summed


def middle_sum(ref, r, a, n):
    centre = ref[r, pl.ds(a, n), :]
    along_x = ref[r - 1, pl.ds(a, n), :] + ref[r + 1, pl.ds(a, n), :]
    along_y = ref[r, pl.ds(a - 1, n), :] + ref[r, pl.ds(a + 1, n), :]
    return centre, along_x + along_y + z_sum(centre, 128)


def pair_x_sum(before, here, after):
    return here + jnp.where(lanes_of(here.shape[0]) < 64, before, after)


def fold_lanes(low, high):
    rows = low.shape[0]
    lane = lanes_of(rows)
    index = (lane * 2) % 128
    low = jnp.take_along_axis(low + rolled(low, -1, 1), index, axis=1)
    high = jnp.take_along_axis(high + rolled(high, -1, 1), index, axis=1)
    return jnp.where(lane < 64, low, high)


def spread_lanes(value):
    lane = lanes_of(value.shape[0])
    index = lane // 2
    return jnp.take_along_axis(value, index, axis=1), jnp.take_along_axis(value, index + 64, axis=1)


def dot(a, b):
    return jnp.dot(a, b, precision=lax.Precision.HIGHEST, preferred_element_type=F32)


def cycle_kernel(
    W, N,
    f_hbm, s_hbm, common_hbm, invx_hbm, invy_hbm,
    out_v, res_v,
    f_in, s_in, common, invx, invy,
    va, wa, v2a, ua, ub, fold,
    vb, wb, v2b, tb, ub1, ub2, fb, db, foldb,
    gvw, gv2, t2, u2,
    modes, tally,
    in_sem, send_sem, recv_sem, far_send, far_recv, gather_send, gather_recv, wide_send, wide_recv,
):
    i = lax.axis_index("wide")
    n = lax.axis_index("narrow")

    loads = [
        pltpu.make_async_copy(src, dst, in_sem.at[min(k, 2)])
        for k, (src, dst) in enumerate(
            (
                (s_hbm, s_in),
                (f_hbm, f_in),
                (common_hbm, common),
                (invx_hbm.at[pl.ds(i, 5)], invx),
                (invy_hbm.at[n], invy),
            )
        )
    ]
    barrier = pltpu.get_barrier_semaphore()

    def greet(wide_id, narrow_id):
        pl.semaphore_signal(barrier, inc=1, device_id=(wide_id, narrow_id), device_id_type=MESH)

    has_low, has_high = i > 0, i < W - 1

    def there(dx, dy):
        terms = []
        if dx > 0:
            terms.append(i < W - dx)
        if dx < 0:
            terms.append(i >= -dx)
        if dy > 0:
            terms.append(n < N - dy)
        if dy < 0:
            terms.append(n >= -dy)
        return functools.reduce(jnp.logical_and, terms)

    def flipped(index, mask):
        result, bit = index, 1
        while bit <= mask:
            if mask & bit:
                result = result + bit * (1 - 2 * lax.rem(lax.div(index, bit), 2))
            bit *= 2
        return result

    far_columns = sorted(range(1, N), key=lambda m: (m // 4, min(m % 4, 4 - m % 4), m), reverse=True)
    far_rows = sorted(range(1, W), key=lambda m: (m // 8 + min(m // 2 % 4, 4 - m // 2 % 4), m), reverse=True)
    for m in far_columns:
        other = flipped(n, m)
        pl.when(has_low)(functools.partial(greet, i - 1, other))
        pl.when(has_high)(functools.partial(greet, i + 1, other))
        greet(i, other)
    for m in far_rows:
        greet(flipped(i, m), n)

    for load in loads:
        load.start()

    sides = (-1, 1)
    corners = [(dx, dy) for dx in sides for dy in sides]

    def zero(ref, *index):
        shape = ref.at[index].shape if index else ref.shape
        ref[index if index else ...] = jnp.zeros(shape, F32)

    all_ = slice(None)

    @pl.when(i == 0)
    def _():
        for ref in (va, wa):
            zero(ref, pl.ds(0, 4))
        for ref in (vb, wb, v2b):
            zero(ref, pl.ds(0, 4))
        zero(gvw, pl.ds(0, 2))
        zero(gv2, pl.ds(0, 2))

    @pl.when(i == W - 1)
    def _():
        for ref in (va, wa):
            zero(ref, pl.ds(12, 4))
        for ref in (vb, wb, v2b):
            zero(ref, pl.ds(8, 4))
        zero(gvw, pl.ds(3, 2))
        zero(gv2, pl.ds(3, 2))

    @pl.when(i == 1)
    def _():
        zero(gvw, 0)
        zero(gv2, 0)

    @pl.when(i == W - 2)
    def _():
        zero(gvw, 4)
        zero(gv2, 4)

    @pl.when(n == 0)
    def _():
        for ref in (va, wa):
            zero(ref, all_, all_, pl.ds(0, 8))
        for ref in (vb, wb, v2b):
            zero(ref, all_, pl.ds(0, 8))

    @pl.when(n == N - 1)
    def _():
        for ref in (va, wa):
            zero(ref, all_, all_, pl.ds(40, 8))
        for ref in (vb, wb, v2b):
            zero(ref, all_, pl.ds(24, 8))

    cols = 8 * N
    zero(gvw, pl.ds(1, 3), all_, pl.ds(0, 8))
    zero(gvw, pl.ds(1, 3), all_, pl.ds(8 + cols, 8))
    zero(gv2, 2, pl.ds(0, 8))
    zero(gv2, 2, pl.ds(8 + cols, 8))
    zero(t2, all_, pl.ds(0, 8))
    zero(t2, all_, pl.ds(8 + cols, 8))

    loads[0].wait()
    loads[1].wait()

    def start_fine(r, _):
        for h in range(2):
            screen = s_in[r, :, pl.ds(128 * h, 128)]
            weight = OMEGA / (6.0 + screen)
            wa[r + 4, h, pl.ds(8, 32), :] = weight
            va[r + 4, h, pl.ds(8, 32), :] = f_in[r, :, pl.ds(128 * h, 128)] * weight
        return 0

    lax.fori_loop(0, 8, start_fine, 0, unroll=True)

    directions = [(0, -1), (0, 1)] + corners + [(-1, 0), (1, 0)]
    rows_of = {}

    def waiter(rows, send, recv, to):
        part = tally.at[pl.ds(0, rows), :]
        return pltpu.make_async_remote_copy(
            src_ref=part, dst_ref=part, send_sem=send, recv_sem=recv, device_id=to, device_id_type=MESH
        )

    def beside(dx, dy):
        return lax.rem(i + dx + W, W), lax.rem(n + dy + N, N)

    def span(step, first, size, depths):
        if step == 0:
            return pl.ds(first, size), pl.ds(first, size)
        low, high = depths
        count = high - low + 1
        if step > 0:
            return pl.ds(first + size - high, count), pl.ds(first - high, count)
        return pl.ds(first + low - 1, count), pl.ds(first + size + low - 1, count)

    def exchange(family, src, dst, dx, dy):
        d = directions.index((dx, dy))
        rows_of[family, d] = rows_of.get((family, d), 0) + int(np.prod(src.shape)) // 128
        copy = pltpu.make_async_remote_copy(
            src_ref=src, dst_ref=dst, send_sem=send_sem.at[d], recv_sem=recv_sem.at[family, d],
            device_id=beside(dx, dy), device_id_type=MESH,
        )
        return copy, there(dx, dy)

    def fine_piece(family, ref, dx, dy, depth_x=None, depth_y=None):
        src_x, dst_x = span(dx, 4, 8, depth_x)
        src_y, dst_y = span(dy, 8, 32, depth_y)
        return exchange(family, ref.at[src_x, :, src_y, :], ref.at[dst_x, :, dst_y, :], dx, dy)

    def middle_piece(family, ref, dx, dy, depth_x=None, depth_y=None):
        src_x, dst_x = span(dx, 4, 4, depth_x)
        src_y, dst_y = span(dy, 8, 16, depth_y)
        return exchange(family, ref.at[src_x, src_y, :], ref.at[dst_x, dst_y, :], dx, dy)

    def start(pieces):
        for copy, to in pieces:
            pl.when(to)(copy.start)

    def receive(family):
        for d, (dx, dy) in enumerate(directions):
            arrival = waiter(rows_of[family, d], send_sem.at[d], recv_sem.at[family, d], beside(dx, dy))
            pl.when(there(-dx, -dy))(arrival.wait_recv)

    def halo_sent():
        for d, (dx, dy) in enumerate(directions):
            rows = sum(rows_of[family, d] for family in range(4))
            pl.when(there(dx, dy))(waiter(rows, send_sem.at[d], recv_sem.at[0, d], beside(dx, dy)).wait_send)

    fine_near = (
        [fine_piece(0, va, 0, d, None, (1, 2)) for d in sides]
        + [fine_piece(0, wa, 0, d, None, (1, 1)) for d in sides]
        + [fine_piece(0, va, dx, dy, (1, 1), (1, 1)) for dx, dy in corners]
        + [fine_piece(0, va, d, 0, (1, 2)) for d in sides]
        + [fine_piece(0, wa, d, 0, (1, 1)) for d in sides]
    )
    fine_far = (
        [fine_piece(1, va, 0, d, None, (3, 4)) for d in sides]
        + [fine_piece(1, wa, 0, d, None, (2, 3)) for d in sides]
        + [fine_piece(1, va, dx, dy, (1, 1), (2, 3)) for dx, dy in corners]
        + [fine_piece(1, va, dx, dy, (2, 3), (1, 2)) for dx, dy in corners]
        + [fine_piece(1, wa, dx, dy, (1, 2), (1, 2)) for dx, dy in corners]
        + [fine_piece(1, va, d, 0, (3, 4)) for d in sides]
        + [fine_piece(1, wa, d, 0, (2, 3)) for d in sides]
    )

    def middle_pieces(family, ref, depth, corner):
        return (
            [middle_piece(family, ref, 0, d, None, (1, depth)) for d in sides]
            + [middle_piece(family, ref, dx, dy, (1, corner), (1, corner)) for dx, dy in corners]
            + [middle_piece(family, ref, d, 0, (1, depth)) for d in sides]
        )

    middle_w = middle_pieces(2, wb, 3, 2)
    middle_v = middle_pieces(2, vb, 3, 2)
    middle_v2 = middle_pieces(3, v2b, 4, 3)

    window = pl.ds(pl.multiple_of(8 * n, 8), WINDOW)
    reach = (-2, -1, 1, 2)

    def coarse_far(d):
        k = reach.index(d)
        args = dict(
            send_sem=far_send.at[k], recv_sem=far_recv.at[k], device_id=beside(d, 0), device_id_type=MESH
        )
        copies = [pltpu.make_async_remote_copy(src_ref=gv2.at[2, window, :], dst_ref=gv2.at[2 - d, window, :], **args)]
        if abs(d) == 2:
            copies.append(
                pltpu.make_async_remote_copy(
                    src_ref=gvw.at[2, :, window, :], dst_ref=gvw.at[2 - d, :, window, :], **args
                )
            )
        return copies

    def coarse_far_start():
        for d in reach:
            for copy in coarse_far(d):
                pl.when(there(d, 0))(copy.start)

    def coarse_far_waiter(d):
        k = reach.index(d)
        return waiter((3 if abs(d) == 2 else 1) * WINDOW, far_send.at[k], far_recv.at[k], beside(d, 0))

    greeted = (W - 1) + (N - 1) * (1 + has_low.astype(jnp.int32) + has_high.astype(jnp.int32))
    pl.semaphore_wait(barrier, greeted)

    start(fine_near)
    start(fine_far)

    def screen_middle(q, _):
        for h in range(2):
            lanes = pl.ds(128 * h, 128)
            fold[q, h, :, :] = s_in[2 * q, :, lanes] + s_in[2 * q + 1, :, lanes]
        low, high = (
            fold[q, h, pl.ds(0, 16, stride=2), :] + fold[q, h, pl.ds(1, 16, stride=2), :] for h in range(2)
        )
        diagonal = 6.0 + 0.125 * fold_lanes(low, high)
        db[q, :, :] = diagonal
        wb[q + 4, pl.ds(8, 16), :] = OMEGA / diagonal
        return 0

    lax.fori_loop(0, 4, screen_middle, 0, unroll=True)
    start(middle_w)

    for h in range(2):
        foldb[h, :, :] = (db[2 * h, :, :] - 6.0) + (db[2 * h + 1, :, :] - 6.0)
    low, high = (foldb[h, pl.ds(0, 8, stride=2), :] + foldb[h, pl.ds(1, 8, stride=2), :] for h in range(2))
    coarse_d = 6.0 + 0.125 * fold_lanes(low, high)
    own_cols = pl.ds(pl.multiple_of(8 + 8 * n, 8), 8)
    gvw[2, 1, own_cols, :] = coarse_d

    def gather_copy(what, dx, k):
        other = lax.rem(n + k, N)
        target = lax.rem(i + dx + W, W)
        return pltpu.make_async_remote_copy(
            src_ref=gvw.at[2, what, own_cols, :], dst_ref=gvw.at[2 - dx, what, own_cols, :],
            send_sem=gather_send.at[what, dx + 1], recv_sem=gather_recv.at[what, 1 - dx],
            device_id=(target, other), device_id_type=MESH,
        )

    def gather_waiter(what, dx):
        rows = 8 * (N if dx else N - 1)
        target = (lax.rem(i + 1, W), n)
        return waiter(rows, gather_send.at[what, dx + 1], gather_recv.at[what, dx + 1], target)

    def for_each(k, call):
        pl.when(k > 0)(functools.partial(call, 0))
        pl.when(has_low)(functools.partial(call, -1))
        pl.when(has_high)(functools.partial(call, 1))

    def gather_start(what, k, _):
        for_each(k, lambda dx: gather_copy(what, dx, k).start())
        return 0

    def gather_receive(what):
        for_each(1, lambda dx: gather_waiter(what, dx).wait_recv())

    def gather_sent(what):
        for_each(1, lambda dx: gather_waiter(what, dx).wait_send())

    lax.fori_loop(0, N, functools.partial(gather_start, 1), 0)

    def fine_v2(a, count, r, _):
        centre, summed = fine_sum(va, r, a, count)
        for h in range(2):
            v2a[r, h, pl.ds(a, count), :] = (1.0 + KEEP) * centre[h] + wa[r, h, pl.ds(a, count), :] * summed[h]
        return 0

    receive(0)
    fine_v2(8, 32, 3, 0)
    lax.fori_loop(4, 12, functools.partial(fine_v2, 7, 34), 0, unroll=True)
    fine_v2(8, 32, 12, 0)

    def fine_residual(ref, r, h, centre, summed):
        lanes = pl.ds(128 * h, 128)
        return f_in[r, :, lanes] - (6.0 + s_in[r, :, lanes]) * centre + summed

    def fine_down(q, _):
        c0, n0 = fine_sum(v2a, 2 * q + 4, 8, 32)
        c1, n1 = fine_sum(v2a, 2 * q + 5, 8, 32)
        for h in range(2):
            fold[q, h, :, :] = fine_residual(v2a, 2 * q, h, c0[h], n0[h]) + fine_residual(
                v2a, 2 * q + 1, h, c1[h], n1[h]
            )
        low, high = (
            fold[q, h, pl.ds(0, 16, stride=2), :] + fold[q, h, pl.ds(1, 16, stride=2), :] for h in range(2)
        )
        source = 0.5 * fold_lanes(low, high)
        fb[q, :, :] = source
        vb[q + 4, pl.ds(8, 16), :] = source * wb[q + 4, pl.ds(8, 16), :]
        return 0

    lax.fori_loop(0, 4, fine_down, 0, unroll=True)
    start(middle_v)

    receive(1)
    lax.fori_loop(1, 15, functools.partial(fine_v2, 4, 40), 0, unroll=True)

    receive(2)
    for r in range(3, 9):
        centre, summed = middle_sum(vb, r, 4, 24)
        tb[r, pl.ds(4, 24), :] = (1.0 + KEEP) * centre + wb[r, pl.ds(4, 24), :] * summed
    for r in range(4):
        centre, summed = middle_sum(tb, r + 4, 8, 16)
        v2b[r + 4, pl.ds(8, 16), :] = centre
        rest = fb[r, :, :] - db[r, :, :] * centre + summed
        if r % 2 == 0:
            held = rest
        else:
            foldb[r // 2, :, :] = held + rest
    low, high = (foldb[h, pl.ds(0, 8, stride=2), :] + foldb[h, pl.ds(1, 8, stride=2), :] for h in range(2))
    gvw[2, 0, own_cols, :] = 0.5 * fold_lanes(low, high) * (OMEGA / coarse_d)

    lax.fori_loop(0, N, functools.partial(gather_start, 0), 0)
    start(middle_v2)
    gather_receive(1)
    gather_receive(0)

    slab = pl.ds(8, cols)
    turned = [rolled(gvw[t, 0, slab, :], 64, 1) for t in (1, 2, 3)]
    for t in range(3):
        centre = gvw[t + 1, 0, slab, :]
        along_x = pair_x_sum(turned[max(t - 1, 0)], turned[t], turned[min(t + 1, 2)])
        along_y = gvw[t + 1, 0, pl.ds(7, cols), :] + gvw[t + 1, 0, pl.ds(9, cols), :]
        diagonal = gvw[t + 1, 1, slab, :]
        weight = jnp.where(diagonal > 0.0, OMEGA / diagonal, 0.0)
        t2[t, slab, :] = (1.0 + KEEP) * centre + weight * (along_x + along_y + z_sum(centre, 64))
    turned = [rolled(t2[t, slab, :], 64, 1) for t in range(3)]
    centre = t2[1, slab, :]
    gv2[2, slab, :] = centre
    diagonal = gvw[2, 1, slab, :]
    along_x = pair_x_sum(*turned)
    along_y = t2[1, pl.ds(7, cols), :] + t2[1, pl.ds(9, cols), :]
    rest = diagonal * (gvw[2, 0, slab, :] * (1.0 / OMEGA) - centre) + (along_x + along_y + z_sum(centre, 64))

    sizes = (common, invx, invy)
    part = tally.at[pl.ds(0, sum(int(np.prod(ref.shape)) // 128 for ref in sizes)), :]
    pltpu.make_async_copy(part, part, in_sem.at[2]).wait()
    along_z = dot(rest, common[pl.ds(0, 128), :])
    along_yz = dot(common[pl.ds(256, 4 * N), pl.ds(0, cols)], along_z)
    group = lanes_of(N) // 32
    mine = along_yz[0:N, :]
    for g in range(1, 4):
        mine = jnp.where(group == g, along_yz[g * N : (g + 1) * N, :], mine)
    modes[i, pl.ds(0, N), :] = mine
    modes[i, pl.ds(N, 1), :] = jnp.sum(diagonal - 6.0, axis=0, keepdims=True)

    def wide_copy(k):
        return pltpu.make_async_remote_copy(
            src_ref=modes.at[i], dst_ref=modes.at[i], send_sem=wide_send.at[0], recv_sem=wide_recv.at[0],
            device_id=(lax.rem(i + k, W), n), device_id_type=MESH,
        )

    def wide_start(k, _):
        wide_copy(k).start()
        return 0

    everyone = waiter((W - 1) * (N + 1), wide_send.at[0], wide_recv.at[0], (lax.rem(i + 1, W), n))

    lax.fori_loop(1, W, wide_start, 0)
    coarse_far_start()
    halo_sent()
    for what in range(2):
        gather_sent(what)
    receive(3)
    everyone.wait_recv()

    total = jnp.sum(modes[:, N, :], keepdims=True)
    mean = total * (1.0 / (2 * W * 8 * N * 64))
    shifted = common[pl.ds(256 + 4 * N, N), :] + mean
    sine_x, eigen_x = sine_table(W), sine_eigen(W)
    factor = (2.0 / (W + 1.0)) * (2.0 / (4 * N + 1.0)) * (2.0 / 33.0)
    half = W // 2
    even, odd = [], []
    for j in range(half):
        first, second = modes[j, pl.ds(0, N), :], modes[W - 1 - j, pl.ds(0, N), :]
        even.append(first + second)
        odd.append(first - second)
    found = [None] * 5
    for a in range(W):
        values = even if a % 2 == 0 else odd
        acc = None
        for j in range(half):
            term = values[j] * np.float32(sine_x[a, j])
            acc = term if acc is None else acc + term
        scaled = acc * np.float32(factor) / (shifted + np.float32(eigen_x[a]))
        for t in range(5):
            term = invx[t, pl.ds(a, 1), :] * scaled
            found[t] = term if found[t] is None else found[t] + term
    spread = dot(invy[:, pl.ds(0, N)], jnp.concatenate(found, axis=1))
    group = lanes_of(WINDOW) // 32
    parts = []
    for t in range(5):
        lanes = slice(128 * t, 128 * t + 128)
        part = spread[0:WINDOW, lanes]
        for g in range(1, 4):
            part = jnp.where(group == g, spread[g * WINDOW : (g + 1) * WINDOW, lanes], part)
        parts.append(part)
    correction = dot(jnp.concatenate(parts, axis=0), common[pl.ds(128, 128), :])

    for d in reach:
        pl.when(there(-d, 0))(coarse_far_waiter(d).wait_recv)
    u = [gv2[t, window, :] + correction[WINDOW * t : WINDOW * (t + 1), :] for t in range(5)]

    def pair_sweep(u, slots):
        turned = {t: rolled(u[t], 64, 1) for t in u}
        swept = {}
        for t in slots:
            along_x = pair_x_sum(turned.get(t - 1, turned[t]), turned[t], turned.get(t + 1, turned[t]))
            along_y = rolled(u[t], 1, 0) + rolled(u[t], -1, 0)
            diagonal = gvw[t, 1, window, :]
            weight = jnp.where(diagonal > 0.0, OMEGA / diagonal, 0.0)
            summed = along_x + along_y + z_sum(u[t], 64)
            swept[t] = KEEP * u[t] + gvw[t, 0, window, :] + weight * summed
        return swept

    u = pair_sweep(dict(enumerate(u)), range(5))
    u = pair_sweep(u, range(1, 4))

    for t in (1, 2, 3):
        u2[t - 1, :, :] = u[t]
    for t in range(3):
        halves = spread_lanes(u2[t, pl.ds(4, 16), :])
        for h in range(2):
            for k in range(2):
                r = 4 * t + 2 * h + k
                ub1[r, pl.ds(0, 16, stride=2), :] = halves[h]
                ub1[r, pl.ds(1, 16, stride=2), :] = halves[h]
    for r in range(12):
        ub1[r, :, :] = ub1[r, :, :] + v2b[r, :, :]

    def middle_sweep(src, dst, r):
        centre, summed = middle_sum(src, r, 4, 24)
        part = (r, pl.ds(4, 24), slice(None))
        dst[part] = KEEP * centre + vb[part] + wb[part] * summed

    for r in range(1, 11):
        middle_sweep(ub1, ub2, r)
    for r in range(2, 10):
        middle_sweep(ub2, ub1, r)

    def fine_spread(q, _):
        halves = spread_lanes(ub1[q + 2, pl.ds(4, 24), :])
        for k in range(2):
            r = 2 * q + k
            for h in range(2):
                ua[r, h, pl.ds(0, 24, stride=2), :] = halves[h]
                ua[r, h, pl.ds(1, 24, stride=2), :] = halves[h]
        for k in range(2):
            r = 2 * q + k
            for h in range(2):
                ua[r, h, :, :] = ua[r, h, :, :] + v2a[r, h, :, :]
        return 0

    lax.fori_loop(0, 8, fine_spread, 0, unroll=True)

    def fine_sweep(src, dst, r, _):
        centre, summed = fine_sum(src, r, 4, 40)
        for h in range(2):
            part = (r, h, pl.ds(4, 40), slice(None))
            dst[part] = KEEP * centre[h] + va[part] + wa[part] * summed[h]
        return 0

    lax.fori_loop(2, 14, functools.partial(fine_sweep, ua, ub), 0, unroll=True)
    lax.fori_loop(3, 13, functools.partial(fine_sweep, ub, ua), 0, unroll=True)

    def fine_end(r, _):
        centre, summed = fine_sum(ua, r + 4, 8, 32)
        for h in range(2):
            lanes = pl.ds(128 * h, 128)
            out_v[r, :, lanes] = centre[h]
            res_v[r, :, lanes] = fine_residual(ua, r, h, centre[h], summed[h])
        return 0

    lax.fori_loop(0, 8, fine_end, 0, unroll=True)
    for d in reach:
        pl.when(there(d, 0))(coarse_far_waiter(d).wait_send)
    everyone.wait_send()


def store_kernel(out_v, res_v, out_hbm, res_hbm, sem):
    copies = [
        pltpu.make_async_copy(src, dst, sem.at[k]) for k, (src, dst) in enumerate(((out_v, out_hbm), (res_v, res_hbm)))
    ]
    for copy in copies:
        copy.start()
    for copy in copies:
        copy.wait()


def solution(mesh):
    W, N = mesh.shape["wide"], mesh.shape["narrow"]
    common, invx, invy = tables(W, N)
    cols = 8 * N
    vmem = pltpu.VMEM
    dma = pltpu.SemaphoreType.DMA
    fine, middle = (16, 2, 48, 128), (12, 32, 128)
    scratch = [
        vmem((8, 32, 256), F32), vmem((8, 32, 256), F32),
        vmem(common.shape, F32), vmem((5, W, 128), F32), vmem((4 * WINDOW, 128), F32),
        vmem(fine, F32), vmem(fine, F32), vmem(fine, F32), vmem(fine, F32), vmem(fine, F32),
        vmem((4, 2, 32, 128), F32),
        vmem(middle, F32), vmem(middle, F32), vmem(middle, F32), vmem(middle, F32),
        vmem(middle, F32), vmem(middle, F32),
        vmem((4, 16, 128), F32), vmem((4, 16, 128), F32), vmem((2, 16, 128), F32),
        vmem((5, 2, cols + 16, 128), F32), vmem((5, cols + 16, 128), F32),
        vmem((3, cols + 16, 128), F32), vmem((3, WINDOW, 128), F32),
        vmem((W, N + 1, 128), F32), vmem((640, 128), F32),
        dma((3,)), dma((8,)), dma((4, 8)), dma((4,)), dma((4,)), dma((2, 3)), dma((2, 3)), dma((1,)), dma((1,)),
    ]

    def per_device(divergence, screening):
        block = pltpu.VMEM((8, 32, 256), F32)
        results = pl.pallas_call(
            functools.partial(cycle_kernel, W, N),
            out_shape=(block, block),
            in_specs=[pl.BlockSpec(memory_space=pltpu.HBM)] * 5,
            out_specs=(pl.BlockSpec(memory_space=pltpu.VMEM),) * 2,
            scratch_shapes=scratch,
            compiler_params=pltpu.CompilerParams(
                collective_id=0, has_side_effects=True, vmem_limit_bytes=56 * 1024 * 1024
            ),
        )(divergence, screening, jnp.asarray(common), jnp.asarray(invx), jnp.asarray(invy))
        stored = jax.ShapeDtypeStruct((8, 32, 256), F32)
        anywhere = pl.BlockSpec(memory_space=pl.ANY)
        return pl.pallas_call(
            store_kernel,
            out_shape=(stored, stored),
            in_specs=[pl.BlockSpec(memory_space=pltpu.VMEM)] * 2,
            out_specs=(anywhere, anywhere),
            scratch_shapes=[dma((2,))],
            compiler_params=pltpu.CompilerParams(vmem_limit_bytes=4 * 1024 * 1024),
        )(*results)

    spec = P("wide", "narrow", None)
    return jax.shard_map(
        per_device, mesh=mesh, in_specs=(spec, spec), out_specs=(spec, spec), check_vma=False
    )
```

```python
import functools

import numpy as np
import jax
import jax.numpy as jnp
from jax import lax
from jax.experimental import pallas as pl
from jax.experimental.pallas import tpu as pltpu
from jax.sharding import PartitionSpec as P

MESH = pl.DeviceIdType.MESH
F32 = jnp.float32
OMEGA = 0.8
KEEP = 0.2
WINDOW = 24


def sine_table(count):
    ladder = np.arange(count, dtype=np.float64) + 1.0
    return np.sin(np.pi * ladder[:, None] * ladder[None, :] / (count + 1.0))


def sine_eigen(count):
    ladder = np.arange(count, dtype=np.float64) + 1.0
    return 2.0 - 2.0 * np.cos(np.pi * ladder / (count + 1.0))


def tables(wide, narrow):
    count_y, count_z = 4 * narrow, 32
    sine_x, sine_y, sine_z = sine_table(wide), sine_table(count_y), sine_table(count_z)
    to_modes = np.tile(np.repeat(sine_z.T, 2, axis=0), (2, 4))
    from_modes = np.tile(np.repeat(sine_z, 2, axis=1), (4, 2))
    rows_y = 0.5 * np.repeat(sine_y, 2, axis=1)
    rows_y = np.pad(rows_y, ((0, 0), (0, 128 - rows_y.shape[1])))
    eigen_y = sine_eigen(count_y).reshape(4, narrow)
    eigen = eigen_y.T[:, :, None] + sine_eigen(count_z)[None, None, :]
    eigen = eigen.reshape(narrow, 128)
    common = np.concatenate([to_modes, from_modes, rows_y, eigen], axis=0)
    inverse_x = np.pad(sine_x, ((2, 2), (0, 0)))
    inverse_x = np.repeat(inverse_x[:, :, None], 128, axis=2)
    fine_y = np.pad(np.repeat(sine_y, 2, axis=0), ((8, 8), (0, 0)))
    inverse_y = np.zeros((narrow, 4, WINDOW, 128))
    for n in range(narrow):
        for g in range(4):
            inverse_y[n, g, :, :narrow] = fine_y[8 * n : 8 * n + WINDOW, g * narrow : (g + 1) * narrow]
    inverse_y = inverse_y.reshape(narrow, 4 * WINDOW, 128)
    return [a.astype(np.float32) for a in (common, inverse_x, inverse_y)]


def rolled(value, shift, axis):
    return pltpu.roll(value, shift % value.shape[axis], axis)


def lanes_of(rows):
    return lax.broadcasted_iota(jnp.int32, (rows, 128), 1)


def z_sum_halves(low, high):
    lane = lanes_of(low.shape[0])
    up_low, up_high = rolled(low, -1, 1), rolled(high, -1, 1)
    down_low, down_high = rolled(low, 1, 1), rolled(high, 1, 1)
    last, first = lane == 127, lane == 0
    sum_low = jnp.where(last, up_high, up_low) + jnp.where(first, 0.0, down_low)
    sum_high = jnp.where(last, 0.0, up_high) + jnp.where(first, down_low, down_high)
    return sum_low, sum_high


def z_sum(value, period):
    lane = lanes_of(value.shape[0]) % period
    up = jnp.where(lane == period - 1, 0.0, rolled(value, -1, 1))
    return up + jnp.where(lane == 0, 0.0, rolled(value, 1, 1))


def fine_sum(ref, r, a, n):
    centre = [ref[r, h, pl.ds(a, n), :] for h in range(2)]
    along_z = z_sum_halves(*centre)
    summed = []
    for h in range(2):
        along_x = ref[r - 1, h, pl.ds(a, n), :] + ref[r + 1, h, pl.ds(a, n), :]
        along_y = ref[r, h, pl.ds(a - 1, n), :] + ref[r, h, pl.ds(a + 1, n), :]
        summed.append(along_x + along_y + along_z[h])
    return centre, summed


def middle_sum(ref, r, a, n):
    centre = ref[r, pl.ds(a, n), :]
    along_x = ref[r - 1, pl.ds(a, n), :] + ref[r + 1, pl.ds(a, n), :]
    along_y = ref[r, pl.ds(a - 1, n), :] + ref[r, pl.ds(a + 1, n), :]
    return centre, along_x + along_y + z_sum(centre, 128)


def pair_x_sum(before, here, after):
    return here + jnp.where(lanes_of(here.shape[0]) < 64, before, after)


def fold_lanes(low, high):
    rows = low.shape[0]
    lane = lanes_of(rows)
    index = (lane * 2) % 128
    low = jnp.take_along_axis(low + rolled(low, -1, 1), index, axis=1)
    high = jnp.take_along_axis(high + rolled(high, -1, 1), index, axis=1)
    return jnp.where(lane < 64, low, high)


def spread_lanes(value):
    lane = lanes_of(value.shape[0])
    index = lane // 2
    return jnp.take_along_axis(value, index, axis=1), jnp.take_along_axis(value, index + 64, axis=1)


def dot(a, b):
    return jnp.dot(a, b, precision=lax.Precision.HIGHEST, preferred_element_type=F32)


def cycle_kernel(
    W, N,
    f_hbm, s_hbm, common_hbm, invx_hbm, invy_hbm,
    out_v, res_v,
    f_in, s_in, common, invx, invy,
    va, wa, v2a, ua, ub, fold,
    vb, wb, v2b, tb, ub1, ub2, fb, db, foldb,
    gvw, gv2, t2, u2,
    modes, tally,
    in_sem, send_sem, recv_sem, far_send, far_recv, gather_send, gather_recv, wide_send, wide_recv,
):
    i = lax.axis_index("wide")
    n = lax.axis_index("narrow")

    loads = [
        pltpu.make_async_copy(src, dst, in_sem.at[min(k, 2)])
        for k, (src, dst) in enumerate(
            (
                (s_hbm, s_in),
                (f_hbm, f_in),
                (common_hbm, common),
                (invx_hbm.at[pl.ds(i, 5)], invx),
                (invy_hbm.at[n], invy),
            )
        )
    ]
    barrier = pltpu.get_barrier_semaphore()

    def greet(wide_id, narrow_id):
        pl.semaphore_signal(barrier, inc=1, device_id=(wide_id, narrow_id), device_id_type=MESH)

    has_low, has_high = i > 0, i < W - 1

    def there(dx, dy):
        terms = []
        if dx > 0:
            terms.append(i < W - dx)
        if dx < 0:
            terms.append(i >= -dx)
        if dy > 0:
            terms.append(n < N - dy)
        if dy < 0:
            terms.append(n >= -dy)
        return functools.reduce(jnp.logical_and, terms)

    def flipped(index, mask):
        result, bit = index, 1
        while bit <= mask:
            if mask & bit:
                result = result + bit * (1 - 2 * lax.rem(lax.div(index, bit), 2))
            bit *= 2
        return result

    far_columns = sorted(range(1, N), key=lambda m: (m // 4, min(m % 4, 4 - m % 4), m), reverse=True)
    far_rows = sorted(range(1, W), key=lambda m: (m // 8 + min(m // 2 % 4, 4 - m // 2 % 4), m), reverse=True)
    for m in far_columns:
        other = flipped(n, m)
        pl.when(has_low)(functools.partial(greet, i - 1, other))
        pl.when(has_high)(functools.partial(greet, i + 1, other))
        greet(i, other)
    for m in far_rows:
        greet(flipped(i, m), n)

    for load in loads:
        load.start()

    sides = (-1, 1)
    corners = [(dx, dy) for dx in sides for dy in sides]

    def zero(ref, *index):
        shape = ref.at[index].shape if index else ref.shape
        ref[index if index else ...] = jnp.zeros(shape, F32)

    all_ = slice(None)

    @pl.when(i == 0)
    def _():
        for ref in (va, wa):
            zero(ref, pl.ds(0, 4))
        for ref in (vb, wb, v2b):
            zero(ref, pl.ds(0, 4))
        zero(gvw, pl.ds(0, 2))
        zero(gv2, pl.ds(0, 2))

    @pl.when(i == W - 1)
    def _():
        for ref in (va, wa):
            zero(ref, pl.ds(12, 4))
        for ref in (vb, wb, v2b):
            zero(ref, pl.ds(8, 4))
        zero(gvw, pl.ds(3, 2))
        zero(gv2, pl.ds(3, 2))

    @pl.when(i == 1)
    def _():
        zero(gvw, 0)
        zero(gv2, 0)

    @pl.when(i == W - 2)
    def _():
        zero(gvw, 4)
        zero(gv2, 4)

    @pl.when(n == 0)
    def _():
        for ref in (va, wa):
            zero(ref, all_, all_, pl.ds(0, 8))
        for ref in (vb, wb, v2b):
            zero(ref, all_, pl.ds(0, 8))

    @pl.when(n == N - 1)
    def _():
        for ref in (va, wa):
            zero(ref, all_, all_, pl.ds(40, 8))
        for ref in (vb, wb, v2b):
            zero(ref, all_, pl.ds(24, 8))

    cols = 8 * N
    zero(gvw, pl.ds(1, 3), all_, pl.ds(0, 8))
    zero(gvw, pl.ds(1, 3), all_, pl.ds(8 + cols, 8))
    zero(gv2, 2, pl.ds(0, 8))
    zero(gv2, 2, pl.ds(8 + cols, 8))
    zero(t2, all_, pl.ds(0, 8))
    zero(t2, all_, pl.ds(8 + cols, 8))

    loads[0].wait()
    loads[1].wait()

    def start_fine(r, _):
        for h in range(2):
            screen = s_in[r, :, pl.ds(128 * h, 128)]
            weight = OMEGA / (6.0 + screen)
            wa[r + 4, h, pl.ds(8, 32), :] = weight
            va[r + 4, h, pl.ds(8, 32), :] = f_in[r, :, pl.ds(128 * h, 128)] * weight
        return 0

    lax.fori_loop(0, 8, start_fine, 0, unroll=True)

    rows_of = {}
    both_x, both_y = jnp.logical_and(has_low, has_high), jnp.logical_and(n > 0, n < N - 1)

    def by_place(call):
        for sides_x in (1, 2):
            for sides_y in (1, 2):
                here_x = both_x if sides_x == 2 else jnp.logical_not(both_x)
                here_y = both_y if sides_y == 2 else jnp.logical_not(both_y)
                pl.when(jnp.logical_and(here_x, here_y))(functools.partial(call, sides_x, sides_y))

    def waiter(rows, send, recv, to):
        part = tally.at[pl.ds(0, rows), :]
        return pltpu.make_async_remote_copy(
            src_ref=part, dst_ref=part, send_sem=send, recv_sem=recv, device_id=to, device_id_type=MESH
        )

    def beside(dx, dy):
        return lax.rem(i + dx + W, W), lax.rem(n + dy + N, N)

    def span(step, first, size, depths):
        if step == 0:
            return pl.ds(first, size), pl.ds(first, size)
        low, high = depths
        count = high - low + 1
        if step > 0:
            return pl.ds(first + size - high, count), pl.ds(first - high, count)
        return pl.ds(first + low - 1, count), pl.ds(first + size + low - 1, count)

    def exchange(family, src, dst, dx, dy):
        kind = (family, dx != 0, dy != 0)
        if dx >= 0 and dy >= 0:
            rows_of[kind] = rows_of.get(kind, 0) + int(np.prod(src.shape)) // 128
        copy = pltpu.make_async_remote_copy(
            src_ref=src, dst_ref=dst, send_sem=send_sem.at[0], recv_sem=recv_sem.at[family],
            device_id=beside(dx, dy), device_id_type=MESH,
        )
        return copy, there(dx, dy)

    def halo_waiter(families, sides_x, sides_y):
        rows = sum(
            sides_x * rows_of[family, True, False]
            + sides_y * rows_of[family, False, True]
            + sides_x * sides_y * rows_of[family, True, True]
            for family in families
        )
        return waiter(rows, send_sem.at[0], recv_sem.at[families[0]], (lax.rem(i + 1, W), n))

    def fine_piece(family, ref, dx, dy, depth_x=None, depth_y=None):
        src_x, dst_x = span(dx, 4, 8, depth_x)
        src_y, dst_y = span(dy, 8, 32, depth_y)
        return exchange(family, ref.at[src_x, :, src_y, :], ref.at[dst_x, :, dst_y, :], dx, dy)

    def middle_piece(family, ref, dx, dy, depth_x=None, depth_y=None):
        src_x, dst_x = span(dx, 4, 4, depth_x)
        src_y, dst_y = span(dy, 8, 16, depth_y)
        return exchange(family, ref.at[src_x, src_y, :], ref.at[dst_x, dst_y, :], dx, dy)

    def start(pieces):
        for copy, to in pieces:
            pl.when(to)(copy.start)

    def receive(family):
        by_place(lambda sides_x, sides_y: halo_waiter([family], sides_x, sides_y).wait_recv())

    def halo_sent():
        by_place(lambda sides_x, sides_y: halo_waiter(range(3), sides_x, sides_y).wait_send())

    fine_near = (
        [fine_piece(0, va, 0, d, None, (1, 2)) for d in sides]
        + [fine_piece(0, wa, 0, d, None, (1, 1)) for d in sides]
        + [fine_piece(0, va, dx, dy, (1, 1), (1, 1)) for dx, dy in corners]
        + [fine_piece(0, va, d, 0, (1, 2)) for d in sides]
        + [fine_piece(0, wa, d, 0, (1, 1)) for d in sides]
    )
    fine_far = (
        [fine_piece(1, va, 0, d, None, (3, 4)) for d in sides]
        + [fine_piece(1, wa, 0, d, None, (2, 3)) for d in sides]
        + [fine_piece(1, va, dx, dy, (1, 1), (2, 3)) for dx, dy in corners]
        + [fine_piece(1, va, dx, dy, (2, 3), (1, 2)) for dx, dy in corners]
        + [fine_piece(1, wa, dx, dy, (1, 2), (1, 2)) for dx, dy in corners]
        + [fine_piece(1, va, d, 0, (3, 4)) for d in sides]
        + [fine_piece(1, wa, d, 0, (2, 3)) for d in sides]
    )

    def middle_pieces(family, ref, depth, corner):
        return (
            [middle_piece(family, ref, 0, d, None, (1, depth)) for d in sides]
            + [middle_piece(family, ref, dx, dy, (1, corner), (1, corner)) for dx, dy in corners]
            + [middle_piece(family, ref, d, 0, (1, depth)) for d in sides]
        )

    middle_w = middle_pieces(2, wb, 3, 2)
    middle_v = middle_pieces(2, vb, 3, 2)
    middle_v2 = middle_pieces(1, v2b, 4, 3)

    window = pl.ds(pl.multiple_of(8 * n, 8), WINDOW)
    reach = (-2, -1, 1, 2)

    def coarse_far(d):
        args = dict(
            send_sem=far_send.at[0], recv_sem=far_recv.at[0], device_id=beside(d, 0), device_id_type=MESH
        )
        copies = [pltpu.make_async_remote_copy(src_ref=gv2.at[2, window, :], dst_ref=gv2.at[2 - d, window, :], **args)]
        if abs(d) == 2:
            copies.append(
                pltpu.make_async_remote_copy(
                    src_ref=gvw.at[2, :, window, :], dst_ref=gvw.at[2 - d, :, window, :], **args
                )
            )
        return copies

    def coarse_far_start():
        for d in reach:
            for copy in coarse_far(d):
                pl.when(there(d, 0))(copy.start)

    def far_wait(call):
        further = jnp.logical_and(i > 1, i < W - 2)
        cases = (
            (1, 1, jnp.logical_not(both_x)),
            (2, 1, jnp.logical_and(both_x, jnp.logical_not(further))),
            (2, 2, further),
        )
        for near, far, here in cases:
            rows = (near + 3 * far) * WINDOW
            pl.when(here)(functools.partial(call, waiter(rows, far_send.at[0], far_recv.at[0], beside(1, 0))))

    greeted = (W - 1) + (N - 1) * (1 + has_low.astype(jnp.int32) + has_high.astype(jnp.int32))
    pl.semaphore_wait(barrier, greeted)

    start(fine_near)
    start(fine_far)

    def screen_middle(q, _):
        for h in range(2):
            lanes = pl.ds(128 * h, 128)
            fold[q, h, :, :] = s_in[2 * q, :, lanes] + s_in[2 * q + 1, :, lanes]
        low, high = (
            fold[q, h, pl.ds(0, 16, stride=2), :] + fold[q, h, pl.ds(1, 16, stride=2), :] for h in range(2)
        )
        diagonal = 6.0 + 0.125 * fold_lanes(low, high)
        db[q, :, :] = diagonal
        wb[q + 4, pl.ds(8, 16), :] = OMEGA / diagonal
        return 0

    lax.fori_loop(0, 4, screen_middle, 0, unroll=True)
    start(middle_w)

    for h in range(2):
        foldb[h, :, :] = (db[2 * h, :, :] - 6.0) + (db[2 * h + 1, :, :] - 6.0)
    low, high = (foldb[h, pl.ds(0, 8, stride=2), :] + foldb[h, pl.ds(1, 8, stride=2), :] for h in range(2))
    coarse_d = 6.0 + 0.125 * fold_lanes(low, high)
    own_cols = pl.ds(pl.multiple_of(8 + 8 * n, 8), 8)
    gvw[2, 1, own_cols, :] = coarse_d

    def gather_copy(what, dx, k):
        other = lax.rem(n + k, N)
        target = lax.rem(i + dx + W, W)
        return pltpu.make_async_remote_copy(
            src_ref=gvw.at[2, what, own_cols, :], dst_ref=gvw.at[2 - dx, what, own_cols, :],
            send_sem=gather_send.at[0], recv_sem=gather_recv.at[0],
            device_id=(target, other), device_id_type=MESH,
        )

    def gather_wait(call):
        for sides_x, here in ((2, both_x), (1, jnp.logical_not(both_x))):
            rows = 2 * 8 * (N - 1 + sides_x * N)
            target = (lax.rem(i + 1, W), n)
            pl.when(here)(functools.partial(call, waiter(rows, gather_send.at[0], gather_recv.at[0], target)))

    def for_each(k, call):
        pl.when(k > 0)(functools.partial(call, 0))
        pl.when(has_low)(functools.partial(call, -1))
        pl.when(has_high)(functools.partial(call, 1))

    def gather_start(what, k, _):
        for_each(k, lambda dx: gather_copy(what, dx, k).start())
        return 0

    lax.fori_loop(0, N, functools.partial(gather_start, 1), 0)

    def fine_v2(a, count, r, _):
        centre, summed = fine_sum(va, r, a, count)
        for h in range(2):
            v2a[r, h, pl.ds(a, count), :] = (1.0 + KEEP) * centre[h] + wa[r, h, pl.ds(a, count), :] * summed[h]
        return 0

    def fine_down(a, count, q, _):
        cells = pl.ds(a - 8, count)
        sums = [fine_sum(v2a, 2 * q + k + 4, a, count) for k in range(2)]
        for h in range(2):
            lanes = pl.ds(128 * h, 128)
            rest = [
                f_in[2 * q + k, cells, lanes] - (6.0 + s_in[2 * q + k, cells, lanes]) * centre[h] + summed[h]
                for k, (centre, summed) in enumerate(sums)
            ]
            fold[q, h, cells, :] = rest[0] + rest[1]
        low, high = (
            fold[q, h, pl.ds(a - 8, count // 2, stride=2), :] + fold[q, h, pl.ds(a - 7, count // 2, stride=2), :]
            for h in range(2)
        )
        source = 0.5 * fold_lanes(low, high)
        fb[q, pl.ds((a - 8) // 2, count // 2), :] = source
        part = (q + 4, pl.ds(4 + a // 2, count // 2), slice(None))
        vb[part] = source * wb[part]
        return 0

    def fine_level(v2_a, v2_count, outer_a, outer_count, a, count):
        for r in (3, 12):
            fine_v2(outer_a, outer_count, r, 0)
        lax.fori_loop(4, 12, functools.partial(fine_v2, v2_a, v2_count), 0, unroll=True)
        lax.fori_loop(0, 4, functools.partial(fine_down, a, count), 0, unroll=True)

    receive(0)
    fine_level(7, 8, 8, 7, 8, 6)
    fine_level(33, 8, 33, 7, 34, 6)
    start(middle_v[:6])
    fine_level(15, 18, 15, 18, 14, 20)
    start(middle_v[6:])

    receive(2)
    for r in range(3, 9):
        centre, summed = middle_sum(vb, r, 4, 24)
        tb[r, pl.ds(4, 24), :] = (1.0 + KEEP) * centre + wb[r, pl.ds(4, 24), :] * summed
    for r in range(4):
        centre, summed = middle_sum(tb, r + 4, 8, 16)
        v2b[r + 4, pl.ds(8, 16), :] = centre
        rest = fb[r, :, :] - db[r, :, :] * centre + summed
        if r % 2 == 0:
            held = rest
        else:
            foldb[r // 2, :, :] = held + rest
    low, high = (foldb[h, pl.ds(0, 8, stride=2), :] + foldb[h, pl.ds(1, 8, stride=2), :] for h in range(2))
    gvw[2, 0, own_cols, :] = 0.5 * fold_lanes(low, high) * (OMEGA / coarse_d)

    lax.fori_loop(0, N, functools.partial(gather_start, 0), 0)
    start(middle_v2)
    gather_wait(lambda copies: copies.wait_recv())

    slab = pl.ds(8, cols)
    turned = [rolled(gvw[t, 0, slab, :], 64, 1) for t in (1, 2, 3)]
    for t in range(3):
        centre = gvw[t + 1, 0, slab, :]
        along_x = pair_x_sum(turned[max(t - 1, 0)], turned[t], turned[min(t + 1, 2)])
        along_y = gvw[t + 1, 0, pl.ds(7, cols), :] + gvw[t + 1, 0, pl.ds(9, cols), :]
        diagonal = gvw[t + 1, 1, slab, :]
        weight = jnp.where(diagonal > 0.0, OMEGA / diagonal, 0.0)
        t2[t, slab, :] = (1.0 + KEEP) * centre + weight * (along_x + along_y + z_sum(centre, 64))
    turned = [rolled(t2[t, slab, :], 64, 1) for t in range(3)]
    centre = t2[1, slab, :]
    gv2[2, slab, :] = centre
    diagonal = gvw[2, 1, slab, :]
    along_x = pair_x_sum(*turned)
    along_y = t2[1, pl.ds(7, cols), :] + t2[1, pl.ds(9, cols), :]
    rest = diagonal * (gvw[2, 0, slab, :] * (1.0 / OMEGA) - centre) + (along_x + along_y + z_sum(centre, 64))

    sizes = (common, invx, invy)
    part = tally.at[pl.ds(0, sum(int(np.prod(ref.shape)) // 128 for ref in sizes)), :]
    pltpu.make_async_copy(part, part, in_sem.at[2]).wait()
    along_z = dot(rest, common[pl.ds(0, 128), :])
    along_yz = dot(common[pl.ds(256, 4 * N), pl.ds(0, cols)], along_z)
    group = lanes_of(N) // 32
    mine = along_yz[0:N, :]
    for g in range(1, 4):
        mine = jnp.where(group == g, along_yz[g * N : (g + 1) * N, :], mine)
    modes[i, pl.ds(0, N), :] = mine
    modes[i, pl.ds(N, 1), :] = jnp.sum(diagonal - 6.0, axis=0, keepdims=True)

    def wide_copy(k):
        return pltpu.make_async_remote_copy(
            src_ref=modes.at[i], dst_ref=modes.at[i], send_sem=wide_send.at[0], recv_sem=wide_recv.at[0],
            device_id=(lax.rem(i + k, W), n), device_id_type=MESH,
        )

    def wide_start(k, _):
        wide_copy(k).start()
        return 0

    everyone = waiter((W - 1) * (N + 1), wide_send.at[0], wide_recv.at[0], (lax.rem(i + 1, W), n))

    lax.fori_loop(1, W, wide_start, 0)
    coarse_far_start()
    halo_sent()
    gather_wait(lambda copies: copies.wait_send())

    receive(1)
    lax.fori_loop(1, 15, functools.partial(fine_v2, 4, 40), 0, unroll=True)
    everyone.wait_recv()

    total = jnp.sum(modes[:, N, :], keepdims=True)
    mean = total * (1.0 / (2 * W * 8 * N * 64))
    shifted = common[pl.ds(256 + 4 * N, N), :] + mean
    sine_x, eigen_x = sine_table(W), sine_eigen(W)
    factor = (2.0 / (W + 1.0)) * (2.0 / (4 * N + 1.0)) * (2.0 / 33.0)
    half = W // 2
    even, odd = [], []
    for j in range(half):
        first, second = modes[j, pl.ds(0, N), :], modes[W - 1 - j, pl.ds(0, N), :]
        even.append(first + second)
        odd.append(first - second)
    found = [None] * 5
    for a in range(W):
        values = even if a % 2 == 0 else odd
        acc = None
        for j in range(half):
            term = values[j] * np.float32(sine_x[a, j])
            acc = term if acc is None else acc + term
        scaled = acc * np.float32(factor) / (shifted + np.float32(eigen_x[a]))
        for t in range(5):
            term = invx[t, pl.ds(a, 1), :] * scaled
            found[t] = term if found[t] is None else found[t] + term
    spread = dot(invy[:, pl.ds(0, N)], jnp.concatenate(found, axis=1))
    group = lanes_of(WINDOW) // 32
    parts = []
    for t in range(5):
        lanes = slice(128 * t, 128 * t + 128)
        part = spread[0:WINDOW, lanes]
        for g in range(1, 4):
            part = jnp.where(group == g, spread[g * WINDOW : (g + 1) * WINDOW, lanes], part)
        parts.append(part)
    correction = dot(jnp.concatenate(parts, axis=0), common[pl.ds(128, 128), :])

    far_wait(lambda copies: copies.wait_recv())
    u = [gv2[t, window, :] + correction[WINDOW * t : WINDOW * (t + 1), :] for t in range(5)]

    def pair_sweep(u, slots):
        turned = {t: rolled(u[t], 64, 1) for t in u}
        swept = {}
        for t in slots:
            along_x = pair_x_sum(turned.get(t - 1, turned[t]), turned[t], turned.get(t + 1, turned[t]))
            along_y = rolled(u[t], 1, 0) + rolled(u[t], -1, 0)
            diagonal = gvw[t, 1, window, :]
            weight = jnp.where(diagonal > 0.0, OMEGA / diagonal, 0.0)
            summed = along_x + along_y + z_sum(u[t], 64)
            swept[t] = KEEP * u[t] + gvw[t, 0, window, :] + weight * summed
        return swept

    u = pair_sweep(dict(enumerate(u)), range(5))
    u = pair_sweep(u, range(1, 4))

    for t in (1, 2, 3):
        u2[t - 1, :, :] = u[t]
    for t in range(3):
        halves = spread_lanes(u2[t, pl.ds(4, 16), :])
        for h in range(2):
            for k in range(2):
                r = 4 * t + 2 * h + k
                ub1[r, pl.ds(0, 16, stride=2), :] = halves[h]
                ub1[r, pl.ds(1, 16, stride=2), :] = halves[h]
    for r in range(12):
        ub1[r, :, :] = ub1[r, :, :] + v2b[r, :, :]

    def middle_sweep(src, dst, r):
        centre, summed = middle_sum(src, r, 4, 24)
        part = (r, pl.ds(4, 24), slice(None))
        dst[part] = KEEP * centre + vb[part] + wb[part] * summed

    for r in range(1, 11):
        middle_sweep(ub1, ub2, r)
    for r in range(2, 10):
        middle_sweep(ub2, ub1, r)

    def fine_spread(q, _):
        halves = spread_lanes(ub1[q + 2, pl.ds(4, 24), :])
        for k in range(2):
            r = 2 * q + k
            for h in range(2):
                ua[r, h, pl.ds(0, 24, stride=2), :] = halves[h]
                ua[r, h, pl.ds(1, 24, stride=2), :] = halves[h]
        for k in range(2):
            r = 2 * q + k
            for h in range(2):
                ua[r, h, :, :] = ua[r, h, :, :] + v2a[r, h, :, :]
        return 0

    lax.fori_loop(0, 8, fine_spread, 0, unroll=True)

    def fine_sweep(src, dst, r, _):
        centre, summed = fine_sum(src, r, 4, 40)
        for h in range(2):
            part = (r, h, pl.ds(4, 40), slice(None))
            dst[part] = KEEP * centre[h] + va[part] + wa[part] * summed[h]
        return 0

    lax.fori_loop(2, 14, functools.partial(fine_sweep, ua, ub), 0, unroll=True)
    lax.fori_loop(3, 13, functools.partial(fine_sweep, ub, ua), 0, unroll=True)

    def fine_end(r, _):
        centre, summed = fine_sum(ua, r + 4, 8, 32)
        for h in range(2):
            lanes = pl.ds(128 * h, 128)
            out_v[r, :, lanes] = centre[h]
            res_v[r, :, lanes] = f_in[r, :, lanes] - (6.0 + s_in[r, :, lanes]) * centre[h] + summed[h]
        return 0

    lax.fori_loop(0, 8, fine_end, 0, unroll=True)
    far_wait(lambda copies: copies.wait_send())
    everyone.wait_send()


def store_kernel(out_v, res_v, out_hbm, res_hbm, sem):
    copies = [
        pltpu.make_async_copy(src, dst, sem.at[k]) for k, (src, dst) in enumerate(((out_v, out_hbm), (res_v, res_hbm)))
    ]
    for copy in copies:
        copy.start()
    for copy in copies:
        copy.wait()


def solution(mesh):
    W, N = mesh.shape["wide"], mesh.shape["narrow"]
    common, invx, invy = tables(W, N)
    cols = 8 * N
    vmem = pltpu.VMEM
    dma = pltpu.SemaphoreType.DMA
    fine, middle = (16, 2, 48, 128), (12, 32, 128)
    scratch = [
        vmem((8, 32, 256), F32), vmem((8, 32, 256), F32),
        vmem(common.shape, F32), vmem((5, W, 128), F32), vmem((4 * WINDOW, 128), F32),
        vmem(fine, F32), vmem(fine, F32), vmem(fine, F32), vmem(fine, F32), vmem(fine, F32),
        vmem((4, 2, 32, 128), F32),
        vmem(middle, F32), vmem(middle, F32), vmem(middle, F32), vmem(middle, F32),
        vmem(middle, F32), vmem(middle, F32),
        vmem((4, 16, 128), F32), vmem((4, 16, 128), F32), vmem((2, 16, 128), F32),
        vmem((5, 2, cols + 16, 128), F32), vmem((5, cols + 16, 128), F32),
        vmem((3, cols + 16, 128), F32), vmem((3, WINDOW, 128), F32),
        vmem((W, N + 1, 128), F32), vmem((2048, 128), F32),
        dma((3,)), dma((1,)), dma((3,)), dma((1,)), dma((1,)), dma((1,)), dma((1,)), dma((1,)), dma((1,)),
    ]

    def per_device(divergence, screening):
        block = pltpu.VMEM((8, 32, 256), F32)
        results = pl.pallas_call(
            functools.partial(cycle_kernel, W, N),
            out_shape=(block, block),
            in_specs=[pl.BlockSpec(memory_space=pltpu.HBM)] * 5,
            out_specs=(pl.BlockSpec(memory_space=pltpu.VMEM),) * 2,
            scratch_shapes=scratch,
            compiler_params=pltpu.CompilerParams(
                collective_id=0, has_side_effects=True, vmem_limit_bytes=56 * 1024 * 1024
            ),
        )(divergence, screening, jnp.asarray(common), jnp.asarray(invx), jnp.asarray(invy))
        stored = jax.ShapeDtypeStruct((8, 32, 256), F32)
        anywhere = pl.BlockSpec(memory_space=pl.ANY)
        return pl.pallas_call(
            store_kernel,
            out_shape=(stored, stored),
            in_specs=[pl.BlockSpec(memory_space=pltpu.VMEM)] * 2,
            out_specs=(anywhere, anywhere),
            scratch_shapes=[dma((2,))],
            compiler_params=pltpu.CompilerParams(vmem_limit_bytes=4 * 1024 * 1024),
        )(*results)

    spec = P("wide", "narrow", None)
    return jax.shard_map(
        per_device, mesh=mesh, in_specs=(spec, spec), out_specs=(spec, spec), check_vma=False
    )
```

```python
import functools

import numpy as np
import jax
import jax.numpy as jnp
from jax import lax
from jax.experimental import pallas as pl
from jax.experimental.pallas import tpu as pltpu
from jax.sharding import PartitionSpec as P

MESH = pl.DeviceIdType.MESH
F32 = jnp.float32
OMEGA = 0.8
KEEP = 0.2
WINDOW = 24


def sine_table(count):
    ladder = np.arange(count, dtype=np.float64) + 1.0
    return np.sin(np.pi * ladder[:, None] * ladder[None, :] / (count + 1.0))


def sine_eigen(count):
    ladder = np.arange(count, dtype=np.float64) + 1.0
    return 2.0 - 2.0 * np.cos(np.pi * ladder / (count + 1.0))


def tables(wide, narrow):
    count_y, count_z = 4 * narrow, 32
    sine_x, sine_y, sine_z = sine_table(wide), sine_table(count_y), sine_table(count_z)
    to_modes = np.tile(np.repeat(sine_z.T, 2, axis=0), (2, 4))
    from_modes = np.tile(np.repeat(sine_z, 2, axis=1), (4, 2))
    rows_y = 0.5 * np.repeat(sine_y, 2, axis=1)
    rows_y = np.pad(rows_y, ((0, 0), (0, 128 - rows_y.shape[1])))
    eigen_y = sine_eigen(count_y).reshape(4, narrow)
    eigen = eigen_y.T[:, :, None] + sine_eigen(count_z)[None, None, :]
    eigen = eigen.reshape(narrow, 128)
    common = np.concatenate([to_modes, from_modes, rows_y, eigen], axis=0)
    inverse_x = np.pad(sine_x, ((2, 2), (0, 0)))
    inverse_x = np.repeat(inverse_x[:, :, None], 128, axis=2)
    fine_y = np.pad(np.repeat(sine_y, 2, axis=0), ((8, 8), (0, 0)))
    inverse_y = np.zeros((narrow, 4, WINDOW, 128))
    for n in range(narrow):
        for g in range(4):
            inverse_y[n, g, :, :narrow] = fine_y[8 * n : 8 * n + WINDOW, g * narrow : (g + 1) * narrow]
    inverse_y = inverse_y.reshape(narrow, 4 * WINDOW, 128)
    return [a.astype(np.float32) for a in (common, inverse_x, inverse_y)]


def rolled(value, shift, axis):
    return pltpu.roll(value, shift % value.shape[axis], axis)


def lanes_of(rows):
    return lax.broadcasted_iota(jnp.int32, (rows, 128), 1)


def z_sum_halves(low, high):
    lane = lanes_of(low.shape[0])
    up_low, up_high = rolled(low, -1, 1), rolled(high, -1, 1)
    down_low, down_high = rolled(low, 1, 1), rolled(high, 1, 1)
    last, first = lane == 127, lane == 0
    sum_low = jnp.where(last, up_high, up_low) + jnp.where(first, 0.0, down_low)
    sum_high = jnp.where(last, 0.0, up_high) + jnp.where(first, down_low, down_high)
    return sum_low, sum_high


def z_sum(value, period):
    lane = lanes_of(value.shape[0]) % period
    up = jnp.where(lane == period - 1, 0.0, rolled(value, -1, 1))
    return up + jnp.where(lane == 0, 0.0, rolled(value, 1, 1))


def fine_sum(ref, r, a, n):
    centre = [ref[r, h, pl.ds(a, n), :] for h in range(2)]
    along_z = z_sum_halves(*centre)
    summed = []
    for h in range(2):
        along_x = ref[r - 1, h, pl.ds(a, n), :] + ref[r + 1, h, pl.ds(a, n), :]
        along_y = ref[r, h, pl.ds(a - 1, n), :] + ref[r, h, pl.ds(a + 1, n), :]
        summed.append(along_x + along_y + along_z[h])
    return centre, summed


def middle_sum(ref, r, a, n):
    centre = ref[r, pl.ds(a, n), :]
    along_x = ref[r - 1, pl.ds(a, n), :] + ref[r + 1, pl.ds(a, n), :]
    along_y = ref[r, pl.ds(a - 1, n), :] + ref[r, pl.ds(a + 1, n), :]
    return centre, along_x + along_y + z_sum(centre, 128)


def pair_x_sum(before, here, after):
    return here + jnp.where(lanes_of(here.shape[0]) < 64, before, after)


def fold_lanes(low, high):
    rows = low.shape[0]
    lane = lanes_of(rows)
    index = (lane * 2) % 128
    low = jnp.take_along_axis(low + rolled(low, -1, 1), index, axis=1)
    high = jnp.take_along_axis(high + rolled(high, -1, 1), index, axis=1)
    return jnp.where(lane < 64, low, high)


def spread_lanes(value):
    lane = lanes_of(value.shape[0])
    index = lane // 2
    return jnp.take_along_axis(value, index, axis=1), jnp.take_along_axis(value, index + 64, axis=1)


def dot(a, b):
    return jnp.dot(a, b, precision=lax.Precision.HIGHEST, preferred_element_type=F32)


def cycle_kernel(
    W, N,
    f_hbm, s_hbm, common_hbm, invx_hbm, invy_hbm,
    out_v, res_v,
    f_in, s_in, common, invx, invy,
    va, wa, v2a, ua, ub, fold,
    vb, wb, v2b, tb, ub1, ub2, fb, db, foldb,
    gvw, gv2, t2, u2,
    modes, tally,
    in_sem, send_sem, recv_sem, far_send, far_recv, gather_send, gather_recv, wide_send, wide_recv,
):
    i = lax.axis_index("wide")
    n = lax.axis_index("narrow")

    loads = [
        pltpu.make_async_copy(src, dst, in_sem.at[min(k, 2)])
        for k, (src, dst) in enumerate(
            (
                (s_hbm, s_in),
                (f_hbm, f_in),
                (common_hbm, common),
                (invx_hbm.at[pl.ds(i, 5)], invx),
                (invy_hbm.at[n], invy),
            )
        )
    ]
    barrier = pltpu.get_barrier_semaphore()

    def greet(wide_id, narrow_id):
        pl.semaphore_signal(barrier, inc=1, device_id=(wide_id, narrow_id), device_id_type=MESH)

    has_low, has_high = i > 0, i < W - 1

    def there(dx, dy):
        terms = []
        if dx > 0:
            terms.append(i < W - dx)
        if dx < 0:
            terms.append(i >= -dx)
        if dy > 0:
            terms.append(n < N - dy)
        if dy < 0:
            terms.append(n >= -dy)
        return functools.reduce(jnp.logical_and, terms)

    def flipped(index, mask):
        result, bit = index, 1
        while bit <= mask:
            if mask & bit:
                result = result + bit * (1 - 2 * lax.rem(lax.div(index, bit), 2))
            bit *= 2
        return result

    far_columns = sorted(range(1, N), key=lambda m: (m // 4, min(m % 4, 4 - m % 4), m), reverse=True)
    far_rows = sorted(range(1, W), key=lambda m: (m // 8 + min(m // 2 % 4, 4 - m // 2 % 4), m), reverse=True)
    for m in far_columns:
        other = flipped(n, m)
        pl.when(has_low)(functools.partial(greet, i - 1, other))
        pl.when(has_high)(functools.partial(greet, i + 1, other))
        greet(i, other)
    for m in far_rows:
        greet(flipped(i, m), n)

    for load in loads:
        load.start()

    sides = (-1, 1)
    corners = [(dx, dy) for dx in sides for dy in sides]

    def zero(ref, *index):
        shape = ref.at[index].shape if index else ref.shape
        ref[index if index else ...] = jnp.zeros(shape, F32)

    all_ = slice(None)

    @pl.when(i == 0)
    def _():
        for ref in (va, wa, v2a):
            zero(ref, pl.ds(0, 4))
        for ref in (vb, wb, v2b):
            zero(ref, pl.ds(0, 4))
        zero(gvw, pl.ds(0, 2))
        zero(gv2, pl.ds(0, 2))

    @pl.when(i == W - 1)
    def _():
        for ref in (va, wa, v2a):
            zero(ref, pl.ds(12, 4))
        for ref in (vb, wb, v2b):
            zero(ref, pl.ds(8, 4))
        zero(gvw, pl.ds(3, 2))
        zero(gv2, pl.ds(3, 2))

    @pl.when(i == 1)
    def _():
        zero(gvw, 0)
        zero(gv2, 0)

    @pl.when(i == W - 2)
    def _():
        zero(gvw, 4)
        zero(gv2, 4)

    @pl.when(n == 0)
    def _():
        for ref in (va, wa, v2a):
            zero(ref, all_, all_, pl.ds(0, 8))
        for ref in (vb, wb, v2b):
            zero(ref, all_, pl.ds(0, 8))

    @pl.when(n == N - 1)
    def _():
        for ref in (va, wa, v2a):
            zero(ref, all_, all_, pl.ds(40, 8))
        for ref in (vb, wb, v2b):
            zero(ref, all_, pl.ds(24, 8))

    cols = 8 * N
    zero(gvw, pl.ds(1, 3), all_, pl.ds(0, 8))
    zero(gvw, pl.ds(1, 3), all_, pl.ds(8 + cols, 8))
    zero(gv2, 2, pl.ds(0, 8))
    zero(gv2, 2, pl.ds(8 + cols, 8))
    zero(t2, all_, pl.ds(0, 8))
    zero(t2, all_, pl.ds(8 + cols, 8))

    loads[0].wait()
    loads[1].wait()

    def start_fine(r, _):
        for h in range(2):
            screen = s_in[r, :, pl.ds(128 * h, 128)]
            weight = OMEGA / (6.0 + screen)
            wa[r + 4, h, pl.ds(8, 32), :] = weight
            va[r + 4, h, pl.ds(8, 32), :] = f_in[r, :, pl.ds(128 * h, 128)] * weight
        return 0

    lax.fori_loop(0, 8, start_fine, 0, unroll=True)

    rows_of = {}
    both_x, both_y = jnp.logical_and(has_low, has_high), jnp.logical_and(n > 0, n < N - 1)

    def by_place(call):
        for sides_x in (1, 2):
            for sides_y in (1, 2):
                here_x = both_x if sides_x == 2 else jnp.logical_not(both_x)
                here_y = both_y if sides_y == 2 else jnp.logical_not(both_y)
                pl.when(jnp.logical_and(here_x, here_y))(functools.partial(call, sides_x, sides_y))

    def waiter(rows, send, recv, to):
        part = tally.at[pl.ds(0, rows), :]
        return pltpu.make_async_remote_copy(
            src_ref=part, dst_ref=part, send_sem=send, recv_sem=recv, device_id=to, device_id_type=MESH
        )

    def beside(dx, dy):
        return lax.rem(i + dx + W, W), lax.rem(n + dy + N, N)

    def span(step, first, size, depths):
        if step == 0:
            return pl.ds(first, size), pl.ds(first, size)
        low, high = depths
        count = high - low + 1
        if step > 0:
            return pl.ds(first + size - high, count), pl.ds(first - high, count)
        return pl.ds(first + low - 1, count), pl.ds(first + size + low - 1, count)

    def exchange(family, src, dst, dx, dy):
        kind = (family, dx != 0, dy != 0)
        if dx >= 0 and dy >= 0:
            rows_of[kind] = rows_of.get(kind, 0) + int(np.prod(src.shape)) // 128
        copy = pltpu.make_async_remote_copy(
            src_ref=src, dst_ref=dst, send_sem=send_sem.at[0], recv_sem=recv_sem.at[family],
            device_id=beside(dx, dy), device_id_type=MESH,
        )
        return copy, there(dx, dy)

    def halo_waiter(families, sides_x, sides_y):
        rows = sum(
            sides_x * rows_of[family, True, False]
            + sides_y * rows_of[family, False, True]
            + sides_x * sides_y * rows_of[family, True, True]
            for family in families
        )
        return waiter(rows, send_sem.at[0], recv_sem.at[families[0]], (lax.rem(i + 1, W), n))

    def fine_piece(family, ref, dx, dy, depth_x=None, depth_y=None):
        src_x, dst_x = span(dx, 4, 8, depth_x)
        src_y, dst_y = span(dy, 8, 32, depth_y)
        return exchange(family, ref.at[src_x, :, src_y, :], ref.at[dst_x, :, dst_y, :], dx, dy)

    def middle_piece(family, ref, dx, dy, depth_x=None, depth_y=None):
        src_x, dst_x = span(dx, 4, 4, depth_x)
        src_y, dst_y = span(dy, 8, 16, depth_y)
        return exchange(family, ref.at[src_x, src_y, :], ref.at[dst_x, dst_y, :], dx, dy)

    def start(pieces):
        for copy, to in pieces:
            pl.when(to)(copy.start)

    def receive(family):
        by_place(lambda sides_x, sides_y: halo_waiter([family], sides_x, sides_y).wait_recv())

    def halo_sent():
        by_place(lambda sides_x, sides_y: halo_waiter(range(3), sides_x, sides_y).wait_send())

    fine_near = (
        [fine_piece(0, va, 0, d, None, (1, 2)) for d in sides]
        + [fine_piece(0, wa, 0, d, None, (1, 1)) for d in sides]
        + [fine_piece(0, va, dx, dy, (1, 1), (1, 1)) for dx, dy in corners]
        + [fine_piece(0, va, d, 0, (1, 2)) for d in sides]
        + [fine_piece(0, wa, d, 0, (1, 1)) for d in sides]
    )
    fine_far = (
        [fine_piece(1, v2a, 0, d, None, (2, 3)) for d in sides]
        + [fine_piece(1, wa, 0, d, None, (2, 2)) for d in sides]
        + [fine_piece(1, v2a, dx, dy, (1, 1), (1, 2)) for dx, dy in corners]
        + [fine_piece(1, v2a, dx, dy, (2, 2), (1, 1)) for dx, dy in corners]
        + [fine_piece(1, wa, dx, dy, (1, 1), (1, 1)) for dx, dy in corners]
        + [fine_piece(1, v2a, d, 0, (2, 3)) for d in sides]
        + [fine_piece(1, wa, d, 0, (2, 2)) for d in sides]
    )

    def middle_pieces(family, ref, depth, corner):
        return (
            [middle_piece(family, ref, 0, d, None, (1, depth)) for d in sides]
            + [middle_piece(family, ref, dx, dy, (1, corner), (1, corner)) for dx, dy in corners]
            + [middle_piece(family, ref, d, 0, (1, depth)) for d in sides]
        )

    middle_w = middle_pieces(2, wb, 3, 2)
    middle_v = middle_pieces(2, vb, 3, 2)
    middle_v2 = middle_pieces(1, v2b, 4, 3)

    window = pl.ds(pl.multiple_of(8 * n, 8), WINDOW)
    reach = (-2, -1, 1, 2)

    def coarse_far(d):
        args = dict(
            send_sem=far_send.at[0], recv_sem=far_recv.at[0], device_id=beside(d, 0), device_id_type=MESH
        )
        copies = [pltpu.make_async_remote_copy(src_ref=gv2.at[2, window, :], dst_ref=gv2.at[2 - d, window, :], **args)]
        if abs(d) == 2:
            copies.append(
                pltpu.make_async_remote_copy(
                    src_ref=gvw.at[2, :, window, :], dst_ref=gvw.at[2 - d, :, window, :], **args
                )
            )
        return copies

    def coarse_far_start():
        for d in reach:
            for copy in coarse_far(d):
                pl.when(there(d, 0))(copy.start)

    def far_wait(call):
        further = jnp.logical_and(i > 1, i < W - 2)
        cases = (
            (1, 1, jnp.logical_not(both_x)),
            (2, 1, jnp.logical_and(both_x, jnp.logical_not(further))),
            (2, 2, further),
        )
        for near, far, here in cases:
            rows = (near + 3 * far) * WINDOW
            pl.when(here)(functools.partial(call, waiter(rows, far_send.at[0], far_recv.at[0], beside(1, 0))))

    greeted = (W - 1) + (N - 1) * (1 + has_low.astype(jnp.int32) + has_high.astype(jnp.int32))
    pl.semaphore_wait(barrier, greeted)

    start(fine_near)

    def screen_middle(q, _):
        for h in range(2):
            lanes = pl.ds(128 * h, 128)
            fold[q, h, :, :] = s_in[2 * q, :, lanes] + s_in[2 * q + 1, :, lanes]
        low, high = (
            fold[q, h, pl.ds(0, 16, stride=2), :] + fold[q, h, pl.ds(1, 16, stride=2), :] for h in range(2)
        )
        diagonal = 6.0 + 0.125 * fold_lanes(low, high)
        db[q, :, :] = diagonal
        wb[q + 4, pl.ds(8, 16), :] = OMEGA / diagonal
        return 0

    lax.fori_loop(0, 4, screen_middle, 0, unroll=True)
    start(middle_w)

    for h in range(2):
        foldb[h, :, :] = (db[2 * h, :, :] - 6.0) + (db[2 * h + 1, :, :] - 6.0)
    low, high = (foldb[h, pl.ds(0, 8, stride=2), :] + foldb[h, pl.ds(1, 8, stride=2), :] for h in range(2))
    coarse_d = 6.0 + 0.125 * fold_lanes(low, high)
    own_cols = pl.ds(pl.multiple_of(8 + 8 * n, 8), 8)
    gvw[2, 1, own_cols, :] = coarse_d

    def gather_copy(what, dx, k):
        other = lax.rem(n + k, N)
        target = lax.rem(i + dx + W, W)
        return pltpu.make_async_remote_copy(
            src_ref=gvw.at[2, what, own_cols, :], dst_ref=gvw.at[2 - dx, what, own_cols, :],
            send_sem=gather_send.at[0], recv_sem=gather_recv.at[0],
            device_id=(target, other), device_id_type=MESH,
        )

    def gather_wait(call):
        for sides_x, here in ((2, both_x), (1, jnp.logical_not(both_x))):
            rows = 2 * 8 * (N - 1 + sides_x * N)
            target = (lax.rem(i + 1, W), n)
            pl.when(here)(functools.partial(call, waiter(rows, gather_send.at[0], gather_recv.at[0], target)))

    def for_each(k, call):
        pl.when(k > 0)(functools.partial(call, 0))
        pl.when(has_low)(functools.partial(call, -1))
        pl.when(has_high)(functools.partial(call, 1))

    def gather_start(what, k, _):
        for_each(k, lambda dx: gather_copy(what, dx, k).start())
        return 0


    def fine_v2(a, count, r, _):
        centre, summed = fine_sum(va, r, a, count)
        for h in range(2):
            v2a[r, h, pl.ds(a, count), :] = (1.0 + KEEP) * centre[h] + wa[r, h, pl.ds(a, count), :] * summed[h]
        return 0

    def fine_down(a, count, q, _):
        cells = pl.ds(a - 8, count)
        sums = [fine_sum(v2a, 2 * q + k + 4, a, count) for k in range(2)]
        for h in range(2):
            lanes = pl.ds(128 * h, 128)
            rest = [
                f_in[2 * q + k, cells, lanes] - (6.0 + s_in[2 * q + k, cells, lanes]) * centre[h] + summed[h]
                for k, (centre, summed) in enumerate(sums)
            ]
            fold[q, h, cells, :] = rest[0] + rest[1]
        low, high = (
            fold[q, h, pl.ds(a - 8, count // 2, stride=2), :] + fold[q, h, pl.ds(a - 7, count // 2, stride=2), :]
            for h in range(2)
        )
        source = 0.5 * fold_lanes(low, high)
        fb[q, pl.ds((a - 8) // 2, count // 2), :] = source
        part = (q + 4, pl.ds(4 + a // 2, count // 2), slice(None))
        vb[part] = source * wb[part]
        return 0

    def fine_level(v2_a, v2_count, outer_a, outer_count, a, count):
        for r in (3, 12):
            fine_v2(outer_a, outer_count, r, 0)
        lax.fori_loop(4, 12, functools.partial(fine_v2, v2_a, v2_count), 0, unroll=True)
        lax.fori_loop(0, 4, functools.partial(fine_down, a, count), 0, unroll=True)

    receive(0)
    fine_level(7, 8, 8, 7, 8, 6)
    fine_level(33, 8, 33, 7, 34, 6)
    start(middle_v[:6])
    fine_level(15, 18, 15, 18, 14, 20)
    start(middle_v[6:])
    start(fine_far)
    lax.fori_loop(0, N, functools.partial(gather_start, 1), 0)

    receive(2)
    for r in range(3, 9):
        centre, summed = middle_sum(vb, r, 4, 24)
        tb[r, pl.ds(4, 24), :] = (1.0 + KEEP) * centre + wb[r, pl.ds(4, 24), :] * summed
    for r in range(4):
        centre, summed = middle_sum(tb, r + 4, 8, 16)
        v2b[r + 4, pl.ds(8, 16), :] = centre
        rest = fb[r, :, :] - db[r, :, :] * centre + summed
        if r % 2 == 0:
            held = rest
        else:
            foldb[r // 2, :, :] = held + rest
    low, high = (foldb[h, pl.ds(0, 8, stride=2), :] + foldb[h, pl.ds(1, 8, stride=2), :] for h in range(2))
    gvw[2, 0, own_cols, :] = 0.5 * fold_lanes(low, high) * (OMEGA / coarse_d)

    lax.fori_loop(0, N, functools.partial(gather_start, 0), 0)
    start(middle_v2)
    gather_wait(lambda copies: copies.wait_recv())

    slab = pl.ds(8, cols)
    turned = [rolled(gvw[t, 0, slab, :], 64, 1) for t in (1, 2, 3)]
    for t in range(3):
        centre = gvw[t + 1, 0, slab, :]
        along_x = pair_x_sum(turned[max(t - 1, 0)], turned[t], turned[min(t + 1, 2)])
        along_y = gvw[t + 1, 0, pl.ds(7, cols), :] + gvw[t + 1, 0, pl.ds(9, cols), :]
        diagonal = gvw[t + 1, 1, slab, :]
        weight = jnp.where(diagonal > 0.0, OMEGA / diagonal, 0.0)
        t2[t, slab, :] = (1.0 + KEEP) * centre + weight * (along_x + along_y + z_sum(centre, 64))
    turned = [rolled(t2[t, slab, :], 64, 1) for t in range(3)]
    centre = t2[1, slab, :]
    gv2[2, slab, :] = centre
    diagonal = gvw[2, 1, slab, :]
    along_x = pair_x_sum(*turned)
    along_y = t2[1, pl.ds(7, cols), :] + t2[1, pl.ds(9, cols), :]
    rest = diagonal * (gvw[2, 0, slab, :] * (1.0 / OMEGA) - centre) + (along_x + along_y + z_sum(centre, 64))

    sizes = (common, invx, invy)
    part = tally.at[pl.ds(0, sum(int(np.prod(ref.shape)) // 128 for ref in sizes)), :]
    pltpu.make_async_copy(part, part, in_sem.at[2]).wait()
    along_z = dot(rest, common[pl.ds(0, 128), :])
    along_yz = dot(common[pl.ds(256, 4 * N), pl.ds(0, cols)], along_z)
    group = lanes_of(N) // 32
    mine = along_yz[0:N, :]
    for g in range(1, 4):
        mine = jnp.where(group == g, along_yz[g * N : (g + 1) * N, :], mine)
    modes[i, pl.ds(0, N), :] = mine
    modes[i, pl.ds(N, 1), :] = jnp.sum(diagonal - 6.0, axis=0, keepdims=True)

    def wide_copy(k):
        return pltpu.make_async_remote_copy(
            src_ref=modes.at[i], dst_ref=modes.at[i], send_sem=wide_send.at[0], recv_sem=wide_recv.at[0],
            device_id=(lax.rem(i + k, W), n), device_id_type=MESH,
        )

    def wide_start(k, _):
        wide_copy(k).start()
        return 0

    everyone = waiter((W - 1) * (N + 1), wide_send.at[0], wide_recv.at[0], (lax.rem(i + 1, W), n))

    lax.fori_loop(1, W, wide_start, 0)
    coarse_far_start()
    halo_sent()
    gather_wait(lambda copies: copies.wait_send())

    receive(1)
    everyone.wait_recv()

    total = jnp.sum(modes[:, N, :], keepdims=True)
    mean = total * (1.0 / (2 * W * 8 * N * 64))
    shifted = common[pl.ds(256 + 4 * N, N), :] + mean
    sine_x, eigen_x = sine_table(W), sine_eigen(W)
    factor = (2.0 / (W + 1.0)) * (2.0 / (4 * N + 1.0)) * (2.0 / 33.0)
    half = W // 2
    even, odd = [], []
    for j in range(half):
        first, second = modes[j, pl.ds(0, N), :], modes[W - 1 - j, pl.ds(0, N), :]
        even.append(first + second)
        odd.append(first - second)
    found = [None] * 5
    for a in range(W):
        values = even if a % 2 == 0 else odd
        acc = None
        for j in range(half):
            term = values[j] * np.float32(sine_x[a, j])
            acc = term if acc is None else acc + term
        scaled = acc * np.float32(factor) / (shifted + np.float32(eigen_x[a]))
        for t in range(5):
            term = invx[t, pl.ds(a, 1), :] * scaled
            found[t] = term if found[t] is None else found[t] + term
    spread = dot(invy[:, pl.ds(0, N)], jnp.concatenate(found, axis=1))
    group = lanes_of(WINDOW) // 32
    parts = []
    for t in range(5):
        lanes = slice(128 * t, 128 * t + 128)
        part = spread[0:WINDOW, lanes]
        for g in range(1, 4):
            part = jnp.where(group == g, spread[g * WINDOW : (g + 1) * WINDOW, lanes], part)
        parts.append(part)
    correction = dot(jnp.concatenate(parts, axis=0), common[pl.ds(128, 128), :])

    far_wait(lambda copies: copies.wait_recv())
    u = [gv2[t, window, :] + correction[WINDOW * t : WINDOW * (t + 1), :] for t in range(5)]

    def pair_sweep(u, slots):
        turned = {t: rolled(u[t], 64, 1) for t in u}
        swept = {}
        for t in slots:
            along_x = pair_x_sum(turned.get(t - 1, turned[t]), turned[t], turned.get(t + 1, turned[t]))
            along_y = rolled(u[t], 1, 0) + rolled(u[t], -1, 0)
            diagonal = gvw[t, 1, window, :]
            weight = jnp.where(diagonal > 0.0, OMEGA / diagonal, 0.0)
            summed = along_x + along_y + z_sum(u[t], 64)
            swept[t] = KEEP * u[t] + gvw[t, 0, window, :] + weight * summed
        return swept

    u = pair_sweep(dict(enumerate(u)), range(5))
    u = pair_sweep(u, range(1, 4))

    for t in (1, 2, 3):
        u2[t - 1, :, :] = u[t]
    for t in range(3):
        halves = spread_lanes(u2[t, pl.ds(4, 16), :])
        for h in range(2):
            for k in range(2):
                r = 4 * t + 2 * h + k
                ub1[r, pl.ds(0, 16, stride=2), :] = halves[h]
                ub1[r, pl.ds(1, 16, stride=2), :] = halves[h]
    for r in range(12):
        ub1[r, :, :] = ub1[r, :, :] + v2b[r, :, :]

    def middle_sweep(src, dst, r):
        centre, summed = middle_sum(src, r, 4, 24)
        part = (r, pl.ds(4, 24), slice(None))
        dst[part] = KEEP * centre + vb[part] + wb[part] * summed

    for r in range(1, 11):
        middle_sweep(ub1, ub2, r)
    for r in range(2, 10):
        middle_sweep(ub2, ub1, r)

    def fine_spread(q, _):
        halves = spread_lanes(ub1[q + 2, pl.ds(4, 24), :])
        for k in range(2):
            r = 2 * q + k
            for h in range(2):
                ua[r, h, pl.ds(0, 24, stride=2), :] = halves[h]
                ua[r, h, pl.ds(1, 24, stride=2), :] = halves[h]
        for k in range(2):
            r = 2 * q + k
            for h in range(2):
                ua[r, h, :, :] = ua[r, h, :, :] + v2a[r, h, :, :]
        return 0

    lax.fori_loop(0, 8, fine_spread, 0, unroll=True)

    def fine_sweep(src, dst, r, _):
        centre, summed = fine_sum(src, r, 4, 40)
        for h in range(2):
            part = (r, h, pl.ds(4, 40), slice(None))
            dst[part] = KEEP * centre[h] + va[part] + wa[part] * summed[h]
        return 0

    lax.fori_loop(2, 14, functools.partial(fine_sweep, ua, ub), 0, unroll=True)
    lax.fori_loop(3, 13, functools.partial(fine_sweep, ub, ua), 0, unroll=True)

    def fine_end(r, _):
        centre, summed = fine_sum(ua, r + 4, 8, 32)
        for h in range(2):
            lanes = pl.ds(128 * h, 128)
            out_v[r, :, lanes] = centre[h]
            res_v[r, :, lanes] = f_in[r, :, lanes] - (6.0 + s_in[r, :, lanes]) * centre[h] + summed[h]
        return 0

    lax.fori_loop(0, 8, fine_end, 0, unroll=True)
    far_wait(lambda copies: copies.wait_send())
    everyone.wait_send()


def store_kernel(out_v, res_v, out_hbm, res_hbm, sem):
    copies = [
        pltpu.make_async_copy(src, dst, sem.at[k]) for k, (src, dst) in enumerate(((out_v, out_hbm), (res_v, res_hbm)))
    ]
    for copy in copies:
        copy.start()
    for copy in copies:
        copy.wait()


def solution(mesh):
    W, N = mesh.shape["wide"], mesh.shape["narrow"]
    common, invx, invy = tables(W, N)
    cols = 8 * N
    vmem = pltpu.VMEM
    dma = pltpu.SemaphoreType.DMA
    fine, middle = (16, 2, 48, 128), (12, 32, 128)
    scratch = [
        vmem((8, 32, 256), F32), vmem((8, 32, 256), F32),
        vmem(common.shape, F32), vmem((5, W, 128), F32), vmem((4 * WINDOW, 128), F32),
        vmem(fine, F32), vmem(fine, F32), vmem(fine, F32), vmem(fine, F32), vmem(fine, F32),
        vmem((4, 2, 32, 128), F32),
        vmem(middle, F32), vmem(middle, F32), vmem(middle, F32), vmem(middle, F32),
        vmem(middle, F32), vmem(middle, F32),
        vmem((4, 16, 128), F32), vmem((4, 16, 128), F32), vmem((2, 16, 128), F32),
        vmem((5, 2, cols + 16, 128), F32), vmem((5, cols + 16, 128), F32),
        vmem((3, cols + 16, 128), F32), vmem((3, WINDOW, 128), F32),
        vmem((W, N + 1, 128), F32), vmem((2048, 128), F32),
        dma((3,)), dma((1,)), dma((3,)), dma((1,)), dma((1,)), dma((1,)), dma((1,)), dma((1,)), dma((1,)),
    ]

    def per_device(divergence, screening):
        block = pltpu.VMEM((8, 32, 256), F32)
        results = pl.pallas_call(
            functools.partial(cycle_kernel, W, N),
            out_shape=(block, block),
            in_specs=[pl.BlockSpec(memory_space=pltpu.HBM)] * 5,
            out_specs=(pl.BlockSpec(memory_space=pltpu.VMEM),) * 2,
            scratch_shapes=scratch,
            compiler_params=pltpu.CompilerParams(
                collective_id=0, has_side_effects=True, vmem_limit_bytes=56 * 1024 * 1024
            ),
        )(divergence, screening, jnp.asarray(common), jnp.asarray(invx), jnp.asarray(invy))
        stored = jax.ShapeDtypeStruct((8, 32, 256), F32)
        anywhere = pl.BlockSpec(memory_space=pl.ANY)
        return pl.pallas_call(
            store_kernel,
            out_shape=(stored, stored),
            in_specs=[pl.BlockSpec(memory_space=pltpu.VMEM)] * 2,
            out_specs=(anywhere, anywhere),
            scratch_shapes=[dma((2,))],
            compiler_params=pltpu.CompilerParams(vmem_limit_bytes=4 * 1024 * 1024),
        )(*results)

    spec = P("wide", "narrow", None)
    return jax.shard_map(
        per_device, mesh=mesh, in_specs=(spec, spec), out_specs=(spec, spec), check_vma=False
    )
```

```python
import functools

import numpy as np
import jax
import jax.numpy as jnp
from jax import lax
from jax.experimental import pallas as pl
from jax.experimental.pallas import tpu as pltpu
from jax.sharding import PartitionSpec as P

MESH = pl.DeviceIdType.MESH
F32 = jnp.float32
OMEGA = 0.8
KEEP = 0.2
WINDOW = 24


def sine_table(count):
    ladder = np.arange(count, dtype=np.float64) + 1.0
    return np.sin(np.pi * ladder[:, None] * ladder[None, :] / (count + 1.0))


def sine_eigen(count):
    ladder = np.arange(count, dtype=np.float64) + 1.0
    return 2.0 - 2.0 * np.cos(np.pi * ladder / (count + 1.0))


def tables(wide, narrow):
    count_y, count_z = 4 * narrow, 32
    sine_x, sine_y, sine_z = sine_table(wide), sine_table(count_y), sine_table(count_z)
    to_modes = np.tile(np.repeat(sine_z.T, 2, axis=0), (2, 4))
    from_modes = np.tile(np.repeat(sine_z, 2, axis=1), (4, 2))
    rows_y = 0.5 * np.repeat(sine_y, 2, axis=1)
    rows_y = np.pad(rows_y, ((0, 0), (0, 128 - rows_y.shape[1])))
    eigen_y = sine_eigen(count_y).reshape(4, narrow)
    eigen = eigen_y.T[:, :, None] + sine_eigen(count_z)[None, None, :]
    eigen = eigen.reshape(narrow, 128)
    common = np.concatenate([to_modes, from_modes, rows_y, eigen], axis=0)
    inverse_x = np.pad(sine_x, ((2, 2), (0, 0)))
    inverse_x = np.repeat(inverse_x[:, :, None], 128, axis=2)
    fine_y = np.pad(np.repeat(sine_y, 2, axis=0), ((8, 8), (0, 0)))
    inverse_y = np.zeros((narrow, 4, WINDOW, 128))
    for n in range(narrow):
        for g in range(4):
            inverse_y[n, g, :, :narrow] = fine_y[8 * n : 8 * n + WINDOW, g * narrow : (g + 1) * narrow]
    inverse_y = inverse_y.reshape(narrow, 4 * WINDOW, 128)
    return [a.astype(np.float32) for a in (common, inverse_x, inverse_y)]


def rolled(value, shift, axis):
    return pltpu.roll(value, shift % value.shape[axis], axis)


def lanes_of(rows):
    return lax.broadcasted_iota(jnp.int32, (rows, 128), 1)


def z_sum_halves(low, high):
    lane = lanes_of(low.shape[0])
    up_low, up_high = rolled(low, -1, 1), rolled(high, -1, 1)
    down_low, down_high = rolled(low, 1, 1), rolled(high, 1, 1)
    last, first = lane == 127, lane == 0
    sum_low = jnp.where(last, up_high, up_low) + jnp.where(first, 0.0, down_low)
    sum_high = jnp.where(last, 0.0, up_high) + jnp.where(first, down_low, down_high)
    return sum_low, sum_high


def z_sum(value, period):
    lane = lanes_of(value.shape[0]) % period
    up = jnp.where(lane == period - 1, 0.0, rolled(value, -1, 1))
    return up + jnp.where(lane == 0, 0.0, rolled(value, 1, 1))


def fine_sum(ref, r, a, n):
    centre = [ref[r, h, pl.ds(a, n), :] for h in range(2)]
    along_z = z_sum_halves(*centre)
    summed = []
    for h in range(2):
        along_x = ref[r - 1, h, pl.ds(a, n), :] + ref[r + 1, h, pl.ds(a, n), :]
        along_y = ref[r, h, pl.ds(a - 1, n), :] + ref[r, h, pl.ds(a + 1, n), :]
        summed.append(along_x + along_y + along_z[h])
    return centre, summed


def middle_sum(ref, r, a, n):
    centre = ref[r, pl.ds(a, n), :]
    along_x = ref[r - 1, pl.ds(a, n), :] + ref[r + 1, pl.ds(a, n), :]
    along_y = ref[r, pl.ds(a - 1, n), :] + ref[r, pl.ds(a + 1, n), :]
    return centre, along_x + along_y + z_sum(centre, 128)


def pair_x_sum(before, here, after):
    return here + jnp.where(lanes_of(here.shape[0]) < 64, before, after)


def fold_lanes(low, high):
    rows = low.shape[0]
    lane = lanes_of(rows)
    index = (lane * 2) % 128
    low = jnp.take_along_axis(low + rolled(low, -1, 1), index, axis=1)
    high = jnp.take_along_axis(high + rolled(high, -1, 1), index, axis=1)
    return jnp.where(lane < 64, low, high)


def spread_lanes(value):
    lane = lanes_of(value.shape[0])
    index = lane // 2
    return jnp.take_along_axis(value, index, axis=1), jnp.take_along_axis(value, index + 64, axis=1)


def dot(a, b):
    return jnp.dot(a, b, precision=lax.Precision.HIGHEST, preferred_element_type=F32)


def cycle_kernel(
    W, N,
    f_hbm, s_hbm, common_hbm, invx_hbm, invy_hbm,
    out_v, res_v,
    f_in, s_in, common, invx, invy,
    va, wa, v2a, ua, ub, fold,
    vb, wb, v2b, tb, ub1, ub2, fb, db, foldb,
    gvw, gv2, t2, u2,
    modes, tally,
    in_sem, send_sem, recv_sem, far_send, far_recv, gather_send, gather_recv, wide_send, wide_recv,
):
    i = lax.axis_index("wide")
    n = lax.axis_index("narrow")

    loads = [
        pltpu.make_async_copy(src, dst, in_sem.at[min(k, 2)])
        for k, (src, dst) in enumerate(
            (
                (s_hbm, s_in.at[:, pl.ds(0, 32), :]),
                (f_hbm, f_in.at[:, pl.ds(0, 32), :]),
                (common_hbm, common),
                (invx_hbm.at[pl.ds(i, 5)], invx),
                (invy_hbm.at[n], invy),
            )
        )
    ]
    barrier = pltpu.get_barrier_semaphore()

    def greet(wide_id, narrow_id):
        pl.semaphore_signal(barrier, inc=1, device_id=(wide_id, narrow_id), device_id_type=MESH)

    has_low, has_high = i > 0, i < W - 1

    def there(dx, dy):
        terms = []
        if dx > 0:
            terms.append(i < W - dx)
        if dx < 0:
            terms.append(i >= -dx)
        if dy > 0:
            terms.append(n < N - dy)
        if dy < 0:
            terms.append(n >= -dy)
        return functools.reduce(jnp.logical_and, terms)

    def flipped(index, mask):
        result, bit = index, 1
        while bit <= mask:
            if mask & bit:
                result = result + bit * (1 - 2 * lax.rem(lax.div(index, bit), 2))
            bit *= 2
        return result

    far_columns = sorted(range(1, N), key=lambda m: (m // 4, min(m % 4, 4 - m % 4), m), reverse=True)
    far_rows = sorted(range(1, W), key=lambda m: (m // 8 + min(m // 2 % 4, 4 - m // 2 % 4), m), reverse=True)
    for m in far_columns:
        other = flipped(n, m)
        pl.when(has_low)(functools.partial(greet, i - 1, other))
        pl.when(has_high)(functools.partial(greet, i + 1, other))
        greet(i, other)
    for m in far_rows:
        greet(flipped(i, m), n)

    for load in loads:
        load.start()

    sides = (-1, 1)
    corners = [(dx, dy) for dx in sides for dy in sides]

    def zero(ref, *index):
        shape = ref.at[index].shape if index else ref.shape
        ref[index if index else ...] = jnp.zeros(shape, F32)

    all_ = slice(None)

    @pl.when(i == 0)
    def _():
        for ref in (va, wa, v2a):
            zero(ref, pl.ds(0, 4))
        for ref in (vb, wb, v2b):
            zero(ref, pl.ds(0, 4))
        zero(gvw, pl.ds(0, 2))
        zero(gv2, pl.ds(0, 2))

    @pl.when(i == W - 1)
    def _():
        for ref in (va, wa, v2a):
            zero(ref, pl.ds(12, 4))
        for ref in (vb, wb, v2b):
            zero(ref, pl.ds(8, 4))
        zero(gvw, pl.ds(3, 2))
        zero(gv2, pl.ds(3, 2))

    @pl.when(i == 1)
    def _():
        zero(gvw, 0)
        zero(gv2, 0)

    @pl.when(i == W - 2)
    def _():
        zero(gvw, 4)
        zero(gv2, 4)

    @pl.when(n == 0)
    def _():
        for ref in (va, wa, v2a):
            zero(ref, all_, all_, pl.ds(0, 8))
        for ref in (vb, wb, v2b):
            zero(ref, all_, pl.ds(0, 8))

    @pl.when(n == N - 1)
    def _():
        for ref in (va, wa, v2a):
            zero(ref, all_, all_, pl.ds(40, 8))
        for ref in (vb, wb, v2b):
            zero(ref, all_, pl.ds(24, 8))

    cols = 8 * N
    zero(gvw, pl.ds(1, 3), all_, pl.ds(0, 8))
    zero(gvw, pl.ds(1, 3), all_, pl.ds(8 + cols, 8))
    zero(gv2, 2, pl.ds(0, 8))
    zero(gv2, 2, pl.ds(8 + cols, 8))
    zero(t2, all_, pl.ds(0, 8))
    zero(t2, all_, pl.ds(8 + cols, 8))

    loads[0].wait()
    loads[1].wait()

    def start_fine(r, _):
        for h in range(2):
            screen = s_in[r, pl.ds(0, 32), pl.ds(128 * h, 128)]
            weight = OMEGA / (6.0 + screen)
            wa[r + 4, h, pl.ds(8, 32), :] = weight
            va[r + 4, h, pl.ds(8, 32), :] = f_in[r, pl.ds(0, 32), pl.ds(128 * h, 128)] * weight
        return 0

    lax.fori_loop(0, 8, start_fine, 0, unroll=True)

    rows_of = {}
    both_x, both_y = jnp.logical_and(has_low, has_high), jnp.logical_and(n > 0, n < N - 1)

    def by_place(call):
        for sides_x in (1, 2):
            for sides_y in (1, 2):
                here_x = both_x if sides_x == 2 else jnp.logical_not(both_x)
                here_y = both_y if sides_y == 2 else jnp.logical_not(both_y)
                pl.when(jnp.logical_and(here_x, here_y))(functools.partial(call, sides_x, sides_y))

    def waiter(rows, send, recv, to):
        part = tally.at[pl.ds(0, rows), :]
        return pltpu.make_async_remote_copy(
            src_ref=part, dst_ref=part, send_sem=send, recv_sem=recv, device_id=to, device_id_type=MESH
        )

    def beside(dx, dy):
        return lax.rem(i + dx + W, W), lax.rem(n + dy + N, N)

    def span(step, first, size, depths):
        if step == 0:
            return pl.ds(first, size), pl.ds(first, size)
        low, high = depths
        count = high - low + 1
        if step > 0:
            return pl.ds(first + size - high, count), pl.ds(first - high, count)
        return pl.ds(first + low - 1, count), pl.ds(first + size + low - 1, count)

    def exchange(family, src, dst, dx, dy):
        kind = (family, dx != 0, dy != 0)
        if dx >= 0 and dy >= 0:
            rows_of[kind] = rows_of.get(kind, 0) + int(np.prod(src.shape)) // 128
        copy = pltpu.make_async_remote_copy(
            src_ref=src, dst_ref=dst, send_sem=send_sem.at[0], recv_sem=recv_sem.at[family],
            device_id=beside(dx, dy), device_id_type=MESH,
        )
        return copy, there(dx, dy)

    def halo_waiter(families, sides_x, sides_y):
        rows = sum(
            sides_x * rows_of[family, True, False]
            + sides_y * rows_of[family, False, True]
            + sides_x * sides_y * rows_of[family, True, True]
            for family in families
        )
        return waiter(rows, send_sem.at[0], recv_sem.at[families[0]], (lax.rem(i + 1, W), n))

    def fine_piece(family, ref, dx, dy, depth_x=None, depth_y=None):
        src_x, dst_x = span(dx, 4, 8, depth_x)
        src_y, dst_y = span(dy, 8, 32, depth_y)
        return exchange(family, ref.at[src_x, :, src_y, :], ref.at[dst_x, :, dst_y, :], dx, dy)

    def middle_piece(family, ref, dx, dy, depth_x=None, depth_y=None):
        src_x, dst_x = span(dx, 4, 4, depth_x)
        src_y, dst_y = span(dy, 8, 16, depth_y)
        return exchange(family, ref.at[src_x, src_y, :], ref.at[dst_x, dst_y, :], dx, dy)

    def start(pieces):
        for copy, to in pieces:
            pl.when(to)(copy.start)

    def receive(family):
        by_place(lambda sides_x, sides_y: halo_waiter([family], sides_x, sides_y).wait_recv())

    def halo_sent():
        by_place(lambda sides_x, sides_y: halo_waiter(range(3), sides_x, sides_y).wait_send())

    fine_near = (
        [fine_piece(0, va, 0, d, None, (1, 2)) for d in sides]
        + [fine_piece(0, wa, 0, d, None, (1, 1)) for d in sides]
        + [fine_piece(0, va, dx, dy, (1, 1), (1, 1)) for dx, dy in corners]
        + [fine_piece(0, va, d, 0, (1, 2)) for d in sides]
        + [fine_piece(0, wa, d, 0, (1, 1)) for d in sides]
    )
    fine_far = (
        [fine_piece(1, v2a, 0, d, None, (2, 3)) for d in sides]
        + [fine_piece(1, wa, 0, d, None, (2, 2)) for d in sides]
        + [fine_piece(1, v2a, dx, dy, (1, 1), (1, 2)) for dx, dy in corners]
        + [fine_piece(1, v2a, dx, dy, (2, 2), (1, 1)) for dx, dy in corners]
        + [fine_piece(1, wa, dx, dy, (1, 1), (1, 1)) for dx, dy in corners]
        + [fine_piece(1, v2a, d, 0, (2, 3)) for d in sides]
        + [fine_piece(1, wa, d, 0, (2, 2)) for d in sides]
    )

    def middle_pieces(family, ref, depth, corner):
        return (
            [middle_piece(family, ref, 0, d, None, (1, depth)) for d in sides]
            + [middle_piece(family, ref, dx, dy, (1, corner), (1, corner)) for dx, dy in corners]
            + [middle_piece(family, ref, d, 0, (1, depth)) for d in sides]
        )

    middle_w = middle_pieces(2, wb, 3, 2)
    middle_v = middle_pieces(2, vb, 3, 2)
    middle_v2 = middle_pieces(1, v2b, 4, 3)

    window = pl.ds(pl.multiple_of(8 * n, 8), WINDOW)
    reach = (-2, -1, 1, 2)

    def coarse_far(d):
        args = dict(
            send_sem=far_send.at[0], recv_sem=far_recv.at[0], device_id=beside(d, 0), device_id_type=MESH
        )
        copies = [pltpu.make_async_remote_copy(src_ref=gv2.at[2, window, :], dst_ref=gv2.at[2 - d, window, :], **args)]
        if abs(d) == 2:
            copies.append(
                pltpu.make_async_remote_copy(
                    src_ref=gvw.at[2, :, window, :], dst_ref=gvw.at[2 - d, :, window, :], **args
                )
            )
        return copies

    def coarse_far_start():
        for d in reach:
            for copy in coarse_far(d):
                pl.when(there(d, 0))(copy.start)

    def far_wait(call):
        further = jnp.logical_and(i > 1, i < W - 2)
        cases = (
            (1, 1, jnp.logical_not(both_x)),
            (2, 1, jnp.logical_and(both_x, jnp.logical_not(further))),
            (2, 2, further),
        )
        for near, far, here in cases:
            rows = (near + 3 * far) * WINDOW
            pl.when(here)(functools.partial(call, waiter(rows, far_send.at[0], far_recv.at[0], beside(1, 0))))

    greeted = (W - 1) + (N - 1) * (1 + has_low.astype(jnp.int32) + has_high.astype(jnp.int32))
    pl.semaphore_wait(barrier, greeted)

    start(fine_near)

    def screen_middle(q, _):
        for h in range(2):
            lanes = pl.ds(128 * h, 128)
            fold[q, h, pl.ds(0, 32), :] = s_in[2 * q, pl.ds(0, 32), lanes] + s_in[2 * q + 1, pl.ds(0, 32), lanes]
        low, high = (
            fold[q, h, pl.ds(0, 16, stride=2), :] + fold[q, h, pl.ds(1, 16, stride=2), :] for h in range(2)
        )
        diagonal = 6.0 + 0.125 * fold_lanes(low, high)
        db[q, :, :] = diagonal
        wb[q + 4, pl.ds(8, 16), :] = OMEGA / diagonal
        return 0

    lax.fori_loop(0, 4, screen_middle, 0, unroll=True)
    start(middle_w)

    for h in range(2):
        foldb[h, :, :] = (db[2 * h, :, :] - 6.0) + (db[2 * h + 1, :, :] - 6.0)
    low, high = (foldb[h, pl.ds(0, 8, stride=2), :] + foldb[h, pl.ds(1, 8, stride=2), :] for h in range(2))
    coarse_d = 6.0 + 0.125 * fold_lanes(low, high)
    own_cols = pl.ds(pl.multiple_of(8 + 8 * n, 8), 8)
    gvw[2, 1, own_cols, :] = coarse_d

    def gather_copy(what, dx, k):
        other = lax.rem(n + k, N)
        target = lax.rem(i + dx + W, W)
        return pltpu.make_async_remote_copy(
            src_ref=gvw.at[2, what, own_cols, :], dst_ref=gvw.at[2 - dx, what, own_cols, :],
            send_sem=gather_send.at[0], recv_sem=gather_recv.at[0],
            device_id=(target, other), device_id_type=MESH,
        )

    def gather_wait(call):
        for sides_x, here in ((2, both_x), (1, jnp.logical_not(both_x))):
            rows = 2 * 8 * (N - 1 + sides_x * N)
            target = (lax.rem(i + 1, W), n)
            pl.when(here)(functools.partial(call, waiter(rows, gather_send.at[0], gather_recv.at[0], target)))

    def for_each(k, call):
        pl.when(k > 0)(functools.partial(call, 0))
        pl.when(has_low)(functools.partial(call, -1))
        pl.when(has_high)(functools.partial(call, 1))

    def gather_start(what, k, _):
        for_each(k, lambda dx: gather_copy(what, dx, k).start())
        return 0


    def fine_v2(a, count, r, _):
        centre, summed = fine_sum(va, r, a, count)
        for h in range(2):
            v2a[r, h, pl.ds(a, count), :] = (1.0 + KEEP) * centre[h] + wa[r, h, pl.ds(a, count), :] * summed[h]
        return 0

    def fine_down(a, count, q, _):
        cells = pl.ds(a - 8, count)
        sums = [fine_sum(v2a, 2 * q + k + 4, a, count) for k in range(2)]
        for h in range(2):
            lanes = pl.ds(128 * h, 128)
            rest = [
                f_in[2 * q + k, cells, lanes] - (6.0 + s_in[2 * q + k, cells, lanes]) * centre[h] + summed[h]
                for k, (centre, summed) in enumerate(sums)
            ]
            fold[q, h, cells, :] = rest[0] + rest[1]
        low, high = (
            fold[q, h, pl.ds(a - 8, count // 2, stride=2), :] + fold[q, h, pl.ds(a - 7, count // 2, stride=2), :]
            for h in range(2)
        )
        source = 0.5 * fold_lanes(low, high)
        fb[q, pl.ds((a - 8) // 2, count // 2), :] = source
        part = (q + 4, pl.ds(4 + a // 2, count // 2), slice(None))
        vb[part] = source * wb[part]
        return 0

    def fine_level(v2_a, v2_count, outer_a, outer_count, a, count):
        for r in (3, 12):
            fine_v2(outer_a, outer_count, r, 0)
        lax.fori_loop(4, 12, functools.partial(fine_v2, v2_a, v2_count), 0, unroll=True)
        lax.fori_loop(0, 4, functools.partial(fine_down, a, count), 0, unroll=True)

    receive(0)
    fine_level(7, 8, 8, 7, 8, 6)
    fine_level(33, 8, 33, 7, 34, 6)
    start(middle_v[:6])
    fine_level(15, 18, 15, 18, 14, 20)
    start(middle_v[6:])
    start(fine_far)
    lax.fori_loop(0, N, functools.partial(gather_start, 1), 0)

    receive(2)
    for r in range(3, 9):
        centre, summed = middle_sum(vb, r, 4, 24)
        tb[r, pl.ds(4, 24), :] = (1.0 + KEEP) * centre + wb[r, pl.ds(4, 24), :] * summed
    for r in range(4):
        centre, summed = middle_sum(tb, r + 4, 8, 16)
        v2b[r + 4, pl.ds(8, 16), :] = centre
        rest = fb[r, pl.ds(0, 16), :] - db[r, :, :] * centre + summed
        if r % 2 == 0:
            held = rest
        else:
            foldb[r // 2, :, :] = held + rest
    low, high = (foldb[h, pl.ds(0, 8, stride=2), :] + foldb[h, pl.ds(1, 8, stride=2), :] for h in range(2))
    gvw[2, 0, own_cols, :] = 0.5 * fold_lanes(low, high) * (OMEGA / coarse_d)

    lax.fori_loop(0, N, functools.partial(gather_start, 0), 0)
    start(middle_v2)
    gather_wait(lambda copies: copies.wait_recv())

    slab = pl.ds(8, cols)
    turned = [rolled(gvw[t, 0, slab, :], 64, 1) for t in (1, 2, 3)]
    for t in range(3):
        centre = gvw[t + 1, 0, slab, :]
        along_x = pair_x_sum(turned[max(t - 1, 0)], turned[t], turned[min(t + 1, 2)])
        along_y = gvw[t + 1, 0, pl.ds(7, cols), :] + gvw[t + 1, 0, pl.ds(9, cols), :]
        diagonal = gvw[t + 1, 1, slab, :]
        weight = jnp.where(diagonal > 0.0, OMEGA / diagonal, 0.0)
        t2[t, slab, :] = (1.0 + KEEP) * centre + weight * (along_x + along_y + z_sum(centre, 64))
    turned = [rolled(t2[t, slab, :], 64, 1) for t in range(3)]
    centre = t2[1, slab, :]
    gv2[2, slab, :] = centre
    diagonal = gvw[2, 1, slab, :]
    along_x = pair_x_sum(*turned)
    along_y = t2[1, pl.ds(7, cols), :] + t2[1, pl.ds(9, cols), :]
    rest = diagonal * (gvw[2, 0, slab, :] * (1.0 / OMEGA) - centre) + (along_x + along_y + z_sum(centre, 64))

    sizes = (common, invx, invy)
    part = tally.at[pl.ds(0, sum(int(np.prod(ref.shape)) // 128 for ref in sizes)), :]
    pltpu.make_async_copy(part, part, in_sem.at[2]).wait()
    along_z = dot(rest, common[pl.ds(0, 128), :])
    along_yz = dot(common[pl.ds(256, 4 * N), pl.ds(0, cols)], along_z)
    group = lanes_of(N) // 32
    mine = along_yz[0:N, :]
    for g in range(1, 4):
        mine = jnp.where(group == g, along_yz[g * N : (g + 1) * N, :], mine)
    modes[i, pl.ds(0, N), :] = mine
    modes[i, pl.ds(N, 1), :] = jnp.sum(diagonal - 6.0, axis=0, keepdims=True)

    def wide_copy(k):
        return pltpu.make_async_remote_copy(
            src_ref=modes.at[i], dst_ref=modes.at[i], send_sem=wide_send.at[0], recv_sem=wide_recv.at[0],
            device_id=(lax.rem(i + k, W), n), device_id_type=MESH,
        )

    def wide_start(k, _):
        wide_copy(k).start()
        return 0

    everyone = waiter((W - 1) * (N + 1), wide_send.at[0], wide_recv.at[0], (lax.rem(i + 1, W), n))

    lax.fori_loop(1, W, wide_start, 0)
    coarse_far_start()
    halo_sent()
    gather_wait(lambda copies: copies.wait_send())

    receive(1)
    everyone.wait_recv()

    total = jnp.sum(modes[:, N, :], keepdims=True)
    mean = total * (1.0 / (2 * W * 8 * N * 64))
    shifted = common[pl.ds(256 + 4 * N, N), :] + mean
    sine_x, eigen_x = sine_table(W), sine_eigen(W)
    factor = (2.0 / (W + 1.0)) * (2.0 / (4 * N + 1.0)) * (2.0 / 33.0)
    half = W // 2
    even, odd = [], []
    for j in range(half):
        first, second = modes[j, pl.ds(0, N), :], modes[W - 1 - j, pl.ds(0, N), :]
        even.append(first + second)
        odd.append(first - second)
    found = [None] * 5
    for a in range(W):
        values = even if a % 2 == 0 else odd
        acc = None
        for j in range(half):
            term = values[j] * np.float32(sine_x[a, j])
            acc = term if acc is None else acc + term
        scaled = acc * np.float32(factor) / (shifted + np.float32(eigen_x[a]))
        for t in range(5):
            term = invx[t, pl.ds(a, 1), :] * scaled
            found[t] = term if found[t] is None else found[t] + term
    spread = dot(invy[:, pl.ds(0, N)], jnp.concatenate(found, axis=1))
    group = lanes_of(WINDOW) // 32
    parts = []
    for t in range(5):
        lanes = slice(128 * t, 128 * t + 128)
        part = spread[0:WINDOW, lanes]
        for g in range(1, 4):
            part = jnp.where(group == g, spread[g * WINDOW : (g + 1) * WINDOW, lanes], part)
        parts.append(part)
    correction = dot(jnp.concatenate(parts, axis=0), common[pl.ds(128, 128), :])

    far_wait(lambda copies: copies.wait_recv())
    u = [gv2[t, window, :] + correction[WINDOW * t : WINDOW * (t + 1), :] for t in range(5)]

    def pair_sweep(u, slots):
        turned = {t: rolled(u[t], 64, 1) for t in u}
        swept = {}
        for t in slots:
            along_x = pair_x_sum(turned.get(t - 1, turned[t]), turned[t], turned.get(t + 1, turned[t]))
            along_y = rolled(u[t], 1, 0) + rolled(u[t], -1, 0)
            diagonal = gvw[t, 1, window, :]
            weight = jnp.where(diagonal > 0.0, OMEGA / diagonal, 0.0)
            summed = along_x + along_y + z_sum(u[t], 64)
            swept[t] = KEEP * u[t] + gvw[t, 0, window, :] + weight * summed
        return swept

    u = pair_sweep(dict(enumerate(u)), range(5))
    u = pair_sweep(u, range(1, 4))

    for t in (1, 2, 3):
        u2[t - 1, :, :] = u[t]
    for t in range(3):
        halves = spread_lanes(u2[t, pl.ds(4, 16), :])
        for h in range(2):
            for k in range(2):
                r = 4 * t + 2 * h + k
                ub1[r, pl.ds(0, 16, stride=2), :] = halves[h]
                ub1[r, pl.ds(1, 16, stride=2), :] = halves[h]
    for r in range(12):
        ub1[r, :, :] = ub1[r, :, :] + v2b[r, :, :]

    def middle_sweep(src, dst, r):
        centre, summed = middle_sum(src, r, 4, 24)
        part = (r, pl.ds(4, 24), slice(None))
        dst[part] = KEEP * centre + vb[part] + wb[part] * summed

    for r in range(1, 11):
        middle_sweep(ub1, ub2, r)
    for r in range(2, 10):
        middle_sweep(ub2, ub1, r)

    def fine_spread(q, _):
        halves = spread_lanes(ub1[q + 2, pl.ds(4, 24), :])
        for k in range(2):
            r = 2 * q + k
            for h in range(2):
                ua[r, h, pl.ds(0, 24, stride=2), :] = halves[h]
                ua[r, h, pl.ds(1, 24, stride=2), :] = halves[h]
        for k in range(2):
            r = 2 * q + k
            for h in range(2):
                ua[r, h, :, :] = ua[r, h, :, :] + v2a[r, h, :, :]
        return 0

    lax.fori_loop(0, 8, fine_spread, 0, unroll=True)

    def fine_sweep(src, dst, r, _):
        centre, summed = fine_sum(src, r, 4, 40)
        for h in range(2):
            part = (r, h, pl.ds(4, 40), slice(None))
            dst[part] = KEEP * centre[h] + va[part] + wa[part] * summed[h]
        return 0

    lax.fori_loop(2, 14, functools.partial(fine_sweep, ua, ub), 0, unroll=True)
    lax.fori_loop(3, 13, functools.partial(fine_sweep, ub, ua), 0, unroll=True)

    def fine_end(r, _):
        centre, summed = fine_sum(ua, r + 4, 8, 32)
        for h in range(2):
            lanes = pl.ds(128 * h, 128)
            out_v[r, :, lanes] = centre[h]
            res_v[r, :, lanes] = f_in[r, pl.ds(0, 32), lanes] - (6.0 + s_in[r, pl.ds(0, 32), lanes]) * centre[h] + summed[h]
        return 0

    lax.fori_loop(0, 8, fine_end, 0, unroll=True)
    far_wait(lambda copies: copies.wait_send())
    everyone.wait_send()


def store_kernel(out_v, res_v, out_hbm, res_hbm, sem):
    copies = [
        pltpu.make_async_copy(src, dst, sem.at[k]) for k, (src, dst) in enumerate(((out_v, out_hbm), (res_v, res_hbm)))
    ]
    for copy in copies:
        copy.start()
    for copy in copies:
        copy.wait()


def solution(mesh):
    W, N = mesh.shape["wide"], mesh.shape["narrow"]
    common, invx, invy = tables(W, N)
    cols = 8 * N
    vmem = pltpu.VMEM
    dma = pltpu.SemaphoreType.DMA
    fine, middle = (16, 2, 48, 128), (12, 32, 128)
    scratch = [
        vmem((8, 40, 256), F32), vmem((8, 40, 256), F32),
        vmem(common.shape, F32), vmem((5, W, 128), F32), vmem((4 * WINDOW, 128), F32),
        vmem(fine, F32), vmem(fine, F32), vmem(fine, F32), vmem(fine, F32), vmem(fine, F32),
        vmem((4, 2, 48, 128), F32),
        vmem(middle, F32), vmem(middle, F32), vmem(middle, F32), vmem(middle, F32),
        vmem(middle, F32), vmem(middle, F32),
        vmem((4, 24, 128), F32), vmem((4, 16, 128), F32), vmem((2, 16, 128), F32),
        vmem((5, 2, cols + 16, 128), F32), vmem((5, cols + 16, 128), F32),
        vmem((3, cols + 16, 128), F32), vmem((3, WINDOW, 128), F32),
        vmem((W, N + 1, 128), F32), vmem((2048, 128), F32),
        dma((3,)), dma((1,)), dma((3,)), dma((1,)), dma((1,)), dma((1,)), dma((1,)), dma((1,)), dma((1,)),
    ]

    def per_device(divergence, screening):
        block = pltpu.VMEM((8, 32, 256), F32)
        results = pl.pallas_call(
            functools.partial(cycle_kernel, W, N),
            out_shape=(block, block),
            in_specs=[pl.BlockSpec(memory_space=pltpu.HBM)] * 5,
            out_specs=(pl.BlockSpec(memory_space=pltpu.VMEM),) * 2,
            scratch_shapes=scratch,
            compiler_params=pltpu.CompilerParams(
                collective_id=0, has_side_effects=True, vmem_limit_bytes=56 * 1024 * 1024
            ),
        )(divergence, screening, jnp.asarray(common), jnp.asarray(invx), jnp.asarray(invy))
        stored = jax.ShapeDtypeStruct((8, 32, 256), F32)
        anywhere = pl.BlockSpec(memory_space=pl.ANY)
        return pl.pallas_call(
            store_kernel,
            out_shape=(stored, stored),
            in_specs=[pl.BlockSpec(memory_space=pltpu.VMEM)] * 2,
            out_specs=(anywhere, anywhere),
            scratch_shapes=[dma((2,))],
            compiler_params=pltpu.CompilerParams(vmem_limit_bytes=4 * 1024 * 1024),
        )(*results)

    spec = P("wide", "narrow", None)
    return jax.shard_map(
        per_device, mesh=mesh, in_specs=(spec, spec), out_specs=(spec, spec), check_vma=False
    )
```

```python
import functools

import numpy as np
import jax
import jax.numpy as jnp
from jax import lax
from jax.experimental import pallas as pl
from jax.experimental.pallas import tpu as pltpu
from jax.sharding import PartitionSpec as P

MESH = pl.DeviceIdType.MESH
F32 = jnp.float32
OMEGA = 0.8
KEEP = 0.2
WINDOW = 24


def sine_table(count):
    ladder = np.arange(count, dtype=np.float64) + 1.0
    return np.sin(np.pi * ladder[:, None] * ladder[None, :] / (count + 1.0))


def sine_eigen(count):
    ladder = np.arange(count, dtype=np.float64) + 1.0
    return 2.0 - 2.0 * np.cos(np.pi * ladder / (count + 1.0))


def tables(wide, narrow):
    count_y, count_z = 4 * narrow, 32
    sine_x, sine_y, sine_z = sine_table(wide), sine_table(count_y), sine_table(count_z)
    to_modes = np.tile(np.repeat(sine_z.T, 2, axis=0), (2, 4))
    from_modes = np.tile(np.repeat(sine_z, 2, axis=1), (4, 2))
    rows_y = 0.5 * np.repeat(sine_y, 2, axis=1)
    rows_y = np.pad(rows_y, ((0, 0), (0, 128 - rows_y.shape[1])))
    eigen_y = sine_eigen(count_y).reshape(4, narrow)
    eigen = eigen_y.T[:, :, None] + sine_eigen(count_z)[None, None, :]
    eigen = eigen.reshape(narrow, 128)
    common = np.concatenate([to_modes, from_modes, rows_y, eigen], axis=0)
    inverse_x = np.pad(sine_x, ((2, 2), (0, 0)))
    inverse_x = np.repeat(inverse_x[:, :, None], 128, axis=2)
    fine_y = np.pad(np.repeat(sine_y, 2, axis=0), ((8, 8), (0, 0)))
    inverse_y = np.zeros((narrow, 4, WINDOW, 128))
    for n in range(narrow):
        for g in range(4):
            inverse_y[n, g, :, :narrow] = fine_y[8 * n : 8 * n + WINDOW, g * narrow : (g + 1) * narrow]
    inverse_y = inverse_y.reshape(narrow, 4 * WINDOW, 128)
    return [a.astype(np.float32) for a in (common, inverse_x, inverse_y)]


def rolled(value, shift, axis):
    return pltpu.roll(value, shift % value.shape[axis], axis)


def lanes_of(rows):
    return lax.broadcasted_iota(jnp.int32, (rows, 128), 1)


def z_sum_halves(low, high):
    lane = lanes_of(low.shape[0])
    up_low, up_high = rolled(low, -1, 1), rolled(high, -1, 1)
    down_low, down_high = rolled(low, 1, 1), rolled(high, 1, 1)
    last, first = lane == 127, lane == 0
    sum_low = jnp.where(last, up_high, up_low) + jnp.where(first, 0.0, down_low)
    sum_high = jnp.where(last, 0.0, up_high) + jnp.where(first, down_low, down_high)
    return sum_low, sum_high


def z_sum(value, period):
    lane = lanes_of(value.shape[0]) % period
    up = jnp.where(lane == period - 1, 0.0, rolled(value, -1, 1))
    return up + jnp.where(lane == 0, 0.0, rolled(value, 1, 1))


def fine_sum(ref, r, a, n):
    centre = [ref[r, h, pl.ds(a, n), :] for h in range(2)]
    along_z = z_sum_halves(*centre)
    summed = []
    for h in range(2):
        along_x = ref[r - 1, h, pl.ds(a, n), :] + ref[r + 1, h, pl.ds(a, n), :]
        along_y = ref[r, h, pl.ds(a - 1, n), :] + ref[r, h, pl.ds(a + 1, n), :]
        summed.append(along_x + along_y + along_z[h])
    return centre, summed


def middle_sum(ref, r, a, n):
    centre = ref[r, pl.ds(a, n), :]
    along_x = ref[r - 1, pl.ds(a, n), :] + ref[r + 1, pl.ds(a, n), :]
    along_y = ref[r, pl.ds(a - 1, n), :] + ref[r, pl.ds(a + 1, n), :]
    return centre, along_x + along_y + z_sum(centre, 128)


def pair_x_sum(before, here, after):
    return here + jnp.where(lanes_of(here.shape[0]) < 64, before, after)


def fold_lanes(low, high):
    rows = low.shape[0]
    lane = lanes_of(rows)
    index = (lane * 2) % 128
    low = jnp.take_along_axis(low + rolled(low, -1, 1), index, axis=1)
    high = jnp.take_along_axis(high + rolled(high, -1, 1), index, axis=1)
    return jnp.where(lane < 64, low, high)


def spread_lanes(value):
    lane = lanes_of(value.shape[0])
    index = lane // 2
    return jnp.take_along_axis(value, index, axis=1), jnp.take_along_axis(value, index + 64, axis=1)


def dot(a, b):
    return jnp.dot(a, b, precision=lax.Precision.HIGHEST, preferred_element_type=F32)


def cycle_kernel(
    W, N,
    f_hbm, s_hbm, common_hbm, invx_hbm, invy_hbm,
    out_v, res_v,
    f_in, s_in, common, invx, invy,
    va, wa, v2a, ua, ub, fold,
    vb, wb, v2b, tb, ub1, ub2, fb, db, foldb,
    gvw, gv2, t2, u2,
    modes, tally,
    in_sem, send_sem, recv_sem, far_send, far_recv, gather_send, gather_recv, wide_send, wide_recv,
):
    i = lax.axis_index("wide")
    n = lax.axis_index("narrow")

    loads = [
        pltpu.make_async_copy(src, dst, in_sem.at[min(k, 2)])
        for k, (src, dst) in enumerate(
            (
                (s_hbm, s_in.at[:, pl.ds(0, 32), :]),
                (f_hbm, f_in.at[:, pl.ds(0, 32), :]),
                (common_hbm, common),
                (invx_hbm.at[pl.ds(i, 5)], invx),
                (invy_hbm.at[n], invy),
            )
        )
    ]
    barrier = pltpu.get_barrier_semaphore()

    def greet(wide_id, narrow_id):
        pl.semaphore_signal(barrier, inc=1, device_id=(wide_id, narrow_id), device_id_type=MESH)

    has_low, has_high = i > 0, i < W - 1

    def there(dx, dy):
        terms = []
        if dx > 0:
            terms.append(i < W - dx)
        if dx < 0:
            terms.append(i >= -dx)
        if dy > 0:
            terms.append(n < N - dy)
        if dy < 0:
            terms.append(n >= -dy)
        return functools.reduce(jnp.logical_and, terms)

    def flipped(index, mask):
        result, bit = index, 1
        while bit <= mask:
            if mask & bit:
                result = result + bit * (1 - 2 * lax.rem(lax.div(index, bit), 2))
            bit *= 2
        return result

    far_columns = sorted(range(1, N), key=lambda m: (m // 4, min(m % 4, 4 - m % 4), m), reverse=True)
    far_rows = sorted(range(1, W), key=lambda m: (m // 8 + min(m // 2 % 4, 4 - m // 2 % 4), m), reverse=True)
    for m in far_columns:
        other = flipped(n, m)
        pl.when(has_low)(functools.partial(greet, i - 1, other))
        pl.when(has_high)(functools.partial(greet, i + 1, other))
        greet(i, other)
    for m in far_rows:
        greet(flipped(i, m), n)

    for load in loads:
        load.start()

    sides = (-1, 1)
    corners = [(dx, dy) for dx in sides for dy in sides]

    def zero(ref, *index):
        shape = ref.at[index].shape if index else ref.shape
        ref[index if index else ...] = jnp.zeros(shape, F32)

    all_ = slice(None)

    @pl.when(i == 0)
    def _():
        for ref in (va, wa, v2a):
            zero(ref, pl.ds(0, 4))
        for ref in (vb, wb, v2b):
            zero(ref, pl.ds(0, 4))
        zero(gvw, pl.ds(0, 2))
        zero(gv2, pl.ds(0, 2))

    @pl.when(i == W - 1)
    def _():
        for ref in (va, wa, v2a):
            zero(ref, pl.ds(12, 4))
        for ref in (vb, wb, v2b):
            zero(ref, pl.ds(8, 4))
        zero(gvw, pl.ds(3, 2))
        zero(gv2, pl.ds(3, 2))

    @pl.when(i == 1)
    def _():
        zero(gvw, 0)
        zero(gv2, 0)

    @pl.when(i == W - 2)
    def _():
        zero(gvw, 4)
        zero(gv2, 4)

    @pl.when(n == 0)
    def _():
        for ref in (va, wa, v2a):
            zero(ref, all_, all_, pl.ds(0, 8))
        for ref in (vb, wb, v2b):
            zero(ref, all_, pl.ds(0, 8))

    @pl.when(n == N - 1)
    def _():
        for ref in (va, wa, v2a):
            zero(ref, all_, all_, pl.ds(40, 8))
        for ref in (vb, wb, v2b):
            zero(ref, all_, pl.ds(24, 8))

    cols = 8 * N
    zero(gvw, pl.ds(1, 3), all_, pl.ds(0, 8))
    zero(gvw, pl.ds(1, 3), all_, pl.ds(8 + cols, 8))
    zero(gv2, 2, pl.ds(0, 8))
    zero(gv2, 2, pl.ds(8 + cols, 8))
    zero(t2, all_, pl.ds(0, 8))
    zero(t2, all_, pl.ds(8 + cols, 8))

    loads[0].wait()
    loads[1].wait()

    def start_fine(r, _):
        for h in range(2):
            screen = s_in[r, pl.ds(0, 32), pl.ds(128 * h, 128)]
            weight = OMEGA / (6.0 + screen)
            wa[r + 4, h, pl.ds(8, 32), :] = weight
            va[r + 4, h, pl.ds(8, 32), :] = f_in[r, pl.ds(0, 32), pl.ds(128 * h, 128)] * weight
        return 0

    lax.fori_loop(0, 8, start_fine, 0, unroll=True)

    rows_of = {}
    both_x, both_y = jnp.logical_and(has_low, has_high), jnp.logical_and(n > 0, n < N - 1)

    def by_place(call):
        for sides_x in (1, 2):
            for sides_y in (1, 2):
                here_x = both_x if sides_x == 2 else jnp.logical_not(both_x)
                here_y = both_y if sides_y == 2 else jnp.logical_not(both_y)
                pl.when(jnp.logical_and(here_x, here_y))(functools.partial(call, sides_x, sides_y))

    def waiter(rows, send, recv, to):
        part = tally.at[pl.ds(0, rows), :]
        return pltpu.make_async_remote_copy(
            src_ref=part, dst_ref=part, send_sem=send, recv_sem=recv, device_id=to, device_id_type=MESH
        )

    def beside(dx, dy):
        return lax.rem(i + dx + W, W), lax.rem(n + dy + N, N)

    def span(step, first, size, depths):
        if step == 0:
            return pl.ds(first, size), pl.ds(first, size)
        low, high = depths
        count = high - low + 1
        if step > 0:
            return pl.ds(first + size - high, count), pl.ds(first - high, count)
        return pl.ds(first + low - 1, count), pl.ds(first + size + low - 1, count)

    def exchange(family, src, dst, dx, dy):
        kind = (family, dx != 0, dy != 0)
        if dx >= 0 and dy >= 0:
            rows_of[kind] = rows_of.get(kind, 0) + int(np.prod(src.shape)) // 128
        copy = pltpu.make_async_remote_copy(
            src_ref=src, dst_ref=dst, send_sem=send_sem.at[0], recv_sem=recv_sem.at[family],
            device_id=beside(dx, dy), device_id_type=MESH,
        )
        return copy, there(dx, dy)

    def halo_waiter(families, sides_x, sides_y):
        rows = sum(
            sides_x * rows_of[family, True, False]
            + sides_y * rows_of[family, False, True]
            + sides_x * sides_y * rows_of[family, True, True]
            for family in families
        )
        return waiter(rows, send_sem.at[0], recv_sem.at[families[0]], (lax.rem(i + 1, W), n))

    def fine_piece(family, ref, dx, dy, depth_x=None, depth_y=None):
        src_x, dst_x = span(dx, 4, 8, depth_x)
        src_y, dst_y = span(dy, 8, 32, depth_y)
        return exchange(family, ref.at[src_x, :, src_y, :], ref.at[dst_x, :, dst_y, :], dx, dy)

    def middle_piece(family, ref, dx, dy, depth_x=None, depth_y=None):
        src_x, dst_x = span(dx, 4, 4, depth_x)
        src_y, dst_y = span(dy, 8, 16, depth_y)
        return exchange(family, ref.at[src_x, src_y, :], ref.at[dst_x, dst_y, :], dx, dy)

    def start(pieces):
        for copy, to in pieces:
            pl.when(to)(copy.start)

    def receive(family):
        by_place(lambda sides_x, sides_y: halo_waiter([family], sides_x, sides_y).wait_recv())

    def halo_sent():
        by_place(lambda sides_x, sides_y: halo_waiter(range(3), sides_x, sides_y).wait_send())

    fine_near = (
        [fine_piece(0, va, 0, d, None, (1, 2)) for d in sides]
        + [fine_piece(0, wa, 0, d, None, (1, 1)) for d in sides]
        + [fine_piece(0, va, dx, dy, (1, 1), (1, 1)) for dx, dy in corners]
        + [fine_piece(0, va, d, 0, (1, 2)) for d in sides]
        + [fine_piece(0, wa, d, 0, (1, 1)) for d in sides]
    )
    fine_far = (
        [fine_piece(1, v2a, 0, d, None, (2, 3)) for d in sides]
        + [fine_piece(1, wa, 0, d, None, (2, 2)) for d in sides]
        + [fine_piece(1, v2a, dx, dy, (1, 2), (1, 2)) for dx, dy in corners]
        + [fine_piece(1, wa, dx, dy, (1, 1), (1, 1)) for dx, dy in corners]
        + [fine_piece(1, v2a, d, 0, (2, 3)) for d in sides]
        + [fine_piece(1, wa, d, 0, (2, 2)) for d in sides]
    )

    def middle_pieces(family, ref, depth, corner):
        return (
            [middle_piece(family, ref, 0, d, None, (1, depth)) for d in sides]
            + [middle_piece(family, ref, dx, dy, (1, corner), (1, corner)) for dx, dy in corners]
            + [middle_piece(family, ref, d, 0, (1, depth)) for d in sides]
        )

    middle_w = middle_pieces(2, wb, 3, 2)
    middle_v = middle_pieces(2, vb, 3, 2)
    middle_v2 = middle_pieces(1, v2b, 4, 3)

    window = pl.ds(pl.multiple_of(8 * n, 8), WINDOW)
    reach = (-2, -1, 1, 2)

    def coarse_far(d):
        args = dict(
            send_sem=far_send.at[0], recv_sem=far_recv.at[0], device_id=beside(d, 0), device_id_type=MESH
        )
        copies = [pltpu.make_async_remote_copy(src_ref=gv2.at[2, window, :], dst_ref=gv2.at[2 - d, window, :], **args)]
        if abs(d) == 2:
            copies.append(
                pltpu.make_async_remote_copy(
                    src_ref=gvw.at[2, :, window, :], dst_ref=gvw.at[2 - d, :, window, :], **args
                )
            )
        return copies

    def coarse_far_start():
        for d in reach:
            for copy in coarse_far(d):
                pl.when(there(d, 0))(copy.start)

    def far_wait(call):
        further = jnp.logical_and(i > 1, i < W - 2)
        cases = (
            (1, 1, jnp.logical_not(both_x)),
            (2, 1, jnp.logical_and(both_x, jnp.logical_not(further))),
            (2, 2, further),
        )
        for near, far, here in cases:
            rows = (near + 3 * far) * WINDOW
            pl.when(here)(functools.partial(call, waiter(rows, far_send.at[0], far_recv.at[0], beside(1, 0))))

    greeted = (W - 1) + (N - 1) * (1 + has_low.astype(jnp.int32) + has_high.astype(jnp.int32))
    pl.semaphore_wait(barrier, greeted)

    start(fine_near)

    def screen_middle(q, _):
        for h in range(2):
            lanes = pl.ds(128 * h, 128)
            fold[q, h, pl.ds(0, 32), :] = s_in[2 * q, pl.ds(0, 32), lanes] + s_in[2 * q + 1, pl.ds(0, 32), lanes]
        low, high = (
            fold[q, h, pl.ds(0, 16, stride=2), :] + fold[q, h, pl.ds(1, 16, stride=2), :] for h in range(2)
        )
        diagonal = 6.0 + 0.125 * fold_lanes(low, high)
        db[q, :, :] = diagonal
        wb[q + 4, pl.ds(8, 16), :] = OMEGA / diagonal
        return 0

    lax.fori_loop(0, 4, screen_middle, 0, unroll=True)
    start(middle_w)

    for h in range(2):
        foldb[h, :, :] = (db[2 * h, :, :] - 6.0) + (db[2 * h + 1, :, :] - 6.0)
    low, high = (foldb[h, pl.ds(0, 8, stride=2), :] + foldb[h, pl.ds(1, 8, stride=2), :] for h in range(2))
    coarse_d = 6.0 + 0.125 * fold_lanes(low, high)
    own_cols = pl.ds(pl.multiple_of(8 + 8 * n, 8), 8)
    gvw[2, 1, own_cols, :] = coarse_d

    def gather_copy(what, dx, k):
        other = lax.rem(n + k, N)
        target = lax.rem(i + dx + W, W)
        return pltpu.make_async_remote_copy(
            src_ref=gvw.at[2, what, own_cols, :], dst_ref=gvw.at[2 - dx, what, own_cols, :],
            send_sem=gather_send.at[0], recv_sem=gather_recv.at[0],
            device_id=(target, other), device_id_type=MESH,
        )

    def gather_wait(call):
        for sides_x, here in ((2, both_x), (1, jnp.logical_not(both_x))):
            rows = 2 * 8 * (N - 1 + sides_x * N)
            target = (lax.rem(i + 1, W), n)
            pl.when(here)(functools.partial(call, waiter(rows, gather_send.at[0], gather_recv.at[0], target)))

    def for_each(k, call):
        pl.when(k > 0)(functools.partial(call, 0))
        pl.when(has_low)(functools.partial(call, -1))
        pl.when(has_high)(functools.partial(call, 1))

    def gather_start(what, k, _):
        for_each(k, lambda dx: gather_copy(what, dx, k).start())
        return 0


    def fine_v2(a, count, r, _):
        centre, summed = fine_sum(va, r, a, count)
        for h in range(2):
            v2a[r, h, pl.ds(a, count), :] = (1.0 + KEEP) * centre[h] + wa[r, h, pl.ds(a, count), :] * summed[h]
        return 0

    def fine_down(a, count, q, _):
        cells = pl.ds(a - 8, count)
        sums = [fine_sum(v2a, 2 * q + k + 4, a, count) for k in range(2)]
        for h in range(2):
            lanes = pl.ds(128 * h, 128)
            rest = [
                f_in[2 * q + k, cells, lanes] - (6.0 + s_in[2 * q + k, cells, lanes]) * centre[h] + summed[h]
                for k, (centre, summed) in enumerate(sums)
            ]
            fold[q, h, cells, :] = rest[0] + rest[1]
        low, high = (
            fold[q, h, pl.ds(a - 8, count // 2, stride=2), :] + fold[q, h, pl.ds(a - 7, count // 2, stride=2), :]
            for h in range(2)
        )
        source = 0.5 * fold_lanes(low, high)
        fb[q, pl.ds((a - 8) // 2, count // 2), :] = source
        part = (q + 4, pl.ds(4 + a // 2, count // 2), slice(None))
        vb[part] = source * wb[part]
        return 0

    def fine_level(v2_a, v2_count, outer_a, outer_count, a, count):
        for r in (3, 12):
            fine_v2(outer_a, outer_count, r, 0)
        lax.fori_loop(4, 12, functools.partial(fine_v2, v2_a, v2_count), 0, unroll=True)
        lax.fori_loop(0, 4, functools.partial(fine_down, a, count), 0, unroll=True)

    receive(0)
    fine_level(7, 8, 8, 7, 8, 6)
    fine_level(33, 8, 33, 7, 34, 6)
    start(middle_v[:6])
    fine_level(15, 18, 15, 18, 14, 20)
    start(middle_v[6:])
    start(fine_far)
    lax.fori_loop(0, N, functools.partial(gather_start, 1), 0)

    receive(2)
    for r in range(3, 9):
        centre, summed = middle_sum(vb, r, 4, 24)
        tb[r, pl.ds(4, 24), :] = (1.0 + KEEP) * centre + wb[r, pl.ds(4, 24), :] * summed
    for r in range(4):
        centre, summed = middle_sum(tb, r + 4, 8, 16)
        v2b[r + 4, pl.ds(8, 16), :] = centre
        rest = fb[r, pl.ds(0, 16), :] - db[r, :, :] * centre + summed
        if r % 2 == 0:
            held = rest
        else:
            foldb[r // 2, :, :] = held + rest
    low, high = (foldb[h, pl.ds(0, 8, stride=2), :] + foldb[h, pl.ds(1, 8, stride=2), :] for h in range(2))
    gvw[2, 0, own_cols, :] = 0.5 * fold_lanes(low, high) * (OMEGA / coarse_d)

    lax.fori_loop(0, N, functools.partial(gather_start, 0), 0)
    start(middle_v2)
    gather_wait(lambda copies: copies.wait_recv())

    slab = pl.ds(8, cols)
    turned = [rolled(gvw[t, 0, slab, :], 64, 1) for t in (1, 2, 3)]
    for t in range(3):
        centre = gvw[t + 1, 0, slab, :]
        along_x = pair_x_sum(turned[max(t - 1, 0)], turned[t], turned[min(t + 1, 2)])
        along_y = gvw[t + 1, 0, pl.ds(7, cols), :] + gvw[t + 1, 0, pl.ds(9, cols), :]
        diagonal = gvw[t + 1, 1, slab, :]
        weight = jnp.where(diagonal > 0.0, OMEGA / diagonal, 0.0)
        t2[t, slab, :] = (1.0 + KEEP) * centre + weight * (along_x + along_y + z_sum(centre, 64))
    turned = [rolled(t2[t, slab, :], 64, 1) for t in range(3)]
    centre = t2[1, slab, :]
    gv2[2, slab, :] = centre
    diagonal = gvw[2, 1, slab, :]
    along_x = pair_x_sum(*turned)
    along_y = t2[1, pl.ds(7, cols), :] + t2[1, pl.ds(9, cols), :]
    rest = diagonal * (gvw[2, 0, slab, :] * (1.0 / OMEGA) - centre) + (along_x + along_y + z_sum(centre, 64))

    sizes = (common, invx, invy)
    part = tally.at[pl.ds(0, sum(int(np.prod(ref.shape)) // 128 for ref in sizes)), :]
    pltpu.make_async_copy(part, part, in_sem.at[2]).wait()
    along_z = dot(rest, common[pl.ds(0, 128), :])
    along_yz = dot(common[pl.ds(256, 4 * N), pl.ds(0, cols)], along_z)
    group = lanes_of(N) // 32
    mine = along_yz[0:N, :]
    for g in range(1, 4):
        mine = jnp.where(group == g, along_yz[g * N : (g + 1) * N, :], mine)
    modes[i, pl.ds(0, N), :] = mine
    modes[i, pl.ds(N, 1), :] = jnp.sum(diagonal - 6.0, axis=0, keepdims=True)

    def wide_copy(k):
        return pltpu.make_async_remote_copy(
            src_ref=modes.at[i], dst_ref=modes.at[i], send_sem=wide_send.at[0], recv_sem=wide_recv.at[0],
            device_id=(lax.rem(i + k, W), n), device_id_type=MESH,
        )

    def wide_start(k, _):
        wide_copy(k).start()
        return 0

    everyone = waiter((W - 1) * (N + 1), wide_send.at[0], wide_recv.at[0], (lax.rem(i + 1, W), n))

    lax.fori_loop(1, W, wide_start, 0)
    coarse_far_start()
    halo_sent()
    gather_wait(lambda copies: copies.wait_send())

    receive(1)
    everyone.wait_recv()

    total = jnp.sum(modes[:, N, :], keepdims=True)
    mean = total * (1.0 / (2 * W * 8 * N * 64))
    shifted = common[pl.ds(256 + 4 * N, N), :] + mean
    sine_x, eigen_x = sine_table(W), sine_eigen(W)
    factor = (2.0 / (W + 1.0)) * (2.0 / (4 * N + 1.0)) * (2.0 / 33.0)
    half = W // 2
    even, odd = [], []
    for j in range(half):
        first, second = modes[j, pl.ds(0, N), :], modes[W - 1 - j, pl.ds(0, N), :]
        even.append(first + second)
        odd.append(first - second)
    found = [None] * 5
    for a in range(W):
        values = even if a % 2 == 0 else odd
        acc = None
        for j in range(half):
            term = values[j] * np.float32(sine_x[a, j])
            acc = term if acc is None else acc + term
        scaled = acc * np.float32(factor) / (shifted + np.float32(eigen_x[a]))
        for t in range(5):
            term = invx[t, pl.ds(a, 1), :] * scaled
            found[t] = term if found[t] is None else found[t] + term
    spread = dot(invy[:, pl.ds(0, N)], jnp.concatenate(found, axis=1))
    group = lanes_of(WINDOW) // 32
    parts = []
    for t in range(5):
        lanes = slice(128 * t, 128 * t + 128)
        part = spread[0:WINDOW, lanes]
        for g in range(1, 4):
            part = jnp.where(group == g, spread[g * WINDOW : (g + 1) * WINDOW, lanes], part)
        parts.append(part)
    correction = dot(jnp.concatenate(parts, axis=0), common[pl.ds(128, 128), :])

    far_wait(lambda copies: copies.wait_recv())
    u = [gv2[t, window, :] + correction[WINDOW * t : WINDOW * (t + 1), :] for t in range(5)]

    def pair_sweep(u, slots):
        turned = {t: rolled(u[t], 64, 1) for t in u}
        swept = {}
        for t in slots:
            along_x = pair_x_sum(turned.get(t - 1, turned[t]), turned[t], turned.get(t + 1, turned[t]))
            along_y = rolled(u[t], 1, 0) + rolled(u[t], -1, 0)
            diagonal = gvw[t, 1, window, :]
            weight = jnp.where(diagonal > 0.0, OMEGA / diagonal, 0.0)
            summed = along_x + along_y + z_sum(u[t], 64)
            swept[t] = KEEP * u[t] + gvw[t, 0, window, :] + weight * summed
        return swept

    u = pair_sweep(dict(enumerate(u)), range(5))
    u = pair_sweep(u, range(1, 4))

    for t in (1, 2, 3):
        u2[t - 1, :, :] = u[t]
    for t in range(3):
        halves = spread_lanes(u2[t, pl.ds(4, 16), :])
        for h in range(2):
            for k in range(2):
                r = 4 * t + 2 * h + k
                ub1[r, pl.ds(0, 16, stride=2), :] = halves[h]
                ub1[r, pl.ds(1, 16, stride=2), :] = halves[h]
    for r in range(12):
        ub1[r, :, :] = ub1[r, :, :] + v2b[r, :, :]

    def middle_sweep(src, dst, r):
        centre, summed = middle_sum(src, r, 4, 24)
        part = (r, pl.ds(4, 24), slice(None))
        dst[part] = KEEP * centre + vb[part] + wb[part] * summed

    for r in range(1, 11):
        middle_sweep(ub1, ub2, r)
    for r in range(2, 10):
        middle_sweep(ub2, ub1, r)

    def fine_spread(q, _):
        halves = spread_lanes(ub1[q + 2, pl.ds(4, 24), :])
        for k in range(2):
            r = 2 * q + k
            for h in range(2):
                ua[r, h, pl.ds(0, 24, stride=2), :] = halves[h]
                ua[r, h, pl.ds(1, 24, stride=2), :] = halves[h]
        for k in range(2):
            r = 2 * q + k
            for h in range(2):
                ua[r, h, :, :] = ua[r, h, :, :] + v2a[r, h, :, :]
        return 0

    lax.fori_loop(0, 8, fine_spread, 0, unroll=True)

    def fine_sweep(src, dst, r, _):
        centre, summed = fine_sum(src, r, 4, 40)
        for h in range(2):
            part = (r, h, pl.ds(4, 40), slice(None))
            dst[part] = KEEP * centre[h] + va[part] + wa[part] * summed[h]
        return 0

    lax.fori_loop(2, 14, functools.partial(fine_sweep, ua, ub), 0, unroll=True)
    lax.fori_loop(3, 13, functools.partial(fine_sweep, ub, ua), 0, unroll=True)

    def fine_end(r, _):
        centre, summed = fine_sum(ua, r + 4, 8, 32)
        for h in range(2):
            lanes = pl.ds(128 * h, 128)
            out_v[r, :, lanes] = centre[h]
            res_v[r, :, lanes] = f_in[r, pl.ds(0, 32), lanes] - (6.0 + s_in[r, pl.ds(0, 32), lanes]) * centre[h] + summed[h]
        return 0

    lax.fori_loop(0, 8, fine_end, 0, unroll=True)
    far_wait(lambda copies: copies.wait_send())
    everyone.wait_send()


def store_kernel(out_v, res_v, out_hbm, res_hbm, sem):
    copies = [
        pltpu.make_async_copy(src, dst, sem.at[k]) for k, (src, dst) in enumerate(((out_v, out_hbm), (res_v, res_hbm)))
    ]
    for copy in copies:
        copy.start()
    for copy in copies:
        copy.wait()


def solution(mesh):
    W, N = mesh.shape["wide"], mesh.shape["narrow"]
    common, invx, invy = tables(W, N)
    cols = 8 * N
    vmem = pltpu.VMEM
    dma = pltpu.SemaphoreType.DMA
    fine, middle = (16, 2, 48, 128), (12, 32, 128)
    scratch = [
        vmem((8, 40, 256), F32), vmem((8, 40, 256), F32),
        vmem(common.shape, F32), vmem((5, W, 128), F32), vmem((4 * WINDOW, 128), F32),
        vmem(fine, F32), vmem(fine, F32), vmem(fine, F32), vmem(fine, F32), vmem(fine, F32),
        vmem((4, 2, 48, 128), F32),
        vmem(middle, F32), vmem(middle, F32), vmem(middle, F32), vmem(middle, F32),
        vmem(middle, F32), vmem(middle, F32),
        vmem((4, 24, 128), F32), vmem((4, 16, 128), F32), vmem((2, 16, 128), F32),
        vmem((5, 2, cols + 16, 128), F32), vmem((5, cols + 16, 128), F32),
        vmem((3, cols + 16, 128), F32), vmem((3, WINDOW, 128), F32),
        vmem((W, N + 1, 128), F32), vmem((2048, 128), F32),
        dma((3,)), dma((1,)), dma((3,)), dma((1,)), dma((1,)), dma((1,)), dma((1,)), dma((1,)), dma((1,)),
    ]

    def per_device(divergence, screening):
        block = pltpu.VMEM((8, 32, 256), F32)
        results = pl.pallas_call(
            functools.partial(cycle_kernel, W, N),
            out_shape=(block, block),
            in_specs=[pl.BlockSpec(memory_space=pltpu.HBM)] * 5,
            out_specs=(pl.BlockSpec(memory_space=pltpu.VMEM),) * 2,
            scratch_shapes=scratch,
            compiler_params=pltpu.CompilerParams(
                collective_id=0, has_side_effects=True, vmem_limit_bytes=56 * 1024 * 1024
            ),
        )(divergence, screening, jnp.asarray(common), jnp.asarray(invx), jnp.asarray(invy))
        stored = jax.ShapeDtypeStruct((8, 32, 256), F32)
        anywhere = pl.BlockSpec(memory_space=pl.ANY)
        return pl.pallas_call(
            store_kernel,
            out_shape=(stored, stored),
            in_specs=[pl.BlockSpec(memory_space=pltpu.VMEM)] * 2,
            out_specs=(anywhere, anywhere),
            scratch_shapes=[dma((2,))],
            compiler_params=pltpu.CompilerParams(vmem_limit_bytes=4 * 1024 * 1024),
        )(*results)

    spec = P("wide", "narrow", None)
    return jax.shard_map(
        per_device, mesh=mesh, in_specs=(spec, spec), out_specs=(spec, spec), check_vma=False
    )
```
